128 devices in a mesh: wide: 16 (over z, x), narrow: 8 (over y, core).
Axes of the slice: x: 4, y: 4, z: 4, core: 2. Of those that a mesh axis runs over, the one named last changes fastest.
Arguments:
- queries: bfloat16 [4096, 4096], P('wide'), may hold values from -256 to 256
- span_keys: bfloat16 [4096, 1024], P('wide'), may hold values from -6 to 6
- span_values: bfloat16 [4096, 1024], P('wide'), may hold values from -6 to 6
- cache_keys: bfloat16 [524288, 128], P(('wide', 'narrow')), may hold values from -6 to 6
- cache_values: bfloat16 [524288, 128], P(('wide', 'narrow')), may hold values from -6 to 6
- chosen: int32 [8, 3], replicated, may hold values from 0 to 15, all different within a row; in each aligned block of 8 rows (0 to 7, 8 to 15, ...) at most 4 rows name the same one
- out_weight: bfloat16 [4096, 4096], P('wide', 'narrow'), may hold values from -0.09375 to 0.09375
Outputs:
- projected: bfloat16 [4096, 4096], P('wide', 'narrow')
The draws below stay inside these ranges and needn't reach their ends.
Inputs may be any that keep to these rules, and one draw needn't show every extreme that they name: `chosen`: each row names 3 different key blocks; each key block is named by at most 4 rows and some block by exactly 4; every block is named by some row.
All inputs are finite; a program needn't handle non-finite values.
Results may differ from the reference program's by a relative error of at most 0.019.
Values may be sent and summed in bfloat16 or wider, within the bound.
A program may use at most 128 MiB of HBM per device.

```python
import math
import jax
import jax.numpy as jnp
import numpy as np
from jax import lax

D = 4096
HD = 128
GROUP = 4
QB = 512
KB = 4096
TOPK = 3
MOST = 4
H = 32
KVH = 8
NQB = 8
TOKENS = 4096
NKB = 16
PREFIX = 65536


def draw_queries(key, part):
    key = jax.random.fold_in(key, 7)
    base_key = jax.random.fold_in(key, 0)
    values = jnp.clip(jax.random.normal(base_key, (TOKENS, H * HD), jnp.float32), -4.0, 4.0)
    return values.astype(jnp.bfloat16)


def block_scale(key, shape, pieces, least, high):
    factor_of, own = 1.0, jax.random.fold_in(key, 6)
    for dim, parts in pieces:
        steps = jnp.exp(jax.random.uniform(jax.random.fold_in(own, dim), (parts,), jnp.float32, least / len(pieces), high / len(pieces)))
        factor_of = factor_of * jnp.repeat(steps, shape[dim] // parts).reshape([-1 if axis == dim else 1 for axis in range(len(shape))])
    return factor_of


def routed_block(rng, own, number, rows, count, top, limit, skew):
    sequence = jax.random.permutation(rng, count)
    heavy_load, common = shares(count, rows * top, limit, skew, True), shares(count, rows * top, limit, skew, False)
    places = jnp.arange(count)

    def named(tallies, rotation):
        used = int((tallies > 0).sum())
        fixed = max(1, used // 4)
        moved = fixed + (places - fixed + rotation * (used - fixed)) % max(1, count - fixed)
        return jnp.zeros((count,), jnp.int32).at[sequence[jnp.where(places < fixed, places, moved)]].set(jnp.asarray(tallies, jnp.int32))

    tallies = jnp.where(number % 4 == 0, named(heavy_load, number // 4), named(common, number - number // 4 - 1))
    mixed = jax.random.permutation(jax.random.fold_in(own, 3), count)
    donor, receiver = mixed[0:count // 2 * 2:2], mixed[1:count // 2 * 2:2]
    room = jnp.minimum(tallies[donor] - 1, limit - tallies[receiver]) // 2
    room = jnp.where((donor == sequence[0]) | (receiver == sequence[0]) | (tallies[receiver] == 0), 0, jnp.maximum(room, 0))
    moved = jax.random.randint(jax.random.fold_in(own, 4), (count // 2,), 0, 1 << 20) % (room + 1)
    tallies = tallies.at[donor].add(-moved).at[receiver].add(moved)
    members = jnp.searchsorted(jnp.cumsum(tallies), jnp.arange(rows * top), side="right").astype(jnp.int32)
    listing = members.reshape(top, rows).T
    listing = listing[jax.random.permutation(jax.random.fold_in(own, 1), rows)]
    rotation = jax.random.randint(jax.random.fold_in(own, 2), (rows, 1), 0, top)
    return jnp.take_along_axis(listing, (jnp.arange(top)[None, :] + rotation) % top, axis=1)


def shares(number_of, total, reach, lean, full):
    weights = [(1 << 20) // math.isqrt(grade ** lean) + 1 for grade in range(1, number_of + 1)]
    largest = reach if full else min(reach, max(-(-total // number_of), total * weights[0] // sum(weights)))
    least = 1 if total - largest >= number_of - 1 else 0
    holding, rest = [largest] + [least] * (number_of - 1), total - largest - least * (number_of - 1)
    while rest > 0:
        candidates = [i for i in range(1, number_of) if holding[i] < largest] or [i for i in range(1, number_of) if holding[i] < reach]
        pool, remaining = sum([weights[i] for i in candidates]), rest
        for i in candidates:
            extra = min(reach - holding[i], max(1, remaining * weights[i] // pool), rest)
            holding[i] = holding[i] + extra
            rest = rest - extra
    return np.array(holding)


def gaussian(own_key, shape, width, most, cuts=(), kind=jnp.bfloat16):
    drawn = jax.random.normal(own_key, shape, jnp.float32) * width
    if len(cuts) > 0:
        drawn = block_scale(own_key, shape, cuts, -0.22, 0.18) * drawn
    return jnp.clip(drawn, min=-most, max=most).astype(kind)


def setup_inputs(seed: int = 0) -> dict:
    splits = jax.random.split(jax.random.key(seed), 8)
    queries = draw_queries(jax.random.fold_in(splits[7], 71), 0)
    span_keys = gaussian(splits[1], (TOKENS, KVH * HD), 1.0, 6.0, ((0, 16),))
    span_values = gaussian(splits[2], (TOKENS, KVH * HD), 1.0, 6.0, ((0, 16),))
    cache_keys = gaussian(splits[3], (KVH * PREFIX, HD), 1.0, 6.0, ((0, 128),))
    cache_values = gaussian(splits[4], (KVH * PREFIX, HD), 1.0, 6.0, ((0, 128),))
    chosen_keys = jax.random.split(jax.random.fold_in(splits[5], 1), NQB // NQB)
    chosen_turns = jax.random.permutation(jax.random.fold_in(splits[5], 3), NQB // NQB)
    chosen = jax.vmap(lambda own, number: routed_block(jax.random.fold_in(splits[5], 2), own, number, NQB, NKB, TOPK, MOST, 2))(chosen_keys, chosen_turns).reshape((NQB, TOPK))
    out_weight = gaussian(splits[6], (H * HD, D), (H * HD) ** -0.5, 0.09375, ((0, 16), (1, 8)))
    return dict(queries=queries, span_keys=span_keys, span_values=span_values, cache_keys=cache_keys, cache_values=cache_values, chosen=chosen, out_weight=out_weight)


FLOOR_SCORE = -1e+30

def segment_terms(query_rows, key_rows, value_rows, key_mask):
    scores = jnp.einsum('vgqd,vkd->vgqk', query_rows.astype(jnp.float32), key_rows.astype(jnp.float32)) * (1.0 / math.sqrt(HD))
    if key_mask is not None:
        scores = jnp.where(key_mask, scores, FLOOR_SCORE)
    row_peak = lax.optimization_barrier(jnp.max(scores, axis=-1))
    weights = jnp.exp(scores - row_peak[..., None])
    row_total = lax.optimization_barrier(jnp.sum(weights, axis=-1))
    rounded = lax.optimization_barrier(weights.astype(jnp.bfloat16))
    summed = jnp.einsum('vgqk,vkd->vgqd', rounded.astype(jnp.float32), value_rows.astype(jnp.float32))
    return (row_peak, row_total, summed)

def reference(queries, span_keys, span_values, cache_keys, cache_values, chosen, out_weight):
    cache_k = cache_keys.reshape(KVH, PREFIX, HD)
    cache_v = cache_values.reshape(KVH, PREFIX, HD)
    span_k = span_keys.reshape(TOKENS, KVH, HD)
    span_v = span_values.reshape(TOKENS, KVH, HD)
    causal = jnp.arange(QB)[:, None] >= jnp.arange(QB)[None, :]

    def one_block(block_index):
        row_start = (block_index * QB).astype(jnp.int32)
        query_rows = lax.dynamic_slice_in_dim(queries, row_start, QB, 0).reshape(QB, KVH, GROUP, HD).transpose(1, 2, 0, 3)
        own_k = lax.dynamic_slice_in_dim(span_k, row_start, QB, 0).transpose(1, 0, 2)
        own_v = lax.dynamic_slice_in_dim(span_v, row_start, QB, 0).transpose(1, 0, 2)
        segments = [segment_terms(query_rows, own_k, own_v, causal[None, None])]
        for slot_index in range(TOPK):
            first_row = (chosen[block_index, slot_index] * KB).astype(jnp.int32)
            block_k = lax.dynamic_slice_in_dim(cache_k, first_row, KB, 1)
            block_v = lax.dynamic_slice_in_dim(cache_v, first_row, KB, 1)
            segments.append(segment_terms(query_rows, block_k, block_v, None))
        row_peak = segments[0][0]
        for segment in segments[1:]:
            row_peak = jnp.maximum(row_peak, segment[0])
        row_total = jnp.zeros_like(row_peak)
        summed = jnp.zeros(row_peak.shape + (HD,), jnp.float32)
        for segment in segments:
            factor = jnp.exp(segment[0] - row_peak)
            row_total = row_total + segment[1] * factor
            summed = summed + segment[2] * factor[..., None]
        result = (summed / row_total[..., None]).transpose(2, 0, 1, 3).reshape(QB, H * HD)
        return result.astype(jnp.bfloat16)
    attended = lax.map(one_block, jnp.arange(NQB, dtype=jnp.int32)).reshape(TOKENS, H * HD)
    return jnp.dot(attended, out_weight, preferred_element_type=jnp.float32).astype(jnp.bfloat16)
```

```python
import math

import jax
import jax.numpy as jnp
from jax import lax
from jax.experimental import pallas as pl
from jax.experimental.pallas import tpu as pltpu
from jax.sharding import PartitionSpec as P

HD = 128
QB = 512
KB = 4096
NQB = 8
NW = 16
KVH = 8
HALF = 256
ROWS = 2 * QB
CHUNK = 512
FLOOR_SCORE = -1e30
SCALE2 = math.log2(math.e) / math.sqrt(HD)
MESH = pl.DeviceIdType.MESH
MIB = 2**20


def place():
    wide = lax.axis_index("wide")
    narrow = lax.axis_index("narrow")
    return wide, narrow, narrow // 2, narrow % 2


def remote(src, dst, send_sem, recv_sem, device):
    return pltpu.make_async_remote_copy(
        src_ref=src, dst_ref=dst, send_sem=send_sem, recv_sem=recv_sem, device_id=device, device_id_type=MESH
    )


def spread_kernel(
    queries, span_k, span_v, cache_k, cache_v,
    q_out, pk_out, pv_out, sk_out, sv_out,
    q_send, q_recv, kv_send, kv_recv, span_send, span_recv, local_sem, span_local,
):
    wide, narrow, y, core = place()
    buddy = y * 2 + 1 - core
    block, half = wide // 2, wide % 2
    barrier = pltpu.get_barrier_semaphore()

    def greet(step, carry):
        pl.semaphore_signal(
            barrier, inc=1, device_id=((wide + step) % NW, narrow), device_id_type=MESH
        )
        return carry

    lax.fori_loop(1, NW, greet, 0)
    pl.semaphore_signal(barrier, inc=1, device_id=(wide, buddy), device_id_type=MESH)
    pl.semaphore_wait(barrier, NW)

    def q_src(kv, head):
        column = pl.multiple_of(kv * 512 + core * 256 + head * HD, HD)
        return queries.at[:, pl.ds(column, HD)]

    def q_dst(source, head):
        return q_out.at[source // 2, pl.ds(pl.multiple_of(head * QB + source % 2 * HALF, HALF), HALF), :]

    def span_pair(kv, which):
        src = (span_k, span_v)[which].at[:, pl.ds(pl.multiple_of(kv * HD, HD), HD)]
        return src

    def span_dst(part, which):
        return (sk_out, sv_out)[which].at[pl.ds(pl.multiple_of(part * HALF, HALF), HALF), :]

    def q_copy(step, head):
        target = (wide + step) % NW
        return remote(
            q_src(target // 2, head), q_dst(wide, head),
            q_send.at[step, head], q_recv.at[wide, head], (target, narrow),
        )

    kv_copies = [
        remote(src, dst, kv_send.at[i], kv_recv.at[i], (wide, buddy))
        for i, (src, dst) in enumerate(((cache_k, pk_out), (cache_v, pv_out)))
    ]
    span_owner = y == block % 4

    def span_copy(kv, which):
        return remote(
            span_pair(kv, which), span_dst(half, which),
            span_send.at[kv, which], span_recv.at[half, which], (kv * 2 + block // 4, narrow),
        )

    def span_own(kv, which):
        return pltpu.make_async_copy(span_pair(kv, which), span_dst(half, which), span_local.at[which])

    self_span = span_owner & (half == block // 4)

    def start_q(step, carry):
        for head in range(2):
            q_copy(step, head).start()
        return carry

    lax.fori_loop(1, NW, start_q, 0)
    for head in range(2):
        pltpu.make_async_copy(q_src(wide // 2, head), q_dst(wide, head), local_sem.at[head]).start()

    def each_span(kv, carry, act):
        @pl.when(span_owner & (kv * 2 + block // 4 != wide))
        def _():
            for which in range(2):
                act(span_copy(kv, which))

        return carry

    lax.fori_loop(0, KVH, lambda kv, c: each_span(kv, c, lambda copy: copy.start()), 0)

    @pl.when(self_span)
    def _():
        for which in range(2):
            span_own(block, which).start()

    for copy in kv_copies:
        copy.start()

    for head in range(2):
        pltpu.make_async_copy(q_src(wide // 2, head), q_dst(wide, head), local_sem.at[head]).wait()

    def wait_q(step, carry):
        source = (wide + NW - step) % NW
        for head in range(2):
            q_copy(step, head).wait_send()
            remote(
                q_src(0, head), q_dst(source, head), q_send.at[step, head], q_recv.at[source, head], (source, narrow)
            ).wait_recv()
        return carry

    lax.fori_loop(1, NW, wait_q, 0)
    lax.fori_loop(0, KVH, lambda kv, c: each_span(kv, c, lambda copy: copy.wait_send()), 0)

    @pl.when(self_span)
    def _():
        for which in range(2):
            span_own(block, which).wait()

    held = wide % 2 * 4 + y
    for part in range(2):
        @pl.when(held * 2 + part != wide)
        def _():
            for which in range(2):
                remote(
                    span_pair(0, which), span_dst(part, which),
                    span_send.at[0, which], span_recv.at[part, which], (wide, buddy),
                ).wait_recv()

    for copy in kv_copies:
        copy.wait()


def spread(queries, span_k, span_v, cache_k, cache_v):
    anywhere = pl.BlockSpec(memory_space=pl.ANY)
    shape = lambda *dims: jax.ShapeDtypeStruct(dims, jnp.bfloat16)
    dma = pltpu.SemaphoreType.DMA
    return pl.pallas_call(
        spread_kernel,
        out_shape=[shape(NQB, ROWS, HD), shape(KB, HD), shape(KB, HD), shape(QB, HD), shape(QB, HD)],
        in_specs=[anywhere] * 5,
        out_specs=[anywhere] * 5,
        scratch_shapes=[
            dma((NW, 2)), dma((NW, 2)), dma((2,)), dma((2,)), dma((KVH, 2)), dma((2, 2)), dma((2,)), dma((2,)),
        ],
        compiler_params=pltpu.CompilerParams(collective_id=0, has_side_effects=True),
    )(queries, span_k, span_v, cache_k, cache_v)


def attend_kernel(chosen, q, k_own, v_own, k_pair, v_pair, sk, sv, out, lse, k_both, v_wide, s_wide, acc, peak):
    wide, narrow, y, core = place()
    held = wide % 2 * 4 + y
    first = wide % 2 * 8 + y * 2
    k_both[0] = k_own[...]
    k_both[1] = k_pair[...]
    for i, v in enumerate((v_own, v_pair)):
        v_wide[i, :, :HD] = v[...]
        v_wide[i, :, HD:] = jnp.ones((KB, HD), jnp.bfloat16)
    s_wide[:, :HD] = sv[...]
    s_wide[:, HD:] = jnp.ones((QB, HD), jnp.bfloat16)

    def fold(state, queries, keys, values, mask):
        top, total = state
        scores = lax.dot_general(queries, keys, (((1,), (1,)), ((), ())), preferred_element_type=jnp.float32)
        if mask is not None:
            scores = jnp.where(mask, scores, FLOOR_SCORE)
        new_top = jnp.maximum(top, jnp.max(scores, axis=1, keepdims=True))
        decay = jnp.exp2((top - new_top) * SCALE2)
        weights = jnp.exp2((scores - new_top) * SCALE2).astype(jnp.bfloat16)
        total = total * decay + jnp.dot(weights, values, preferred_element_type=jnp.float32)
        return new_top, total

    def load():
        return peak[:, :1], acc[...]

    def save(state):
        peak[...] = jnp.broadcast_to(state[0], (ROWS, HD))
        acc[...] = state[1]

    def one_block(b, carry):
        hits = []
        for i in range(2):
            c = first + jnp.where(core == 0, i, 1 - i)
            hits.append((chosen[b, 0] == c) | (chosen[b, 1] == c) | (chosen[b, 2] == c))
        used = hits[0] | hits[1] | (b == held)

        @pl.when(used)
        def _():
            acc[...] = jnp.zeros((ROWS, 2 * HD), jnp.float32)
            peak[...] = jnp.full((ROWS, HD), FLOOR_SCORE, jnp.float32)

        @pl.when(b == held)
        def _():
            row = lax.broadcasted_iota(jnp.int32, (ROWS, QB), 0) % QB
            mask = row >= lax.broadcasted_iota(jnp.int32, (ROWS, QB), 1)
            save(fold(load(), q[b], sk[...], s_wide[...], mask))

        def cached(i, carry):
            @pl.when(jnp.where(i == 0, hits[0], hits[1]))
            def _():
                queries = q[b]
                state = load()
                for start in range(0, KB, CHUNK):
                    state = fold(
                        state, queries, k_both[i, start:start + CHUNK, :], v_wide[i, start:start + CHUNK, :], None
                    )
                save(state)

            return carry

        lax.fori_loop(0, 2, cached, 0)

        @pl.when(used)
        def _():
            total = acc[:, HD:]
            out[b] = (acc[:, :HD] / total).astype(jnp.bfloat16)
            logs = peak[...] * SCALE2 + jnp.log2(total)
            eye = lax.broadcasted_iota(jnp.int32, (HD, HD), 0) == lax.broadcasted_iota(jnp.int32, (HD, HD), 1)
            for g in range(ROWS // HD):
                lse[b, g:g + 1, :] = jnp.sum(
                    jnp.where(eye, logs[g * HD:(g + 1) * HD], 0.0), axis=0, keepdims=True
                )

        @pl.when(jnp.logical_not(used))
        def _():
            out[b] = jnp.zeros((ROWS, HD), jnp.bfloat16)
            lse[b] = jnp.full((8, HD), FLOOR_SCORE, jnp.float32)

        return carry

    lax.fori_loop(0, NQB, one_block, 0)


def attend(chosen, q, k_own, v_own, k_pair, v_pair, sk, sv):
    vmem = pl.BlockSpec(memory_space=pltpu.VMEM)
    return pl.pallas_call(
        attend_kernel,
        out_shape=[
            jax.ShapeDtypeStruct((NQB, ROWS, HD), jnp.bfloat16),
            jax.ShapeDtypeStruct((NQB, 8, HD), jnp.float32),
        ],
        in_specs=[pl.BlockSpec(memory_space=pltpu.SMEM)] + [vmem] * 7,
        out_specs=[vmem] * 2,
        scratch_shapes=[
            pltpu.VMEM((2, KB, HD), jnp.bfloat16),
            pltpu.VMEM((2, KB, 2 * HD), jnp.bfloat16),
            pltpu.VMEM((QB, 2 * HD), jnp.bfloat16),
            pltpu.VMEM((ROWS, 2 * HD), jnp.float32),
            pltpu.VMEM((ROWS, HD), jnp.float32),
        ],
        compiler_params=pltpu.CompilerParams(vmem_limit_bytes=56 * MIB),
        cost_estimate=pl.CostEstimate(flops=14 * 10**9, bytes_accessed=10 * MIB, transcendentals=25 * 10**6),
    )(chosen, q, k_own, v_own, k_pair, v_pair, sk, sv)


def finish_kernel(
    part, lse, weight, result,
    p_in, l_in, w_in, rows_out, rows_in,
    p_send, p_recv, l_send, l_recv, a_send, a_recv, f_send, f_recv, local_sem,
):
    wide, narrow, y, core = place()
    buddy = y * 2 + 1 - core
    kv = wide // 2
    held = wide % 2 * 4 + y
    mine = wide // 2
    barrier = pltpu.get_barrier_semaphore()

    def combiner(b):
        return kv * 2 + b // 4, b % 4 * 2 + core

    def source(s):
        return s * 2 + mine // 4, mine % 4 * 2 + core

    def target(t):
        return held * 2 + t // 4, t % 4 * 2 + core

    own_target = wide // 2 == held
    fetch = pltpu.make_async_copy(weight, w_in, local_sem.at[0])
    fetch.start()
    keep = [
        pltpu.make_async_copy(part.at[held], p_in.at[held], local_sem.at[1]),
        pltpu.make_async_copy(lse.at[held], l_in.at[held], local_sem.at[2]),
    ]
    for copy in keep:
        copy.start()

    def greet(step, carry):
        pl.semaphore_signal(barrier, inc=1, device_id=combiner((held + step) % 8), device_id_type=MESH)
        return carry

    lax.fori_loop(1, 8, greet, 0)

    def greet_source(s, carry):
        @pl.when(jnp.logical_not(own_target & (s == kv)))
        def _():
            pl.semaphore_signal(barrier, inc=1, device_id=source(s), device_id_type=MESH)

        return carry

    lax.fori_loop(0, 8, greet_source, 0)
    pl.semaphore_signal(barrier, inc=1, device_id=(wide, buddy), device_id_type=MESH)
    pl.semaphore_wait(barrier, 16 - own_target.astype(jnp.int32))

    def part_copies(step):
        b = (held + step) % 8
        return [
            remote(part.at[b], p_in.at[held], p_send.at[step], p_recv.at[held], combiner(b)),
            remote(lse.at[b], l_in.at[held], l_send.at[step], l_recv.at[held], combiner(b)),
        ]

    def start_part(step, carry):
        for copy in part_copies(step):
            copy.start()
        return carry

    lax.fori_loop(1, 8, start_part, 0)
    for copy in keep:
        copy.wait()

    def wait_part(step, carry):
        for copy in part_copies(step):
            copy.wait_send()
        s = (held + step) % 8
        remote(part.at[s], p_in.at[s], p_send.at[step], p_recv.at[s], combiner(s)).wait_recv()
        remote(lse.at[s], l_in.at[s], l_send.at[step], l_recv.at[s], combiner(s)).wait_recv()
        return carry

    lax.fori_loop(1, 8, wait_part, 0)

    logs = l_in[...]
    shares = jnp.exp2(logs - jnp.max(logs, axis=0, keepdims=True))
    shares = shares / jnp.sum(shares, axis=0, keepdims=True)
    turned = jnp.transpose(jnp.concatenate([shares.reshape(64, HD)] * 2, axis=0))
    for g in range(8):
        total = jnp.zeros((HD, HD), jnp.float32)
        for s in range(8):
            rows = p_in[s, g * HD:(g + 1) * HD, :].astype(jnp.float32)
            total = total + rows * turned[:, s * 8 + g:s * 8 + g + 1]
        rows_out[g % 4 * HD:(g % 4 + 1) * HD, g // 4 * HD:(g // 4 + 1) * HD] = total.astype(jnp.bfloat16)

    slot = kv * 2 + core

    def out_part(t):
        return rows_out.at[pl.ds(pl.multiple_of(t // 4 * HALF, HALF), HALF), :]

    def row_copy(t):
        return remote(out_part(t), rows_in.at[slot], a_send.at[t], a_recv.at[slot], target(t))

    own_number = wide % 2 * 4 + y

    def start_row(t, carry):
        away = jnp.logical_not(own_target & (t == own_number))

        @pl.when(away)
        def _():
            row_copy(t).start()

        @pl.when(jnp.logical_not(away))
        def _():
            copy = pltpu.make_async_copy(out_part(t), rows_in.at[slot], local_sem.at[3])
            copy.start()
            copy.wait()

        return carry

    lax.fori_loop(0, 8, start_row, 0)

    def forward(s):
        n = s * 2 + core
        return remote(rows_in.at[n], rows_in.at[n], f_send.at[s], f_recv.at[n], (wide, buddy))

    fetch.wait()

    def product(n):
        return jnp.dot(
            rows_in[n], w_in[pl.ds(pl.multiple_of(n * HALF, HALF), HALF), :], preferred_element_type=jnp.float32
        )

    def arrive(s, total):
        n = s * 2 + core

        @pl.when(jnp.logical_not(own_target & (s == kv)))
        def _():
            remote(rows_in.at[n], rows_in.at[n], f_send.at[s], a_recv.at[n], (wide, buddy)).wait_recv()

        forward(s).start()
        return total + product(n)

    total = lax.fori_loop(0, 8, arrive, jnp.zeros((HALF, 512), jnp.float32))

    def arrive_pair(s, total):
        n = s * 2 + 1 - core
        remote(rows_in.at[n], rows_in.at[n], f_send.at[s], f_recv.at[n], (wide, buddy)).wait_recv()
        return total + product(n)

    total = lax.fori_loop(0, 8, arrive_pair, total)
    result[...] = total.astype(jnp.bfloat16)

    def drain(t, carry):
        @pl.when(jnp.logical_not(own_target & (t == own_number)))
        def _():
            row_copy(t).wait_send()

        forward(t).wait_send()
        return carry

    lax.fori_loop(0, 8, drain, 0)


def finish(part, lse, weight):
    anywhere = pl.BlockSpec(memory_space=pl.ANY)
    dma = pltpu.SemaphoreType.DMA
    return pl.pallas_call(
        finish_kernel,
        out_shape=jax.ShapeDtypeStruct((HALF, 512), jnp.bfloat16),
        in_specs=[anywhere] * 3,
        out_specs=pl.BlockSpec(memory_space=pltpu.VMEM),
        scratch_shapes=[
            pltpu.VMEM((8, ROWS, HD), jnp.bfloat16),
            pltpu.VMEM((8, 8, HD), jnp.float32),
            pltpu.VMEM((4096, 512), jnp.bfloat16),
            pltpu.VMEM((QB, 256), jnp.bfloat16),
            pltpu.VMEM((16, HALF, 256), jnp.bfloat16),
            dma((8,)), dma((8,)), dma((8,)), dma((8,)), dma((8,)), dma((16,)), dma((8,)), dma((16,)), dma((4,)),
        ],
        compiler_params=pltpu.CompilerParams(
            collective_id=1, has_side_effects=True, vmem_limit_bytes=48 * MIB
        ),
    )(part, lse, weight)


def shards(queries, span_keys, span_values, cache_keys, cache_values, chosen, out_weight):
    weight = lax.all_gather(out_weight, "wide", axis=0, tiled=True)
    q, k_pair, v_pair, sk, sv = spread(queries, span_keys, span_values, cache_keys, cache_values)
    part, lse = attend(chosen, q, cache_keys, cache_values, k_pair, v_pair, sk, sv)
    return finish(part, lse, weight)


def solution(mesh):
    return jax.shard_map(
        shards,
        mesh=mesh,
        in_specs=(
            P("wide", None),
            P("wide", None),
            P("wide", None),
            P(("wide", "narrow"), None),
            P(("wide", "narrow"), None),
            P(),
            P("wide", "narrow"),
        ),
        out_specs=P("wide", "narrow"),
        check_vma=False,
    )
```

```python
import math

import jax
import jax.numpy as jnp
from jax import lax
from jax.experimental import pallas as pl
from jax.experimental.pallas import tpu as pltpu
from jax.sharding import PartitionSpec as P

HD = 128
QB = 512
KB = 4096
NQB = 8
NW = 16
KVH = 8
HALF = 256
ROWS = 2 * QB
CHUNK = 256
FLOOR_SCORE = -1e30
SCALE2 = math.log2(math.e) / math.sqrt(HD)
MESH = pl.DeviceIdType.MESH
MIB = 2**20


def place():
    wide = lax.axis_index("wide")
    narrow = lax.axis_index("narrow")
    return wide, narrow, narrow // 2, narrow % 2


def remote(src, dst, send_sem, recv_sem, device):
    return pltpu.make_async_remote_copy(
        src_ref=src, dst_ref=dst, send_sem=send_sem, recv_sem=recv_sem, device_id=device, device_id_type=MESH
    )


def spread_kernel(
    queries, span_k, span_v, cache_k, cache_v,
    q_out, pk_out, pv_out, sk_out, sv_out,
    q_send, q_recv, kv_send, kv_recv, span_send, span_recv, local_sem, span_local,
):
    wide, narrow, y, core = place()
    buddy = y * 2 + 1 - core
    block, half = wide // 2, wide % 2
    barrier = pltpu.get_barrier_semaphore()

    def greet(step, carry):
        pl.semaphore_signal(
            barrier, inc=1, device_id=((wide + step) % NW, narrow), device_id_type=MESH
        )
        return carry

    lax.fori_loop(1, NW, greet, 0)
    pl.semaphore_signal(barrier, inc=1, device_id=(wide, buddy), device_id_type=MESH)
    pl.semaphore_wait(barrier, NW)

    def q_src(kv, head):
        column = pl.multiple_of(kv * 512 + core * 256 + head * HD, HD)
        return queries.at[:, pl.ds(column, HD)]

    def q_dst(source, head):
        return q_out.at[source // 2, pl.ds(pl.multiple_of(head * QB + source % 2 * HALF, HALF), HALF), :]

    def span_pair(kv, which):
        src = (span_k, span_v)[which].at[:, pl.ds(pl.multiple_of(kv * HD, HD), HD)]
        return src

    def span_dst(part, which):
        return (sk_out, sv_out)[which].at[pl.ds(pl.multiple_of(part * HALF, HALF), HALF), :]

    def q_copy(step, head):
        target = (wide + step) % NW
        return remote(
            q_src(target // 2, head), q_dst(wide, head),
            q_send.at[step, head], q_recv.at[wide, head], (target, narrow),
        )

    kv_copies = [
        remote(src, dst, kv_send.at[i], kv_recv.at[i], (wide, buddy))
        for i, (src, dst) in enumerate(((cache_k, pk_out), (cache_v, pv_out)))
    ]
    span_owner = y == block % 4

    def span_copy(kv, which):
        return remote(
            span_pair(kv, which), span_dst(half, which),
            span_send.at[kv, which], span_recv.at[half, which], (kv * 2 + block // 4, narrow),
        )

    def span_own(kv, which):
        return pltpu.make_async_copy(span_pair(kv, which), span_dst(half, which), span_local.at[which])

    self_span = span_owner & (half == block // 4)

    def start_q(step, carry):
        for head in range(2):
            q_copy(step, head).start()
        return carry

    lax.fori_loop(1, NW, start_q, 0)
    for head in range(2):
        pltpu.make_async_copy(q_src(wide // 2, head), q_dst(wide, head), local_sem.at[head]).start()

    def each_span(kv, carry, act):
        @pl.when(span_owner & (kv * 2 + block // 4 != wide))
        def _():
            for which in range(2):
                act(span_copy(kv, which))

        return carry

    lax.fori_loop(0, KVH, lambda kv, c: each_span(kv, c, lambda copy: copy.start()), 0)

    @pl.when(self_span)
    def _():
        for which in range(2):
            span_own(block, which).start()

    for copy in kv_copies:
        copy.start()

    for head in range(2):
        pltpu.make_async_copy(q_src(wide // 2, head), q_dst(wide, head), local_sem.at[head]).wait()

    def wait_q(step, carry):
        source = (wide + NW - step) % NW
        for head in range(2):
            q_copy(step, head).wait_send()
            remote(
                q_src(0, head), q_dst(source, head), q_send.at[step, head], q_recv.at[source, head], (source, narrow)
            ).wait_recv()
        return carry

    lax.fori_loop(1, NW, wait_q, 0)
    lax.fori_loop(0, KVH, lambda kv, c: each_span(kv, c, lambda copy: copy.wait_send()), 0)

    @pl.when(self_span)
    def _():
        for which in range(2):
            span_own(block, which).wait()

    held = wide % 2 * 4 + y
    for part in range(2):
        @pl.when(held * 2 + part != wide)
        def _():
            for which in range(2):
                remote(
                    span_pair(0, which), span_dst(part, which),
                    span_send.at[0, which], span_recv.at[part, which], (wide, buddy),
                ).wait_recv()

    for copy in kv_copies:
        copy.wait()


def spread(queries, span_k, span_v, cache_k, cache_v):
    anywhere = pl.BlockSpec(memory_space=pl.ANY)
    shape = lambda *dims: jax.ShapeDtypeStruct(dims, jnp.bfloat16)
    dma = pltpu.SemaphoreType.DMA
    return pl.pallas_call(
        spread_kernel,
        out_shape=[shape(NQB, ROWS, HD), shape(KB, HD), shape(KB, HD), shape(QB, HD), shape(QB, HD)],
        in_specs=[anywhere] * 5,
        out_specs=[anywhere] * 5,
        scratch_shapes=[
            dma((NW, 2)), dma((NW, 2)), dma((2,)), dma((2,)), dma((KVH, 2)), dma((2, 2)), dma((2,)), dma((2,)),
        ],
        compiler_params=pltpu.CompilerParams(
            collective_id=0, has_side_effects=True, vmem_limit_bytes=56 * MIB
        ),
    )(queries, span_k, span_v, cache_k, cache_v)


def attend_kernel(
    chosen, q, k_own, v_own, k_pair, v_pair, sk, sv, out, lse,
    q_in, k_both, v_wide, sk_in, s_wide, out_in, acc, peak, sems, out_sem,
):
    wide, narrow, y, core = place()
    held = wide % 2 * 4 + y
    first = wide % 2 * 8 + y * 2
    moves = [
        (q, q_in),
        (sk, sk_in),
        (sv, s_wide.at[:, :HD]),
        (k_own, k_both.at[0]),
        (v_own, v_wide.at[0, :, :HD]),
        (k_pair, k_both.at[1]),
        (v_pair, v_wide.at[1, :, :HD]),
    ]
    loads = [pltpu.make_async_copy(src, dst, sems.at[i]) for i, (src, dst) in enumerate(moves)]
    for copy in loads:
        copy.start()
    s_wide[:, HD:] = jnp.ones((QB, HD), jnp.bfloat16)
    for i in range(2):
        v_wide[i, :, HD:] = jnp.ones((KB, HD), jnp.bfloat16)

    def fold(state, queries, keys, values, mask):
        top, total = state
        scores = lax.dot_general(queries, keys, (((1,), (1,)), ((), ())), preferred_element_type=jnp.float32)
        if mask is not None:
            scores = jnp.where(mask, scores, FLOOR_SCORE)
        new_top = jnp.maximum(top, jnp.max(scores, axis=1, keepdims=True))
        decay = jnp.exp2((top - new_top) * SCALE2)
        weights = jnp.exp2((scores - new_top) * SCALE2).astype(jnp.bfloat16)
        total = total * decay + jnp.dot(weights, values, preferred_element_type=jnp.float32)
        return new_top, total

    def load():
        return jnp.max(peak[...], axis=1, keepdims=True), acc[...]

    def save(state):
        peak[...] = jnp.broadcast_to(state[0], (ROWS, HD))
        acc[...] = state[1]

    for copy in loads[:3]:
        copy.wait()
    row = lax.broadcasted_iota(jnp.int32, (ROWS, QB), 0) % QB
    mask = row >= lax.broadcasted_iota(jnp.int32, (ROWS, QB), 1)
    fresh = jnp.full((ROWS, 1), FLOOR_SCORE, jnp.float32), jnp.zeros((ROWS, 2 * HD), jnp.float32)
    save(fold(fresh, q_in[held], sk_in[...], s_wide[...], mask))
    for copy in loads[3:]:
        copy.wait()

    def send_out(b):
        return pltpu.make_async_copy(out_in.at[b], out.at[b], out_sem.at[b])

    def one_block(step, carry):
        b = (held + step) % NQB
        hits = []
        for i in range(2):
            c = first + jnp.where(core == 0, i, 1 - i)
            hits.append((chosen[b, 0] == c) | (chosen[b, 1] == c) | (chosen[b, 2] == c))
        used = hits[0] | hits[1] | (step == 0)

        @pl.when(used & (step != 0))
        def _():
            acc[...] = jnp.zeros((ROWS, 2 * HD), jnp.float32)
            peak[...] = jnp.full((ROWS, HD), FLOOR_SCORE, jnp.float32)

        def cached(i, carry):
            @pl.when(jnp.where(i == 0, hits[0], hits[1]))
            def _():
                queries = q_in[b]
                state = load()
                for start in range(0, KB, CHUNK):
                    state = fold(
                        state, queries, k_both[i, start:start + CHUNK, :], v_wide[i, start:start + CHUNK, :], None
                    )
                save(state)

            return carry

        lax.fori_loop(0, 2, cached, 0)

        @pl.when(used)
        def _():
            total = acc[:, HD:]
            out_in[b] = (acc[:, :HD] / total).astype(jnp.bfloat16)
            logs = peak[...] * SCALE2 + jnp.log2(total)
            eye = lax.broadcasted_iota(jnp.int32, (HD, HD), 0) == lax.broadcasted_iota(jnp.int32, (HD, HD), 1)
            for g in range(ROWS // HD):
                lse[b, g:g + 1, :] = jnp.sum(
                    jnp.where(eye, logs[g * HD:(g + 1) * HD], 0.0), axis=0, keepdims=True
                )

        @pl.when(jnp.logical_not(used))
        def _():
            out_in[b] = jnp.zeros((ROWS, HD), jnp.bfloat16)
            lse[b] = jnp.full((8, HD), FLOOR_SCORE, jnp.float32)

        send_out(b).start()
        return carry

    lax.fori_loop(0, NQB, one_block, 0)
    for b in range(NQB):
        send_out(b).wait()


def attend(chosen, q, k_own, v_own, k_pair, v_pair, sk, sv):
    anywhere = pl.BlockSpec(memory_space=pl.ANY)
    dma = pltpu.SemaphoreType.DMA
    return pl.pallas_call(
        attend_kernel,
        out_shape=[
            jax.ShapeDtypeStruct((NQB, ROWS, HD), jnp.bfloat16),
            jax.ShapeDtypeStruct((NQB, 8, HD), jnp.float32),
        ],
        in_specs=[pl.BlockSpec(memory_space=pltpu.SMEM)] + [anywhere] * 7,
        out_specs=[anywhere, pl.BlockSpec(memory_space=pltpu.VMEM)],
        scratch_shapes=[
            pltpu.VMEM((NQB, ROWS, HD), jnp.bfloat16),
            pltpu.VMEM((2, KB, HD), jnp.bfloat16),
            pltpu.VMEM((2, KB, 2 * HD), jnp.bfloat16),
            pltpu.VMEM((QB, HD), jnp.bfloat16),
            pltpu.VMEM((QB, 2 * HD), jnp.bfloat16),
            pltpu.VMEM((NQB, ROWS, HD), jnp.bfloat16),
            pltpu.VMEM((ROWS, 2 * HD), jnp.float32),
            pltpu.VMEM((ROWS, HD), jnp.float32),
            dma((7,)), dma((NQB,)),
        ],
        compiler_params=pltpu.CompilerParams(vmem_limit_bytes=56 * MIB),
        cost_estimate=pl.CostEstimate(flops=14 * 10**9, bytes_accessed=10 * MIB, transcendentals=25 * 10**6),
    )(chosen, q, k_own, v_own, k_pair, v_pair, sk, sv)


def finish_kernel(
    part, lse, weight, result,
    p_in, l_in, w_in, rows_out, rows_in,
    p_send, p_recv, l_send, l_recv, a_send, a_recv, f_send, f_recv, local_sem,
):
    wide, narrow, y, core = place()
    buddy = y * 2 + 1 - core
    kv = wide // 2
    held = wide % 2 * 4 + y
    mine = wide // 2
    barrier = pltpu.get_barrier_semaphore()

    def combiner(b):
        return kv * 2 + b // 4, b % 4 * 2 + core

    def source(s):
        return s * 2 + mine // 4, mine % 4 * 2 + core

    def target(t):
        return held * 2 + t // 4, t % 4 * 2 + core

    own_target = wide // 2 == held
    fetch = pltpu.make_async_copy(weight, w_in, local_sem.at[0])
    fetch.start()
    keep = [
        pltpu.make_async_copy(part.at[held], p_in.at[held], local_sem.at[1]),
        pltpu.make_async_copy(lse.at[held], l_in.at[held], local_sem.at[2]),
    ]
    for copy in keep:
        copy.start()

    def greet(step, carry):
        pl.semaphore_signal(barrier, inc=1, device_id=combiner((held + step) % 8), device_id_type=MESH)
        return carry

    lax.fori_loop(1, 8, greet, 0)

    def greet_source(s, carry):
        @pl.when(jnp.logical_not(own_target & (s == kv)))
        def _():
            pl.semaphore_signal(barrier, inc=1, device_id=source(s), device_id_type=MESH)

        return carry

    lax.fori_loop(0, 8, greet_source, 0)
    pl.semaphore_signal(barrier, inc=1, device_id=(wide, buddy), device_id_type=MESH)
    pl.semaphore_wait(barrier, 16 - own_target.astype(jnp.int32))

    def part_copies(step):
        b = (held + step) % 8
        return [
            remote(part.at[b], p_in.at[held], p_send.at[step], p_recv.at[held], combiner(b)),
            remote(lse.at[b], l_in.at[held], l_send.at[step], l_recv.at[held], combiner(b)),
        ]

    def start_part(step, carry):
        for copy in part_copies(step):
            copy.start()
        return carry

    lax.fori_loop(1, 8, start_part, 0)
    for copy in keep:
        copy.wait()

    def wait_part(step, carry):
        for copy in part_copies(step):
            copy.wait_send()
        s = (held + step) % 8
        remote(part.at[s], p_in.at[s], p_send.at[step], p_recv.at[s], combiner(s)).wait_recv()
        remote(lse.at[s], l_in.at[s], l_send.at[step], l_recv.at[s], combiner(s)).wait_recv()
        return carry

    lax.fori_loop(1, 8, wait_part, 0)

    logs = l_in[...]
    shares = jnp.exp2(logs - jnp.max(logs, axis=0, keepdims=True))
    shares = shares / jnp.sum(shares, axis=0, keepdims=True)
    turned = jnp.transpose(jnp.concatenate([shares.reshape(64, HD)] * 2, axis=0))
    for g in range(8):
        total = jnp.zeros((HD, HD), jnp.float32)
        for s in range(8):
            rows = p_in[s, g * HD:(g + 1) * HD, :].astype(jnp.float32)
            total = total + rows * turned[:, s * 8 + g:s * 8 + g + 1]
        rows_out[g % 4 * HD:(g % 4 + 1) * HD, g // 4 * HD:(g // 4 + 1) * HD] = total.astype(jnp.bfloat16)

    slot = kv * 2 + core

    def out_part(t):
        return rows_out.at[pl.ds(pl.multiple_of(t // 4 * HALF, HALF), HALF), :]

    def row_copy(t):
        return remote(out_part(t), rows_in.at[slot], a_send.at[t], a_recv.at[slot], target(t))

    own_number = wide % 2 * 4 + y

    def start_row(t, carry):
        away = jnp.logical_not(own_target & (t == own_number))

        @pl.when(away)
        def _():
            row_copy(t).start()

        @pl.when(jnp.logical_not(away))
        def _():
            copy = pltpu.make_async_copy(out_part(t), rows_in.at[slot], local_sem.at[3])
            copy.start()
            copy.wait()

        return carry

    lax.fori_loop(0, 8, start_row, 0)

    def forward(s):
        n = s * 2 + core
        return remote(rows_in.at[n], rows_in.at[n], f_send.at[s], f_recv.at[n], (wide, buddy))

    fetch.wait()

    def product(n):
        return jnp.dot(
            rows_in[n], w_in[pl.ds(pl.multiple_of(n * HALF, HALF), HALF), :], preferred_element_type=jnp.float32
        )

    def arrive(s, total):
        n = s * 2 + core

        @pl.when(jnp.logical_not(own_target & (s == kv)))
        def _():
            remote(rows_in.at[n], rows_in.at[n], f_send.at[s], a_recv.at[n], (wide, buddy)).wait_recv()

        forward(s).start()
        return total + product(n)

    total = lax.fori_loop(0, 8, arrive, jnp.zeros((HALF, 512), jnp.float32))

    def arrive_pair(s, total):
        n = s * 2 + 1 - core
        remote(rows_in.at[n], rows_in.at[n], f_send.at[s], f_recv.at[n], (wide, buddy)).wait_recv()
        return total + product(n)

    total = lax.fori_loop(0, 8, arrive_pair, total)
    result[...] = total.astype(jnp.bfloat16)

    def drain(t, carry):
        @pl.when(jnp.logical_not(own_target & (t == own_number)))
        def _():
            row_copy(t).wait_send()

        forward(t).wait_send()
        return carry

    lax.fori_loop(0, 8, drain, 0)


def finish(part, lse, weight):
    anywhere = pl.BlockSpec(memory_space=pl.ANY)
    dma = pltpu.SemaphoreType.DMA
    return pl.pallas_call(
        finish_kernel,
        out_shape=jax.ShapeDtypeStruct((HALF, 512), jnp.bfloat16),
        in_specs=[anywhere] * 3,
        out_specs=pl.BlockSpec(memory_space=pltpu.VMEM),
        scratch_shapes=[
            pltpu.VMEM((8, ROWS, HD), jnp.bfloat16),
            pltpu.VMEM((8, 8, HD), jnp.float32),
            pltpu.VMEM((4096, 512), jnp.bfloat16),
            pltpu.VMEM((QB, 256), jnp.bfloat16),
            pltpu.VMEM((16, HALF, 256), jnp.bfloat16),
            dma((8,)), dma((8,)), dma((8,)), dma((8,)), dma((8,)), dma((16,)), dma((8,)), dma((16,)), dma((4,)),
        ],
        compiler_params=pltpu.CompilerParams(
            collective_id=1, has_side_effects=True, vmem_limit_bytes=48 * MIB
        ),
    )(part, lse, weight)


def shards(queries, span_keys, span_values, cache_keys, cache_values, chosen, out_weight):
    q, k_pair, v_pair, sk, sv = spread(queries, span_keys, span_values, cache_keys, cache_values)
    out_weight, q = lax.optimization_barrier((out_weight, q))
    weight = lax.all_gather(out_weight, "wide", axis=0, tiled=True)
    part, lse = attend(chosen, q, cache_keys, cache_values, k_pair, v_pair, sk, sv)
    return finish(part, lse, weight)


def solution(mesh):
    return jax.shard_map(
        shards,
        mesh=mesh,
        in_specs=(
            P("wide", None),
            P("wide", None),
            P("wide", None),
            P(("wide", "narrow"), None),
            P(("wide", "narrow"), None),
            P(),
            P("wide", "narrow"),
        ),
        out_specs=P("wide", "narrow"),
        check_vma=False,
    )
```

```python
import math

import jax
import jax.numpy as jnp
from jax import lax
from jax.experimental import pallas as pl
from jax.experimental.pallas import tpu as pltpu
from jax.sharding import PartitionSpec as P

HD = 128
QB = 512
KB = 4096
NQB = 8
NW = 16
KVH = 8
HALF = 256
ROWS = 2 * QB
NY = 4
PIECE = HALF // NY
CHUNK = 256
FLOOR_SCORE = -1e30
SCALE2 = math.log2(math.e) / math.sqrt(HD)
MESH = pl.DeviceIdType.MESH
MIB = 2**20


def place():
    wide = lax.axis_index("wide")
    narrow = lax.axis_index("narrow")
    return wide, narrow, narrow // 2, narrow % 2


def remote(src, dst, send_sem, recv_sem, device):
    return pltpu.make_async_remote_copy(
        src_ref=src, dst_ref=dst, send_sem=send_sem, recv_sem=recv_sem, device_id=device, device_id_type=MESH
    )


def spread_kernel(
    queries, span_k, span_v, cache_k, cache_v,
    q_out, pk_out, pv_out, sk_out, sv_out,
    q_send, q_recv, ring_send, ring_recv, pass_send, pass_recv,
    kv_send, kv_recv, span_send, span_recv, local_sem, span_local,
):
    wide, narrow, y, core = place()
    buddy = y * 2 + 1 - core
    block, half = wide // 2, wide % 2
    barrier = pltpu.get_barrier_semaphore()

    def greet(step, carry):
        pl.semaphore_signal(
            barrier, inc=1, device_id=((wide + step) % NW, narrow), device_id_type=MESH
        )
        return carry

    lax.fori_loop(1, NW, greet, 0)
    ring = [(y + 1) % NY * 2 + core, (y + NY - 1) % NY * 2 + core]
    for neighbour in (buddy, *ring):
        pl.semaphore_signal(barrier, inc=1, device_id=(wide, neighbour), device_id_type=MESH)
    pl.semaphore_wait(barrier, NW + 2)

    def q_src(kv, head):
        column = pl.multiple_of(kv * 512 + core * 256 + head * HD, HD)
        return queries.at[pl.ds(pl.multiple_of(y * PIECE, PIECE), PIECE), pl.ds(column, HD)]

    def q_dst(source, head):
        return q_out.at[head, source, y]

    def batch(group, head, piece):
        return q_out.at[head, pl.ds(group * 4, 4), piece]

    def ring_copy(group, head, direction, piece):
        return remote(
            batch(group, head, piece), batch(group, head, piece),
            ring_send.at[group, head, direction], ring_recv.at[group, head, direction], (wide, ring[direction]),
        )

    def pass_copy(group, head, piece):
        return remote(
            batch(group, head, piece), batch(group, head, piece),
            pass_send.at[group, head], pass_recv.at[group, head], (wide, ring[head]),
        )

    def span_pair(kv, which):
        src = (span_k, span_v)[which].at[:, pl.ds(pl.multiple_of(kv * HD, HD), HD)]
        return src

    def span_dst(part, which):
        return (sk_out, sv_out)[which].at[pl.ds(pl.multiple_of(part * HALF, HALF), HALF), :]

    def q_copy(step, head):
        target = (wide + step) % NW
        return remote(
            q_src(target // 2, head), q_dst(wide, head),
            q_send.at[step, head], q_recv.at[wide, head], (target, narrow),
        )

    kv_copies = [
        remote(src, dst, kv_send.at[i], kv_recv.at[i], (wide, buddy))
        for i, (src, dst) in enumerate(((cache_k, pk_out), (cache_v, pv_out)))
    ]
    span_owner = y == block % 4

    def span_copy(kv, which):
        return remote(
            span_pair(kv, which), span_dst(half, which),
            span_send.at[kv, which], span_recv.at[half, which], (kv * 2 + block // 4, narrow),
        )

    def span_own(kv, which):
        return pltpu.make_async_copy(span_pair(kv, which), span_dst(half, which), span_local.at[which])

    self_span = span_owner & (half == block // 4)

    def start_q(step, carry):
        for head in range(2):
            q_copy(step, head).start()
        return carry

    lax.fori_loop(1, NW, start_q, 0)
    for head in range(2):
        pltpu.make_async_copy(q_src(wide // 2, head), q_dst(wide, head), local_sem.at[head]).start()

    def each_span(kv, carry, act):
        @pl.when(span_owner & (kv * 2 + block // 4 != wide))
        def _():
            for which in range(2):
                act(span_copy(kv, which))

        return carry

    lax.fori_loop(0, KVH, lambda kv, c: each_span(kv, c, lambda copy: copy.start()), 0)

    @pl.when(self_span)
    def _():
        for which in range(2):
            span_own(block, which).start()

    for copy in kv_copies:
        copy.start()

    for head in range(2):
        pltpu.make_async_copy(q_src(wide // 2, head), q_dst(wide, head), local_sem.at[head]).wait()
    behind = [(y + NY - 1) % NY, (y + 1) % NY]

    def gather_batch(step, carry):
        group = (wide // 4 + step) % 4

        def wait_source(i, carry):
            source = group * 4 + i

            @pl.when(source != wide)
            def _():
                for head in range(2):
                    remote(
                        q_src(0, head), q_dst(source, head),
                        q_send.at[0, head], q_recv.at[source, head], (source, narrow),
                    ).wait_recv()

            return carry

        lax.fori_loop(0, 4, wait_source, 0)
        for head in range(2):
            for direction in range(2):
                ring_copy(group, head, direction, y).start()
        return carry

    lax.fori_loop(0, 4, gather_batch, 0)

    def pass_batch(step, carry):
        group = (wide // 4 + step) % 4
        for head in range(2):
            ring_copy(group, head, head, behind[head]).wait_recv()
            pass_copy(group, head, behind[head]).start()
        return carry

    lax.fori_loop(0, 4, pass_batch, 0)

    def finish_batch(step, carry):
        group = (wide // 4 + step) % 4
        for head in range(2):
            ring_copy(group, head, 1 - head, behind[1 - head]).wait_recv()
            pass_copy(group, head, (y + 2) % NY).wait_recv()
            pass_copy(group, head, behind[head]).wait_send()
            for direction in range(2):
                ring_copy(group, head, direction, y).wait_send()
        return carry

    lax.fori_loop(0, 4, finish_batch, 0)

    def wait_q(step, carry):
        for head in range(2):
            q_copy(step, head).wait_send()
        return carry

    lax.fori_loop(1, NW, wait_q, 0)
    lax.fori_loop(0, KVH, lambda kv, c: each_span(kv, c, lambda copy: copy.wait_send()), 0)

    @pl.when(self_span)
    def _():
        for which in range(2):
            span_own(block, which).wait()

    held = wide % 2 * 4 + y
    for part in range(2):
        @pl.when(held * 2 + part != wide)
        def _():
            for which in range(2):
                remote(
                    span_pair(0, which), span_dst(part, which),
                    span_send.at[0, which], span_recv.at[part, which], (wide, buddy),
                ).wait_recv()

    for copy in kv_copies:
        copy.wait()


def spread(queries, span_k, span_v, cache_k, cache_v):
    anywhere = pl.BlockSpec(memory_space=pl.ANY)
    shape = lambda *dims: jax.ShapeDtypeStruct(dims, jnp.bfloat16)
    dma = pltpu.SemaphoreType.DMA
    return pl.pallas_call(
        spread_kernel,
        out_shape=[shape(2, NW, NY, PIECE, HD), shape(KB, HD), shape(KB, HD), shape(QB, HD), shape(QB, HD)],
        in_specs=[anywhere] * 5,
        out_specs=[anywhere] * 5,
        scratch_shapes=[
            dma((NW, 2)), dma((NW, 2)), dma((4, 2, 2)), dma((4, 2, 2)), dma((4, 2)), dma((4, 2)),
            dma((2,)), dma((2,)), dma((KVH, 2)), dma((2, 2)), dma((2,)), dma((2,)),
        ],
        compiler_params=pltpu.CompilerParams(
            collective_id=0, has_side_effects=True, vmem_limit_bytes=56 * MIB
        ),
    )(queries, span_k, span_v, cache_k, cache_v)


def attend_kernel(
    chosen, q, k_own, v_own, k_pair, v_pair, sk, sv, out, lse,
    q_in, k_both, v_wide, sk_in, s_wide, out_in, acc, peak, sems, out_sem,
):
    wide, narrow, y, core = place()
    held = wide % 2 * 4 + y
    first = wide % 2 * 8 + y * 2
    moves = [
        (q, q_in),
        (sk, sk_in),
        (sv, s_wide.at[:, :HD]),
        (k_own, k_both.at[0]),
        (v_own, v_wide.at[0, :, :HD]),
        (k_pair, k_both.at[1]),
        (v_pair, v_wide.at[1, :, :HD]),
    ]
    loads = [pltpu.make_async_copy(src, dst, sems.at[i]) for i, (src, dst) in enumerate(moves)]
    for copy in loads:
        copy.start()
    s_wide[:, HD:] = jnp.ones((QB, HD), jnp.bfloat16)
    for i in range(2):
        v_wide[i, :, HD:] = jnp.ones((KB, HD), jnp.bfloat16)

    def fold(state, queries, keys, values, mask):
        top, total = state
        scores = lax.dot_general(queries, keys, (((1,), (1,)), ((), ())), preferred_element_type=jnp.float32)
        if mask is not None:
            scores = jnp.where(mask, scores, FLOOR_SCORE)
        new_top = jnp.maximum(top, jnp.max(scores, axis=1, keepdims=True))
        decay = jnp.exp2((top - new_top) * SCALE2)
        weights = jnp.exp2((scores - new_top) * SCALE2).astype(jnp.bfloat16)
        total = total * decay + jnp.dot(weights, values, preferred_element_type=jnp.float32)
        return new_top, total

    def block_queries(b):
        return q_in[:, pl.ds(b * 2, 2)].reshape(ROWS, HD)

    def load():
        return jnp.max(peak[...], axis=1, keepdims=True), acc[...]

    def save(state):
        peak[...] = jnp.broadcast_to(state[0], (ROWS, HD))
        acc[...] = state[1]

    for copy in loads[:3]:
        copy.wait()
    row = lax.broadcasted_iota(jnp.int32, (ROWS, QB), 0) % QB
    mask = row >= lax.broadcasted_iota(jnp.int32, (ROWS, QB), 1)
    fresh = jnp.full((ROWS, 1), FLOOR_SCORE, jnp.float32), jnp.zeros((ROWS, 2 * HD), jnp.float32)
    save(fold(fresh, block_queries(held), sk_in[...], s_wide[...], mask))
    for copy in loads[3:]:
        copy.wait()

    def send_out(b):
        return pltpu.make_async_copy(out_in.at[b], out.at[b], out_sem.at[b])

    def one_block(step, carry):
        b = (held + step) % NQB
        hits = []
        for i in range(2):
            c = first + jnp.where(core == 0, i, 1 - i)
            hits.append((chosen[b, 0] == c) | (chosen[b, 1] == c) | (chosen[b, 2] == c))
        used = hits[0] | hits[1] | (step == 0)

        @pl.when(used & (step != 0))
        def _():
            acc[...] = jnp.zeros((ROWS, 2 * HD), jnp.float32)
            peak[...] = jnp.full((ROWS, HD), FLOOR_SCORE, jnp.float32)

        def cached(i, carry):
            @pl.when(jnp.where(i == 0, hits[0], hits[1]))
            def _():
                queries = block_queries(b)
                state = load()
                for start in range(0, KB, CHUNK):
                    state = fold(
                        state, queries, k_both[i, start:start + CHUNK, :], v_wide[i, start:start + CHUNK, :], None
                    )
                save(state)

            return carry

        lax.fori_loop(0, 2, cached, 0)

        @pl.when(used)
        def _():
            total = acc[:, HD:]
            out_in[b] = (acc[:, :HD] / total).astype(jnp.bfloat16)
            logs = peak[...] * SCALE2 + jnp.log2(total)
            eye = lax.broadcasted_iota(jnp.int32, (HD, HD), 0) == lax.broadcasted_iota(jnp.int32, (HD, HD), 1)
            for g in range(ROWS // HD):
                lse[b, g:g + 1, :] = jnp.sum(
                    jnp.where(eye, logs[g * HD:(g + 1) * HD], 0.0), axis=0, keepdims=True
                )

        @pl.when(jnp.logical_not(used))
        def _():
            out_in[b] = jnp.zeros((ROWS, HD), jnp.bfloat16)
            lse[b] = jnp.full((8, HD), FLOOR_SCORE, jnp.float32)

        send_out(b).start()
        return carry

    lax.fori_loop(0, NQB, one_block, 0)
    for b in range(NQB):
        send_out(b).wait()


def attend(chosen, q, k_own, v_own, k_pair, v_pair, sk, sv):
    anywhere = pl.BlockSpec(memory_space=pl.ANY)
    dma = pltpu.SemaphoreType.DMA
    return pl.pallas_call(
        attend_kernel,
        out_shape=[
            jax.ShapeDtypeStruct((NQB, ROWS, HD), jnp.bfloat16),
            jax.ShapeDtypeStruct((NQB, 8, HD), jnp.float32),
        ],
        in_specs=[pl.BlockSpec(memory_space=pltpu.SMEM)] + [anywhere] * 7,
        out_specs=[anywhere, pl.BlockSpec(memory_space=pltpu.VMEM)],
        scratch_shapes=[
            pltpu.VMEM((2, NW, NY, PIECE, HD), jnp.bfloat16),
            pltpu.VMEM((2, KB, HD), jnp.bfloat16),
            pltpu.VMEM((2, KB, 2 * HD), jnp.bfloat16),
            pltpu.VMEM((QB, HD), jnp.bfloat16),
            pltpu.VMEM((QB, 2 * HD), jnp.bfloat16),
            pltpu.VMEM((NQB, ROWS, HD), jnp.bfloat16),
            pltpu.VMEM((ROWS, 2 * HD), jnp.float32),
            pltpu.VMEM((ROWS, HD), jnp.float32),
            dma((7,)), dma((NQB,)),
        ],
        compiler_params=pltpu.CompilerParams(vmem_limit_bytes=56 * MIB),
        cost_estimate=pl.CostEstimate(flops=14 * 10**9, bytes_accessed=10 * MIB, transcendentals=25 * 10**6),
    )(chosen, q, k_own, v_own, k_pair, v_pair, sk, sv)


def finish_kernel(
    part, lse, weight, result,
    p_in, l_in, w_in, rows_out, rows_in,
    p_send, p_recv, l_send, l_recv, a_send, a_recv, f_send, f_recv, local_sem,
):
    wide, narrow, y, core = place()
    buddy = y * 2 + 1 - core
    kv = wide // 2
    held = wide % 2 * 4 + y
    mine = wide // 2
    barrier = pltpu.get_barrier_semaphore()

    def combiner(b):
        return kv * 2 + b // 4, b % 4 * 2 + core

    def source(s):
        return s * 2 + mine // 4, mine % 4 * 2 + core

    def target(t):
        return held * 2 + t // 4, t % 4 * 2 + core

    own_target = wide // 2 == held
    fetch = pltpu.make_async_copy(weight, w_in, local_sem.at[0])
    fetch.start()
    keep = [
        pltpu.make_async_copy(part.at[held], p_in.at[held], local_sem.at[1]),
        pltpu.make_async_copy(lse.at[held], l_in.at[held], local_sem.at[2]),
    ]
    for copy in keep:
        copy.start()

    def greet(step, carry):
        pl.semaphore_signal(barrier, inc=1, device_id=combiner((held + step) % 8), device_id_type=MESH)
        return carry

    lax.fori_loop(1, 8, greet, 0)

    def greet_source(s, carry):
        @pl.when(jnp.logical_not(own_target & (s == kv)))
        def _():
            pl.semaphore_signal(barrier, inc=1, device_id=source(s), device_id_type=MESH)

        return carry

    lax.fori_loop(0, 8, greet_source, 0)
    pl.semaphore_signal(barrier, inc=1, device_id=(wide, buddy), device_id_type=MESH)
    pl.semaphore_wait(barrier, 16 - own_target.astype(jnp.int32))

    def part_copies(step):
        b = (held + step) % 8
        return [
            remote(part.at[b], p_in.at[held], p_send.at[step], p_recv.at[held], combiner(b)),
            remote(lse.at[b], l_in.at[held], l_send.at[step], l_recv.at[held], combiner(b)),
        ]

    def start_part(step, carry):
        for copy in part_copies(step):
            copy.start()
        return carry

    lax.fori_loop(1, 8, start_part, 0)
    for copy in keep:
        copy.wait()

    def wait_part(step, carry):
        for copy in part_copies(step):
            copy.wait_send()
        s = (held + step) % 8
        remote(part.at[s], p_in.at[s], p_send.at[step], p_recv.at[s], combiner(s)).wait_recv()
        remote(lse.at[s], l_in.at[s], l_send.at[step], l_recv.at[s], combiner(s)).wait_recv()
        return carry

    lax.fori_loop(1, 8, wait_part, 0)

    logs = l_in[...]
    shares = jnp.exp2(logs - jnp.max(logs, axis=0, keepdims=True))
    shares = shares / jnp.sum(shares, axis=0, keepdims=True)
    turned = jnp.transpose(jnp.concatenate([shares.reshape(64, HD)] * 2, axis=0))
    for g in range(8):
        total = jnp.zeros((HD, HD), jnp.float32)
        for s in range(8):
            rows = p_in[s, g * HD:(g + 1) * HD, :].astype(jnp.float32)
            total = total + rows * turned[:, s * 8 + g:s * 8 + g + 1]
        rows_out[g % 4 * HD:(g % 4 + 1) * HD, g // 4 * HD:(g // 4 + 1) * HD] = total.astype(jnp.bfloat16)

    slot = kv * 2 + core

    def out_part(t):
        return rows_out.at[pl.ds(pl.multiple_of(t // 4 * HALF, HALF), HALF), :]

    def row_copy(t):
        return remote(out_part(t), rows_in.at[slot], a_send.at[t], a_recv.at[slot], target(t))

    own_number = wide % 2 * 4 + y

    def start_row(t, carry):
        away = jnp.logical_not(own_target & (t == own_number))

        @pl.when(away)
        def _():
            row_copy(t).start()

        @pl.when(jnp.logical_not(away))
        def _():
            copy = pltpu.make_async_copy(out_part(t), rows_in.at[slot], local_sem.at[3])
            copy.start()
            copy.wait()

        return carry

    lax.fori_loop(0, 8, start_row, 0)

    def forward(s):
        n = s * 2 + core
        return remote(rows_in.at[n], rows_in.at[n], f_send.at[s], f_recv.at[n], (wide, buddy))

    fetch.wait()

    def product(n):
        return jnp.dot(
            rows_in[n], w_in[pl.ds(pl.multiple_of(n * HALF, HALF), HALF), :], preferred_element_type=jnp.float32
        )

    def arrive(s, total):
        n = s * 2 + core

        @pl.when(jnp.logical_not(own_target & (s == kv)))
        def _():
            remote(rows_in.at[n], rows_in.at[n], f_send.at[s], a_recv.at[n], (wide, buddy)).wait_recv()

        forward(s).start()
        return total + product(n)

    total = lax.fori_loop(0, 8, arrive, jnp.zeros((HALF, 512), jnp.float32))

    def arrive_pair(s, total):
        n = s * 2 + 1 - core
        remote(rows_in.at[n], rows_in.at[n], f_send.at[s], f_recv.at[n], (wide, buddy)).wait_recv()
        return total + product(n)

    total = lax.fori_loop(0, 8, arrive_pair, total)
    result[...] = total.astype(jnp.bfloat16)

    def drain(t, carry):
        @pl.when(jnp.logical_not(own_target & (t == own_number)))
        def _():
            row_copy(t).wait_send()

        forward(t).wait_send()
        return carry

    lax.fori_loop(0, 8, drain, 0)


def finish(part, lse, weight):
    anywhere = pl.BlockSpec(memory_space=pl.ANY)
    dma = pltpu.SemaphoreType.DMA
    return pl.pallas_call(
        finish_kernel,
        out_shape=jax.ShapeDtypeStruct((HALF, 512), jnp.bfloat16),
        in_specs=[anywhere] * 3,
        out_specs=pl.BlockSpec(memory_space=pltpu.VMEM),
        scratch_shapes=[
            pltpu.VMEM((8, ROWS, HD), jnp.bfloat16),
            pltpu.VMEM((8, 8, HD), jnp.float32),
            pltpu.VMEM((4096, 512), jnp.bfloat16),
            pltpu.VMEM((QB, 256), jnp.bfloat16),
            pltpu.VMEM((16, HALF, 256), jnp.bfloat16),
            dma((8,)), dma((8,)), dma((8,)), dma((8,)), dma((8,)), dma((16,)), dma((8,)), dma((16,)), dma((4,)),
        ],
        compiler_params=pltpu.CompilerParams(
            collective_id=1, has_side_effects=True, vmem_limit_bytes=48 * MIB
        ),
    )(part, lse, weight)


def shards(queries, span_keys, span_values, cache_keys, cache_values, chosen, out_weight):
    weight = lax.all_gather(out_weight, "wide", axis=0, tiled=True)
    q, k_pair, v_pair, sk, sv = spread(queries, span_keys, span_values, cache_keys, cache_values)
    part, lse = attend(chosen, q, cache_keys, cache_values, k_pair, v_pair, sk, sv)
    return finish(part, lse, weight)


def solution(mesh):
    return jax.shard_map(
        shards,
        mesh=mesh,
        in_specs=(
            P("wide", None),
            P("wide", None),
            P("wide", None),
            P(("wide", "narrow"), None),
            P(("wide", "narrow"), None),
            P(),
            P("wide", "narrow"),
        ),
        out_specs=P("wide", "narrow"),
        check_vma=False,
    )
```

```python
import math

import jax
import jax.numpy as jnp
from jax import lax
from jax.experimental import pallas as pl
from jax.experimental.pallas import tpu as pltpu
from jax.sharding import PartitionSpec as P

HD = 128
QB = 512
KB = 4096
NQB = 8
NW = 16
KVH = 8
HALF = 256
ROWS = 2 * QB
NY = 4
PIECE = HALF // NY
CHUNK = 256
FLOOR_SCORE = -1e30
SCALE2 = math.log2(math.e) / math.sqrt(HD)
MESH = pl.DeviceIdType.MESH
MIB = 2**20


def place():
    wide = lax.axis_index("wide")
    narrow = lax.axis_index("narrow")
    return wide, narrow, narrow // 2, narrow % 2


def remote(src, dst, send_sem, recv_sem, device):
    return pltpu.make_async_remote_copy(
        src_ref=src, dst_ref=dst, send_sem=send_sem, recv_sem=recv_sem, device_id=device, device_id_type=MESH
    )


def spread_kernel(
    queries, span_k, span_v, cache_k, cache_v,
    q_out, pk_out, pv_out, sk_out, sv_out,
    q_send, q_recv, ring_send, ring_recv, pass_send, pass_recv,
    kv_send, kv_recv, span_send, span_recv, local_sem, span_local,
):
    wide, narrow, y, core = place()
    buddy = y * 2 + 1 - core
    block, half = wide // 2, wide % 2
    barrier = pltpu.get_barrier_semaphore()

    def greet(step, carry):
        pl.semaphore_signal(
            barrier, inc=1, device_id=((wide + step) % NW, narrow), device_id_type=MESH
        )
        return carry

    lax.fori_loop(1, NW, greet, 0)
    ring = [(y + 1) % NY * 2 + core, (y + NY - 1) % NY * 2 + core]
    for neighbour in (buddy, *ring):
        pl.semaphore_signal(barrier, inc=1, device_id=(wide, neighbour), device_id_type=MESH)
    pl.semaphore_wait(barrier, NW + 2)

    def q_src(kv, head):
        column = pl.multiple_of(kv * 512 + core * 256 + head * HD, HD)
        return queries.at[pl.ds(pl.multiple_of(y * PIECE, PIECE), PIECE), pl.ds(column, HD)]

    def q_dst(source, head):
        return q_out.at[head, source, y]

    def batch(group, head, piece):
        return q_out.at[head, pl.ds(group * 4, 4), piece]

    def ring_copy(group, head, direction, piece):
        return remote(
            batch(group, head, piece), batch(group, head, piece),
            ring_send.at[group, head, direction], ring_recv.at[group, head, direction], (wide, ring[direction]),
        )

    def pass_copy(group, head, piece):
        return remote(
            batch(group, head, piece), batch(group, head, piece),
            pass_send.at[group, head], pass_recv.at[group, head], (wide, ring[head]),
        )

    def span_pair(kv, which):
        src = (span_k, span_v)[which].at[:, pl.ds(pl.multiple_of(kv * HD, HD), HD)]
        return src

    def span_dst(part, which):
        return (sk_out, sv_out)[which].at[pl.ds(pl.multiple_of(part * HALF, HALF), HALF), :]

    def q_copy(step, head):
        target = (wide + step) % NW
        return remote(
            q_src(target // 2, head), q_dst(wide, head),
            q_send.at[step, head], q_recv.at[wide, head], (target, narrow),
        )

    kv_copies = [
        remote(src, dst, kv_send.at[i], kv_recv.at[i], (wide, buddy))
        for i, (src, dst) in enumerate(((cache_k, pk_out), (cache_v, pv_out)))
    ]
    span_owner = y == block % 4

    def span_copy(kv, which):
        return remote(
            span_pair(kv, which), span_dst(half, which),
            span_send.at[kv, which], span_recv.at[half, which], (kv * 2 + block // 4, narrow),
        )

    def span_own(kv, which):
        return pltpu.make_async_copy(span_pair(kv, which), span_dst(half, which), span_local.at[which])

    self_span = span_owner & (half == block // 4)

    def start_q(step, carry):
        for head in range(2):
            q_copy(step, head).start()
        return carry

    lax.fori_loop(1, NW, start_q, 0)
    for head in range(2):
        pltpu.make_async_copy(q_src(wide // 2, head), q_dst(wide, head), local_sem.at[head]).start()

    def each_span(kv, carry, act):
        @pl.when(span_owner & (kv * 2 + block // 4 != wide))
        def _():
            for which in range(2):
                act(span_copy(kv, which))

        return carry

    lax.fori_loop(0, KVH, lambda kv, c: each_span(kv, c, lambda copy: copy.start()), 0)

    @pl.when(self_span)
    def _():
        for which in range(2):
            span_own(block, which).start()

    for copy in kv_copies:
        copy.start()

    for head in range(2):
        pltpu.make_async_copy(q_src(wide // 2, head), q_dst(wide, head), local_sem.at[head]).wait()
    behind = [(y + NY - 1) % NY, (y + 1) % NY]

    def gather_batch(step, carry):
        group = (wide // 4 + step) % 4

        def wait_source(i, carry):
            source = group * 4 + i

            @pl.when(source != wide)
            def _():
                for head in range(2):
                    remote(
                        q_src(0, head), q_dst(source, head),
                        q_send.at[0, head], q_recv.at[source, head], (source, narrow),
                    ).wait_recv()

            return carry

        lax.fori_loop(0, 4, wait_source, 0)
        for head in range(2):
            for direction in range(2):
                ring_copy(group, head, direction, y).start()
        return carry

    lax.fori_loop(0, 4, gather_batch, 0)

    def pass_batch(step, carry):
        group = (wide // 4 + step) % 4
        for head in range(2):
            ring_copy(group, head, head, behind[head]).wait_recv()
            pass_copy(group, head, behind[head]).start()
        return carry

    lax.fori_loop(0, 4, pass_batch, 0)

    def finish_batch(step, carry):
        group = (wide // 4 + step) % 4
        for head in range(2):
            ring_copy(group, head, 1 - head, behind[1 - head]).wait_recv()
            pass_copy(group, head, (y + 2) % NY).wait_recv()
            pass_copy(group, head, behind[head]).wait_send()
            for direction in range(2):
                ring_copy(group, head, direction, y).wait_send()
        return carry

    lax.fori_loop(0, 4, finish_batch, 0)

    def wait_q(step, carry):
        for head in range(2):
            q_copy(step, head).wait_send()
        return carry

    lax.fori_loop(1, NW, wait_q, 0)
    lax.fori_loop(0, KVH, lambda kv, c: each_span(kv, c, lambda copy: copy.wait_send()), 0)

    @pl.when(self_span)
    def _():
        for which in range(2):
            span_own(block, which).wait()

    held = wide % 2 * 4 + y
    for part in range(2):
        @pl.when(held * 2 + part != wide)
        def _():
            for which in range(2):
                remote(
                    span_pair(0, which), span_dst(part, which),
                    span_send.at[0, which], span_recv.at[part, which], (wide, buddy),
                ).wait_recv()

    for copy in kv_copies:
        copy.wait()


def spread(queries, span_k, span_v, cache_k, cache_v):
    anywhere = pl.BlockSpec(memory_space=pl.ANY)
    shape = lambda *dims: jax.ShapeDtypeStruct(dims, jnp.bfloat16)
    dma = pltpu.SemaphoreType.DMA
    return pl.pallas_call(
        spread_kernel,
        out_shape=[shape(2, NW, NY, PIECE, HD), shape(KB, HD), shape(KB, HD), shape(QB, HD), shape(QB, HD)],
        in_specs=[anywhere] * 5,
        out_specs=[anywhere] * 5,
        scratch_shapes=[
            dma((NW, 2)), dma((NW, 2)), dma((4, 2, 2)), dma((4, 2, 2)), dma((4, 2)), dma((4, 2)),
            dma((2,)), dma((2,)), dma((KVH, 2)), dma((2, 2)), dma((2,)), dma((2,)),
        ],
        compiler_params=pltpu.CompilerParams(
            collective_id=0, has_side_effects=True, vmem_limit_bytes=56 * MIB
        ),
    )(queries, span_k, span_v, cache_k, cache_v)


def attend_kernel(
    chosen, q, k_own, v_own, k_pair, v_pair, sk, sv, out, lse,
    q_in, k_both, v_wide, sk_in, s_wide, out_in, lse_in, acc, peak, sems, out_sem,
):
    wide, narrow, y, core = place()
    held = wide % 2 * 4 + y
    first = wide % 2 * 8 + y * 2
    moves = [
        (q, q_in),
        (sk, sk_in),
        (sv, s_wide.at[:, :HD]),
        (k_own, k_both.at[0]),
        (v_own, v_wide.at[0, :, :HD]),
        (k_pair, k_both.at[1]),
        (v_pair, v_wide.at[1, :, :HD]),
    ]
    loads = [pltpu.make_async_copy(src, dst, sems.at[i]) for i, (src, dst) in enumerate(moves)]
    for copy in loads:
        copy.start()
    s_wide[:, HD:] = jnp.ones((QB, HD), jnp.bfloat16)
    for i in range(2):
        v_wide[i, :, HD:] = jnp.ones((KB, HD), jnp.bfloat16)

    def fold(state, queries, keys, values, mask):
        top, total = state
        scores = lax.dot_general(queries, keys, (((1,), (1,)), ((), ())), preferred_element_type=jnp.float32)
        if mask is not None:
            scores = jnp.where(mask, scores, FLOOR_SCORE)
        new_top = jnp.maximum(top, jnp.max(scores, axis=1, keepdims=True))
        decay = jnp.exp2((top - new_top) * SCALE2)
        weights = jnp.exp2((scores - new_top) * SCALE2).astype(jnp.bfloat16)
        total = total * decay + jnp.dot(weights, values, preferred_element_type=jnp.float32)
        return new_top, total

    def block_queries(b):
        return q_in[:, pl.ds(b * 2, 2)].reshape(ROWS, HD)

    def load():
        return jnp.max(peak[...], axis=1, keepdims=True), acc[...]

    def save(state):
        peak[...] = jnp.broadcast_to(state[0], (ROWS, HD))
        acc[...] = state[1]

    for copy in loads[:3]:
        copy.wait()
    row = lax.broadcasted_iota(jnp.int32, (ROWS, QB), 0) % QB
    mask = row >= lax.broadcasted_iota(jnp.int32, (ROWS, QB), 1)
    fresh = jnp.full((ROWS, 1), FLOOR_SCORE, jnp.float32), jnp.zeros((ROWS, 2 * HD), jnp.float32)
    save(fold(fresh, block_queries(held), sk_in[...], s_wide[...], mask))
    for copy in loads[3:]:
        copy.wait()

    def send_out(b):
        return (
            pltpu.make_async_copy(out_in.at[b], out.at[b], out_sem.at[b, 0]),
            pltpu.make_async_copy(lse_in.at[b], lse.at[b], out_sem.at[b, 1]),
        )

    def one_block(step, carry):
        b = (held + step) % NQB
        hits = []
        for i in range(2):
            c = first + jnp.where(core == 0, i, 1 - i)
            hits.append((chosen[b, 0] == c) | (chosen[b, 1] == c) | (chosen[b, 2] == c))
        used = hits[0] | hits[1] | (step == 0)

        @pl.when(used & (step != 0))
        def _():
            acc[...] = jnp.zeros((ROWS, 2 * HD), jnp.float32)
            peak[...] = jnp.full((ROWS, HD), FLOOR_SCORE, jnp.float32)

        def cached(i, carry):
            @pl.when(jnp.where(i == 0, hits[0], hits[1]))
            def _():
                queries = block_queries(b)
                state = load()
                for start in range(0, KB, CHUNK):
                    state = fold(
                        state, queries, k_both[i, start:start + CHUNK, :], v_wide[i, start:start + CHUNK, :], None
                    )
                save(state)

            return carry

        lax.fori_loop(0, 2, cached, 0)

        @pl.when(used)
        def _():
            total = acc[:, HD:]
            out_in[b] = (acc[:, :HD] / total).astype(jnp.bfloat16)
            logs = peak[...] * SCALE2 + jnp.log2(total)
            eye = lax.broadcasted_iota(jnp.int32, (HD, HD), 0) == lax.broadcasted_iota(jnp.int32, (HD, HD), 1)
            for g in range(ROWS // HD):
                lse_in[b, g:g + 1, :] = jnp.sum(
                    jnp.where(eye, logs[g * HD:(g + 1) * HD], 0.0), axis=0, keepdims=True
                )

        @pl.when(jnp.logical_not(used))
        def _():
            out_in[b] = jnp.zeros((ROWS, HD), jnp.bfloat16)
            lse_in[b] = jnp.full((8, HD), FLOOR_SCORE, jnp.float32)

        for copy in send_out(b):
            copy.start()
        return carry

    lax.fori_loop(0, NQB, one_block, 0)
    for b in range(NQB):
        for copy in send_out(b):
            copy.wait()


def attend(chosen, q, k_own, v_own, k_pair, v_pair, sk, sv):
    anywhere = pl.BlockSpec(memory_space=pl.ANY)
    dma = pltpu.SemaphoreType.DMA
    return pl.pallas_call(
        attend_kernel,
        out_shape=[
            jax.ShapeDtypeStruct((NQB, ROWS, HD), jnp.bfloat16),
            jax.ShapeDtypeStruct((NQB, 8, HD), jnp.float32),
        ],
        in_specs=[pl.BlockSpec(memory_space=pltpu.SMEM)] + [anywhere] * 7,
        out_specs=[anywhere] * 2,
        scratch_shapes=[
            pltpu.VMEM((2, NW, NY, PIECE, HD), jnp.bfloat16),
            pltpu.VMEM((2, KB, HD), jnp.bfloat16),
            pltpu.VMEM((2, KB, 2 * HD), jnp.bfloat16),
            pltpu.VMEM((QB, HD), jnp.bfloat16),
            pltpu.VMEM((QB, 2 * HD), jnp.bfloat16),
            pltpu.VMEM((NQB, ROWS, HD), jnp.bfloat16),
            pltpu.VMEM((NQB, 8, HD), jnp.float32),
            pltpu.VMEM((ROWS, 2 * HD), jnp.float32),
            pltpu.VMEM((ROWS, HD), jnp.float32),
            dma((7,)), dma((NQB, 2)),
        ],
        compiler_params=pltpu.CompilerParams(vmem_limit_bytes=56 * MIB),
        cost_estimate=pl.CostEstimate(flops=14 * 10**9, bytes_accessed=10 * MIB, transcendentals=25 * 10**6),
    )(chosen, q, k_own, v_own, k_pair, v_pair, sk, sv)


def finish_kernel(
    part, lse, weight, result,
    p_in, l_in, w_in, relay, rows_out, rows_in,
    p_send, p_recv, l_send, l_recv, relay_send, relay_recv, pass_send,
    a_send, a_recv, y_send, f_send, f_recv, local_sem,
):
    wide, narrow, y, core = place()
    buddy = y * 2 + 1 - core
    kv, side = wide // 2, wide % 2
    held = side * 4 + y
    mine = wide // 2
    from_y = (y + NY - mine % 4) % NY
    ahead, behind = (y + 1) % NY, (y + NY - 1) % NY
    own_target = mine == held
    barrier = pltpu.get_barrier_semaphore()

    def combiner(b):
        return kv * 2 + b // 4, b % 4 * 2 + core

    def source(s):
        return s * 2 + mine // 4, mine % 4 * 2 + core

    fetch = pltpu.make_async_copy(weight, w_in, local_sem.at[0])
    keep = [
        pltpu.make_async_copy(part.at[held], p_in.at[held], local_sem.at[1]),
        pltpu.make_async_copy(lse.at[held], l_in.at[held], local_sem.at[2]),
    ]
    for copy in (*keep, fetch):
        copy.start()

    def greet(step, carry):
        pl.semaphore_signal(barrier, inc=1, device_id=combiner((held + step) % 8), device_id_type=MESH)
        return carry

    lax.fori_loop(1, 8, greet, 0)

    def greet_source(s, carry):
        @pl.when((from_y != 2) & jnp.logical_not(own_target & (s == kv)))
        def _():
            pl.semaphore_signal(barrier, inc=1, device_id=source(s), device_id_type=MESH)

        return carry

    lax.fori_loop(0, 8, greet_source, 0)
    pl.semaphore_signal(barrier, inc=1, device_id=(wide, buddy), device_id_type=MESH)
    pl.semaphore_wait(barrier, 14 - own_target.astype(jnp.int32))

    def head_rows(h):
        return pl.ds(h * QB, QB)

    def relay_copy(across):
        b = (side + across) % 2 * 4 + (y + 2) % NY
        return remote(
            part.at[b, head_rows(1)], relay.at[across],
            relay_send.at[across], relay_recv.at[across], (wide, behind * 2 + core),
        )

    def pass_copy(across):
        origin = side * 4 + ahead
        return remote(
            relay.at[across], p_in.at[origin, head_rows(1)],
            pass_send.at[across], p_recv.at[origin, 1], (kv * 2 + (side + across) % 2, behind * 2 + core),
        )

    def part_copy(step, h):
        b = (held + step) % 8
        return remote(
            part.at[b, head_rows(h)], p_in.at[held, head_rows(h)],
            p_send.at[step, h], p_recv.at[held, h], combiner(b),
        )

    def lse_copy(step):
        b = (held + step) % 8
        return remote(lse.at[b], l_in.at[held], l_send.at[step], l_recv.at[held], combiner(b))

    def straight(step):
        return (held + step) % 4 != (y + 2) % 4

    for across in range(2):
        relay_copy(across).start()

    def start_first(step, carry):
        lse_copy(step).start()
        part_copy(step, 0).start()
        return carry

    lax.fori_loop(1, 8, start_first, 0)

    def start_second(step, carry):
        @pl.when(straight(step))
        def _():
            part_copy(step, 1).start()

        return carry

    lax.fori_loop(1, 8, start_second, 0)
    for across in range(2):
        relay_copy(across).wait_recv()
        pass_copy(across).start()
    for copy in keep:
        copy.wait()

    def wait_lse(step, carry):
        s = (held + step) % 8
        remote(lse.at[s], l_in.at[s], l_send.at[step], l_recv.at[s], combiner(s)).wait_recv()
        return carry

    lax.fori_loop(1, 8, wait_lse, 0)
    logs = l_in[...]
    shares = jnp.exp2(logs - jnp.max(logs, axis=0, keepdims=True))
    shares = shares / jnp.sum(shares, axis=0, keepdims=True)
    turned = jnp.transpose(jnp.concatenate([shares.reshape(64, HD)] * 2, axis=0))

    def row_copy(i, delta, h):
        head = kv * 4 + core * 2 + h
        return remote(
            rows_out.at[h, pl.ds(i * HALF, HALF)], rows_in.at[head],
            a_send.at[i, delta, h], a_recv.at[head], (held * 2 + i, (y + delta) % NY * 2 + core),
        )

    def own_copy(i, h):
        return pltpu.make_async_copy(
            rows_out.at[h, pl.ds(i * HALF, HALF)], rows_in.at[kv * 4 + core * 2 + h], local_sem.at[3 + h]
        )

    def each_target(h, act, act_own):
        for i in range(2):
            for delta in (0, 1, 3):
                if delta:
                    act(row_copy(i, delta, h))
                else:
                    here = own_target & (side == i)

                    @pl.when(here)
                    def _():
                        act_own(own_copy(i, h))

                    @pl.when(jnp.logical_not(here))
                    def _():
                        act(row_copy(i, 0, h))

    for h in range(2):
        def wait_part(step, carry):
            s = (held + step) % 8
            remote(
                part.at[s, head_rows(h)], p_in.at[s, head_rows(h)], p_send.at[step, h], p_recv.at[s, h], combiner(s)
            ).wait_recv()
            return carry

        lax.fori_loop(1, 8, wait_part, 0)
        for g in range(4):
            total = jnp.zeros((HD, HD), jnp.float32)
            for s in range(8):
                column = s * 8 + h * 4 + g
                rows = p_in[s, h * QB + g * HD:h * QB + (g + 1) * HD, :].astype(jnp.float32)
                total = total + rows * turned[:, column:column + 1]
            rows_out[h, g * HD:(g + 1) * HD, :] = total.astype(jnp.bfloat16)
        each_target(h, lambda copy: copy.start(), lambda copy: copy.start())

    fetch.wait()
    duty = ((from_y == 1) & (side == 0)) | ((from_y == 3) & (side == 1))
    onward = jnp.where(side == 0, ahead, behind) * 2 + core

    def product(head):
        return jnp.dot(
            rows_in[head], w_in[pl.ds(pl.multiple_of(head * HD, HD), HD), :], preferred_element_type=jnp.float32
        )

    def forward(s, h):
        head = s * 4 + core * 2 + h
        return remote(rows_in.at[head], rows_in.at[head], f_send.at[s, h], f_recv.at[head], (wide, buddy))

    def along(s, h):
        head = s * 4 + core * 2 + h
        return remote(rows_in.at[head], rows_in.at[head], y_send.at[s, h], a_recv.at[head], (wide, onward))

    total = jnp.zeros((HALF, 512), jnp.float32)
    for h in range(2):
        def arrive(s, total):
            head = s * 4 + core * 2 + h
            local = own_target & (s == kv)

            @pl.when(local)
            def _():
                own_copy(0, h).wait()

            @pl.when(jnp.logical_not(local))
            def _():
                remote(
                    rows_in.at[head], rows_in.at[head], f_send.at[s, h], a_recv.at[head], (wide, buddy)
                ).wait_recv()

            forward(s, h).start()

            @pl.when(duty)
            def _():
                along(s, h).start()

            return total + product(head)

        total = lax.fori_loop(0, 8, arrive, total)

        def arrive_pair(s, total):
            head = s * 4 + (1 - core) * 2 + h
            remote(rows_in.at[head], rows_in.at[head], f_send.at[s, h], f_recv.at[head], (wide, buddy)).wait_recv()
            return total + product(head)

        total = lax.fori_loop(0, 8, arrive_pair, total)
    result[...] = total.astype(jnp.bfloat16)

    def drain(step, carry):
        lse_copy(step).wait_send()
        part_copy(step, 0).wait_send()

        @pl.when(straight(step))
        def _():
            part_copy(step, 1).wait_send()

        return carry

    lax.fori_loop(1, 8, drain, 0)
    for across in range(2):
        relay_copy(across).wait_send()
        pass_copy(across).wait_send()
    for h in range(2):
        each_target(h, lambda copy: copy.wait_send(), lambda copy: None)

        def drain_rows(s, carry):
            forward(s, h).wait_send()

            @pl.when(duty)
            def _():
                along(s, h).wait_send()

            return carry

        lax.fori_loop(0, 8, drain_rows, 0)


def finish(part, lse, weight):
    anywhere = pl.BlockSpec(memory_space=pl.ANY)
    dma = pltpu.SemaphoreType.DMA
    return pl.pallas_call(
        finish_kernel,
        out_shape=jax.ShapeDtypeStruct((HALF, 512), jnp.bfloat16),
        in_specs=[anywhere] * 3,
        out_specs=pl.BlockSpec(memory_space=pltpu.VMEM),
        scratch_shapes=[
            pltpu.VMEM((8, ROWS, HD), jnp.bfloat16),
            pltpu.VMEM((8, 8, HD), jnp.float32),
            pltpu.VMEM((4096, 512), jnp.bfloat16),
            pltpu.VMEM((2, QB, HD), jnp.bfloat16),
            pltpu.VMEM((2, QB, HD), jnp.bfloat16),
            pltpu.VMEM((32, HALF, HD), jnp.bfloat16),
            dma((8, 2)), dma((8, 2)), dma((8,)), dma((8,)), dma((2,)), dma((2,)), dma((2,)),
            dma((2, 4, 2)), dma((32,)), dma((8, 2)), dma((8, 2)), dma((32,)), dma((5,)),
        ],
        compiler_params=pltpu.CompilerParams(
            collective_id=1, has_side_effects=True, vmem_limit_bytes=56 * MIB
        ),
    )(part, lse, weight)


def shards(queries, span_keys, span_values, cache_keys, cache_values, chosen, out_weight):
    weight = lax.all_gather(out_weight, "wide", axis=0, tiled=True)
    q, k_pair, v_pair, sk, sv = spread(queries, span_keys, span_values, cache_keys, cache_values)
    part, lse = attend(chosen, q, cache_keys, cache_values, k_pair, v_pair, sk, sv)
    return finish(part, lse, weight)


def solution(mesh):
    return jax.shard_map(
        shards,
        mesh=mesh,
        in_specs=(
            P("wide", None),
            P("wide", None),
            P("wide", None),
            P(("wide", "narrow"), None),
            P(("wide", "narrow"), None),
            P(),
            P("wide", "narrow"),
        ),
        out_specs=P("wide", "narrow"),
        check_vma=False,
    )
```

```python
import math

import jax
import jax.numpy as jnp
from jax import lax
from jax.experimental import pallas as pl
from jax.experimental.pallas import tpu as pltpu
from jax.sharding import PartitionSpec as P

HD = 128
QB = 512
KB = 4096
NQB = 8
NW = 16
KVH = 8
HALF = 256
ROWS = 2 * QB
NY = 4
PIECE = HALF // NY
CHUNK = 256
FLOOR_SCORE = -1e30
SCALE2 = math.log2(math.e) / math.sqrt(HD)
MESH = pl.DeviceIdType.MESH
MIB = 2**20


def place():
    wide = lax.axis_index("wide")
    narrow = lax.axis_index("narrow")
    return wide, narrow, narrow // 2, narrow % 2


def remote(src, dst, send_sem, recv_sem, device):
    return pltpu.make_async_remote_copy(
        src_ref=src, dst_ref=dst, send_sem=send_sem, recv_sem=recv_sem, device_id=device, device_id_type=MESH
    )


def spread_kernel(
    queries, span_k, span_v, cache_k, cache_v,
    q_out, pk_out, pv_out, sk_out, sv_out,
    q_send, q_recv, ring_send, ring_recv, pass_send, pass_recv,
    kv_send, kv_recv, span_send, span_recv, local_sem, span_local,
):
    wide, narrow, y, core = place()
    buddy = y * 2 + 1 - core
    block, half = wide // 2, wide % 2
    barrier = pltpu.get_barrier_semaphore()

    def greet(step, carry):
        pl.semaphore_signal(
            barrier, inc=1, device_id=((wide + step) % NW, narrow), device_id_type=MESH
        )
        return carry

    lax.fori_loop(1, NW, greet, 0)
    ring = [(y + 1) % NY * 2 + core, (y + NY - 1) % NY * 2 + core]
    for neighbour in (buddy, *ring):
        pl.semaphore_signal(barrier, inc=1, device_id=(wide, neighbour), device_id_type=MESH)
    pl.semaphore_wait(barrier, NW + 2)

    def q_src(kv, head):
        column = pl.multiple_of(kv * 512 + core * 256 + head * HD, HD)
        return queries.at[pl.ds(pl.multiple_of(y * PIECE, PIECE), PIECE), pl.ds(column, HD)]

    def q_dst(source, head):
        return q_out.at[head, source, y]

    def batch(group, head, piece):
        return q_out.at[head, pl.ds(group * 4, 4), piece]

    def ring_copy(group, head, direction, piece):
        return remote(
            batch(group, head, piece), batch(group, head, piece),
            ring_send.at[group, head, direction], ring_recv.at[group, head, direction], (wide, ring[direction]),
        )

    def pass_copy(group, head, piece):
        return remote(
            batch(group, head, piece), batch(group, head, piece),
            pass_send.at[group, head], pass_recv.at[group, head], (wide, ring[head]),
        )

    def span_pair(kv, which):
        src = (span_k, span_v)[which].at[:, pl.ds(pl.multiple_of(kv * HD, HD), HD)]
        return src

    def span_dst(part, which):
        return (sk_out, sv_out)[which].at[pl.ds(pl.multiple_of(part * HALF, HALF), HALF), :]

    def q_copy(step, head):
        target = (wide + step) % NW
        return remote(
            q_src(target // 2, head), q_dst(wide, head),
            q_send.at[step, head], q_recv.at[wide, head], (target, narrow),
        )

    kv_copies = [
        remote(src, dst, kv_send.at[i], kv_recv.at[i], (wide, buddy))
        for i, (src, dst) in enumerate(((cache_k, pk_out), (cache_v, pv_out)))
    ]
    span_owner = y == block % 4

    def span_copy(kv, which):
        return remote(
            span_pair(kv, which), span_dst(half, which),
            span_send.at[kv, which], span_recv.at[half, which], (kv * 2 + block // 4, narrow),
        )

    def span_own(kv, which):
        return pltpu.make_async_copy(span_pair(kv, which), span_dst(half, which), span_local.at[which])

    self_span = span_owner & (half == block // 4)

    def start_q(step, carry):
        for head in range(2):
            q_copy(step, head).start()
        return carry

    lax.fori_loop(1, NW, start_q, 0)
    for head in range(2):
        pltpu.make_async_copy(q_src(wide // 2, head), q_dst(wide, head), local_sem.at[head]).start()

    def each_span(kv, carry, act):
        @pl.when(span_owner & (kv * 2 + block // 4 != wide))
        def _():
            for which in range(2):
                act(span_copy(kv, which))

        return carry

    lax.fori_loop(0, KVH, lambda kv, c: each_span(kv, c, lambda copy: copy.start()), 0)

    @pl.when(self_span)
    def _():
        for which in range(2):
            span_own(block, which).start()

    for copy in kv_copies:
        copy.start()

    for head in range(2):
        pltpu.make_async_copy(q_src(wide // 2, head), q_dst(wide, head), local_sem.at[head]).wait()
    behind = [(y + NY - 1) % NY, (y + 1) % NY]

    def gather_batch(step, carry):
        group = (wide // 4 + step) % 4

        def wait_source(i, carry):
            source = group * 4 + i

            @pl.when(source != wide)
            def _():
                for head in range(2):
                    remote(
                        q_src(0, head), q_dst(source, head),
                        q_send.at[0, head], q_recv.at[source, head], (source, narrow),
                    ).wait_recv()

            return carry

        lax.fori_loop(0, 4, wait_source, 0)
        for head in range(2):
            for direction in range(2):
                ring_copy(group, head, direction, y).start()
        return carry

    lax.fori_loop(0, 4, gather_batch, 0)

    def pass_batch(step, carry):
        group = (wide // 4 + step) % 4
        for head in range(2):
            ring_copy(group, head, head, behind[head]).wait_recv()
            pass_copy(group, head, behind[head]).start()
        return carry

    lax.fori_loop(0, 4, pass_batch, 0)

    def finish_batch(step, carry):
        group = (wide // 4 + step) % 4
        for head in range(2):
            ring_copy(group, head, 1 - head, behind[1 - head]).wait_recv()
            pass_copy(group, head, (y + 2) % NY).wait_recv()
            pass_copy(group, head, behind[head]).wait_send()
            for direction in range(2):
                ring_copy(group, head, direction, y).wait_send()
        return carry

    lax.fori_loop(0, 4, finish_batch, 0)

    def wait_q(step, carry):
        for head in range(2):
            q_copy(step, head).wait_send()
        return carry

    lax.fori_loop(1, NW, wait_q, 0)
    lax.fori_loop(0, KVH, lambda kv, c: each_span(kv, c, lambda copy: copy.wait_send()), 0)

    @pl.when(self_span)
    def _():
        for which in range(2):
            span_own(block, which).wait()

    held = wide % 2 * 4 + y
    for part in range(2):
        @pl.when(held * 2 + part != wide)
        def _():
            for which in range(2):
                remote(
                    span_pair(0, which), span_dst(part, which),
                    span_send.at[0, which], span_recv.at[part, which], (wide, buddy),
                ).wait_recv()

    for copy in kv_copies:
        copy.wait()


def spread(queries, span_k, span_v, cache_k, cache_v):
    anywhere = pl.BlockSpec(memory_space=pl.ANY)
    shape = lambda *dims: jax.ShapeDtypeStruct(dims, jnp.bfloat16)
    dma = pltpu.SemaphoreType.DMA
    return pl.pallas_call(
        spread_kernel,
        out_shape=[shape(2, NW, NY, PIECE, HD), shape(KB, HD), shape(KB, HD), shape(QB, HD), shape(QB, HD)],
        in_specs=[anywhere] * 5,
        out_specs=[anywhere] * 5,
        scratch_shapes=[
            dma((NW, 2)), dma((NW, 2)), dma((4, 2, 2)), dma((4, 2, 2)), dma((4, 2)), dma((4, 2)),
            dma((2,)), dma((2,)), dma((KVH, 2)), dma((2, 2)), dma((2,)), dma((2,)),
        ],
        compiler_params=pltpu.CompilerParams(
            collective_id=0, has_side_effects=True, vmem_limit_bytes=56 * MIB
        ),
    )(queries, span_k, span_v, cache_k, cache_v)


def attend_kernel(
    chosen, q, k_own, v_own, k_pair, v_pair, sk, sv, out, lse,
    q_in, k_both, v_wide, sk_in, s_wide, out_in, lse_in, acc, peak, sems, out_sem,
):
    wide, narrow, y, core = place()
    held = wide % 2 * 4 + y
    first = wide % 2 * 8 + y * 2
    moves = [
        (q, q_in),
        (sk, sk_in),
        (sv, s_wide.at[:, :HD]),
        (k_own, k_both.at[0]),
        (v_own, v_wide.at[0, :, :HD]),
        (k_pair, k_both.at[1]),
        (v_pair, v_wide.at[1, :, :HD]),
    ]
    loads = [pltpu.make_async_copy(src, dst, sems.at[i]) for i, (src, dst) in enumerate(moves)]
    for copy in loads:
        copy.start()
    s_wide[:, HD:] = jnp.ones((QB, HD), jnp.bfloat16)
    lse_in[...] = jnp.full((NY, 2, 16, HD), FLOOR_SCORE, jnp.float32)
    for i in range(2):
        v_wide[i, :, HD:] = jnp.ones((KB, HD), jnp.bfloat16)

    def fold(state, queries, keys, values, mask):
        top, total = state
        scores = lax.dot_general(queries, keys, (((1,), (1,)), ((), ())), preferred_element_type=jnp.float32)
        if mask is not None:
            scores = jnp.where(mask, scores, FLOOR_SCORE)
        new_top = jnp.maximum(top, jnp.max(scores, axis=1, keepdims=True))
        decay = jnp.exp2((top - new_top) * SCALE2)
        weights = jnp.exp2((scores - new_top) * SCALE2).astype(jnp.bfloat16)
        total = total * decay + jnp.dot(weights, values, preferred_element_type=jnp.float32)
        return new_top, total

    def block_queries(b):
        return q_in[:, pl.ds(b * 2, 2)].reshape(ROWS, HD)

    def load():
        return jnp.max(peak[...], axis=1, keepdims=True), acc[...]

    def save(state):
        peak[...] = jnp.broadcast_to(state[0], (ROWS, HD))
        acc[...] = state[1]

    for copy in loads[:3]:
        copy.wait()
    row = lax.broadcasted_iota(jnp.int32, (ROWS, QB), 0) % QB
    mask = row >= lax.broadcasted_iota(jnp.int32, (ROWS, QB), 1)
    fresh = jnp.full((ROWS, 1), FLOOR_SCORE, jnp.float32), jnp.zeros((ROWS, 2 * HD), jnp.float32)
    save(fold(fresh, block_queries(held), sk_in[...], s_wide[...], mask))
    for copy in loads[3:]:
        copy.wait()

    def send_out(b):
        return pltpu.make_async_copy(
            out_in.at[:, pl.ds(b * 2, 2)], out.at[:, pl.ds(b * 2, 2)], out_sem.at[b]
        )

    def one_block(step, carry):
        b = (held + step) % NQB
        hits = []
        for i in range(2):
            c = first + jnp.where(core == 0, i, 1 - i)
            hits.append((chosen[b, 0] == c) | (chosen[b, 1] == c) | (chosen[b, 2] == c))
        used = hits[0] | hits[1] | (step == 0)

        @pl.when(used & (step != 0))
        def _():
            acc[...] = jnp.zeros((ROWS, 2 * HD), jnp.float32)
            peak[...] = jnp.full((ROWS, HD), FLOOR_SCORE, jnp.float32)

        def cached(i, carry):
            @pl.when(jnp.where(i == 0, hits[0], hits[1]))
            def _():
                queries = block_queries(b)
                state = load()
                for start in range(0, KB, CHUNK):
                    state = fold(
                        state, queries, k_both[i, start:start + CHUNK, :], v_wide[i, start:start + CHUNK, :], None
                    )
                save(state)

            return carry

        lax.fori_loop(0, 2, cached, 0)

        @pl.when(used)
        def _():
            total = acc[:, HD:]
            out_in[:, pl.ds(b * 2, 2)] = (
                (acc[:, :HD] / total).astype(jnp.bfloat16).reshape(2, 2, NY, PIECE, HD)
            )
            logs = peak[...] * SCALE2 + jnp.log2(total)
            eye = lax.broadcasted_iota(jnp.int32, (PIECE, HD), 0) == lax.broadcasted_iota(
                jnp.int32, (PIECE, HD), 1
            )
            for piece in range(NY):
                for part in range(4):
                    start = part * HALF + piece * PIECE
                    lse_in[piece, b // 4, pl.ds(b % 4 * 4 + part, 1), :] = jnp.sum(
                        jnp.where(eye, logs[start:start + PIECE], 0.0), axis=0, keepdims=True
                    )

        @pl.when(jnp.logical_not(used))
        def _():
            out_in[:, pl.ds(b * 2, 2)] = jnp.zeros((2, 2, NY, PIECE, HD), jnp.bfloat16)

        send_out(b).start()
        return carry

    lax.fori_loop(0, NQB, one_block, 0)
    lse_copy = pltpu.make_async_copy(lse_in, lse, sems.at[7])
    lse_copy.start()
    for b in range(NQB):
        send_out(b).wait()
    lse_copy.wait()


def attend(chosen, q, k_own, v_own, k_pair, v_pair, sk, sv):
    anywhere = pl.BlockSpec(memory_space=pl.ANY)
    dma = pltpu.SemaphoreType.DMA
    return pl.pallas_call(
        attend_kernel,
        out_shape=[
            jax.ShapeDtypeStruct((2, NW, NY, PIECE, HD), jnp.bfloat16),
            jax.ShapeDtypeStruct((NY, 2, 16, HD), jnp.float32),
        ],
        in_specs=[pl.BlockSpec(memory_space=pltpu.SMEM)] + [anywhere] * 7,
        out_specs=[anywhere] * 2,
        scratch_shapes=[
            pltpu.VMEM((2, NW, NY, PIECE, HD), jnp.bfloat16),
            pltpu.VMEM((2, KB, HD), jnp.bfloat16),
            pltpu.VMEM((2, KB, 2 * HD), jnp.bfloat16),
            pltpu.VMEM((QB, HD), jnp.bfloat16),
            pltpu.VMEM((QB, 2 * HD), jnp.bfloat16),
            pltpu.VMEM((2, NW, NY, PIECE, HD), jnp.bfloat16),
            pltpu.VMEM((NY, 2, 16, HD), jnp.float32),
            pltpu.VMEM((ROWS, 2 * HD), jnp.float32),
            pltpu.VMEM((ROWS, HD), jnp.float32),
            dma((8,)), dma((NQB,)),
        ],
        compiler_params=pltpu.CompilerParams(vmem_limit_bytes=56 * MIB),
        cost_estimate=pl.CostEstimate(flops=14 * 10**9, bytes_accessed=10 * MIB, transcendentals=25 * 10**6),
    )(chosen, q, k_own, v_own, k_pair, v_pair, sk, sv)


def finish_kernel(
    part, lse, weight, result,
    p_in, l_in, w_in, relay, rows_out, rows_in,
    p_send, p_recv, l_send, l_recv, relay_send, relay_recv, pass_send,
    a_send, a_recv, ring_send, ring_recv, on_send, on_recv, f_send, f_recv, local_sem,
):
    wide, narrow, y, core = place()
    buddy = y * 2 + 1 - core
    kv, side = wide // 2, wide % 2
    held = side * 4 + y
    ring = [(y + 1) % NY, (y + NY - 1) % NY]
    behind = ring[::-1]
    own_target = wide // 8 == side
    barrier = pltpu.get_barrier_semaphore()

    def combiner(b):
        return kv * 2 + b // 4, b % 4 * 2 + core

    fetches = [pltpu.make_async_copy(weight.at[:, i], w_in.at[i], local_sem.at[i]) for i in range(4)]
    keep = [
        pltpu.make_async_copy(part.at[h, pl.ds(side * 8, 8), y], p_in.at[held, h], local_sem.at[4 + h])
        for h in range(2)
    ]
    keep.append(pltpu.make_async_copy(lse.at[y, side], l_in.at[held], local_sem.at[6]))
    for copy in (*keep, *fetches):
        copy.start()

    def greet(step, carry):
        pl.semaphore_signal(barrier, inc=1, device_id=combiner((held + step) % 8), device_id_type=MESH)
        return carry

    lax.fori_loop(1, 8, greet, 0)

    def greet_source(s, carry):
        @pl.when(jnp.logical_not(own_target & (s == kv)))
        def _():
            pl.semaphore_signal(barrier, inc=1, device_id=(s * 2 + wide // 8, narrow), device_id_type=MESH)

        return carry

    lax.fori_loop(0, 8, greet_source, 0)
    pl.semaphore_signal(barrier, inc=1, device_id=(wide, buddy), device_id_type=MESH)
    pl.semaphore_wait(barrier, 16 - own_target.astype(jnp.int32))

    def share(b, h):
        return part.at[h, pl.ds(b // 4 * 8, 8), b % 4]

    def relay_copy(across):
        b = (side + across) % 2 * 4 + (y + 2) % NY
        return remote(
            share(b, 1), relay.at[across],
            relay_send.at[across], relay_recv.at[across], (wide, ring[1] * 2 + core),
        )

    def pass_copy(across):
        origin = side * 4 + ring[0]
        return remote(
            relay.at[across], p_in.at[origin, 1],
            pass_send.at[across], p_recv.at[origin, 1], (kv * 2 + (side + across) % 2, ring[1] * 2 + core),
        )

    def part_copy(step, h):
        b = (held + step) % 8
        return remote(share(b, h), p_in.at[held, h], p_send.at[step, h], p_recv.at[held, h], combiner(b))

    def lse_copy(step):
        b = (held + step) % 8
        return remote(lse.at[b % 4, b // 4], l_in.at[held], l_send.at[step], l_recv.at[held], combiner(b))

    def straight(step):
        return (held + step) % 4 != (y + 2) % 4

    for across in range(2):
        relay_copy(across).start()

    def start_first(step, carry):
        lse_copy(step).start()
        part_copy(step, 0).start()
        return carry

    lax.fori_loop(1, 8, start_first, 0)

    def start_second(step, carry):
        @pl.when(straight(step))
        def _():
            part_copy(step, 1).start()

        return carry

    lax.fori_loop(1, 8, start_second, 0)
    for across in range(2):
        relay_copy(across).wait_recv()
        pass_copy(across).start()
    for copy in keep:
        copy.wait()

    def wait_lse(step, carry):
        s = (held + step) % 8
        remote(lse.at[0, 0], l_in.at[s], l_send.at[step], l_recv.at[s], combiner(s)).wait_recv()
        return carry

    lax.fori_loop(1, 8, wait_lse, 0)
    logs = l_in[...]
    shares = jnp.exp2(logs - jnp.max(logs, axis=0, keepdims=True))
    shares = shares / jnp.sum(shares, axis=0, keepdims=True)
    turned = jnp.transpose(shares.reshape(HD, HD))

    def row_copy(i, h):
        return remote(
            rows_out.at[h, i], rows_in.at[core, h, y, kv], a_send.at[i, h], a_recv.at[kv, h], (side * 8 + i, narrow)
        )

    def own_copy(h):
        return pltpu.make_async_copy(rows_out.at[h, wide % 8], rows_in.at[core, h, y, kv], local_sem.at[7 + h])

    def local(i):
        return own_target & (i == wide % 8)

    for h in range(2):
        def wait_part(step, carry):
            s = (held + step) % 8
            remote(share(s, h), p_in.at[s, h], p_send.at[step, h], p_recv.at[s, h], combiner(s)).wait_recv()
            return carry

        lax.fori_loop(1, 8, wait_part, 0)
        for i in range(8):
            total = jnp.zeros((PIECE, HD), jnp.float32)
            for s in range(8):
                column = s * 16 + i // 2 * 4 + h * 2 + i % 2
                total = total + p_in[s, h, i].astype(jnp.float32) * turned[:PIECE, column:column + 1]
            rows_out[h, i] = total.astype(jnp.bfloat16)

        def start_row(i, carry):
            @pl.when(local(i))
            def _():
                own_copy(h).start()

            @pl.when(jnp.logical_not(local(i)))
            def _():
                row_copy(i, h).start()

            return carry

        lax.fori_loop(0, 8, start_row, 0)

    def batch(side_core, h, piece):
        return rows_in.at[side_core, h, piece]

    def ring_copy(h, direction, piece):
        return remote(
            batch(core, h, piece), batch(core, h, piece),
            ring_send.at[h, direction], ring_recv.at[h, direction], (wide, ring[direction] * 2 + core),
        )

    def on_copy(h, piece):
        return remote(
            batch(core, h, piece), batch(core, h, piece), on_send.at[h], on_recv.at[h], (wide, ring[h] * 2 + core)
        )

    def forward(h, piece, side_core):
        return remote(
            batch(side_core, h, piece), batch(side_core, h, piece),
            f_send.at[h, piece], f_recv.at[h, piece], (wide, buddy),
        )

    for h in range(2):
        def wait_row(k, carry):
            mine = own_target & (k == kv)

            @pl.when(mine)
            def _():
                own_copy(h).wait()

            @pl.when(jnp.logical_not(mine))
            def _():
                remote(
                    rows_out.at[h, 0], rows_in.at[core, h, y, k], a_send.at[0, h], a_recv.at[k, h], (wide, buddy)
                ).wait_recv()

            return carry

        lax.fori_loop(0, 8, wait_row, 0)
        for direction in range(2):
            ring_copy(h, direction, y).start()
        forward(h, y, core).start()

    for h in range(2):
        ring_copy(h, h, behind[h]).wait_recv()
        on_copy(h, behind[h]).start()
        forward(h, behind[h], core).start()

    for copy in fetches:
        copy.wait()

    def product(side_core, h):
        rows = jnp.concatenate([rows_in[side_core, h, :, k].reshape(HALF, HD) for k in range(KVH)], axis=1)
        return jnp.dot(
            rows, w_in[side_core * 2 + h].reshape(KVH * HD, 512), preferred_element_type=jnp.float32
        )

    total = jnp.zeros((HALF, 512), jnp.float32)
    for h in range(2):
        ring_copy(h, 1 - h, behind[1 - h]).wait_recv()
        forward(h, behind[1 - h], core).start()
        on_copy(h, (y + 2) % NY).wait_recv()
        forward(h, (y + 2) % NY, core).start()
        total = total + product(core, h)
    for h in range(2):
        for piece in range(NY):
            forward(h, piece, 1 - core).wait_recv()
        total = total + product(1 - core, h)
    result[...] = total.astype(jnp.bfloat16)

    def drain(step, carry):
        lse_copy(step).wait_send()
        part_copy(step, 0).wait_send()

        @pl.when(straight(step))
        def _():
            part_copy(step, 1).wait_send()

        return carry

    lax.fori_loop(1, 8, drain, 0)
    for across in range(2):
        relay_copy(across).wait_send()
        pass_copy(across).wait_send()
    for h in range(2):
        def drain_row(i, carry):
            @pl.when(jnp.logical_not(local(i)))
            def _():
                row_copy(i, h).wait_send()

            return carry

        lax.fori_loop(0, 8, drain_row, 0)
        for direction in range(2):
            ring_copy(h, direction, y).wait_send()
        on_copy(h, behind[h]).wait_send()
        for piece in range(NY):
            forward(h, piece, core).wait_send()


def finish(part, lse, weight):
    anywhere = pl.BlockSpec(memory_space=pl.ANY)
    dma = pltpu.SemaphoreType.DMA
    return pl.pallas_call(
        finish_kernel,
        out_shape=jax.ShapeDtypeStruct((HALF, 512), jnp.bfloat16),
        in_specs=[anywhere] * 3,
        out_specs=pl.BlockSpec(memory_space=pltpu.VMEM),
        scratch_shapes=[
            pltpu.VMEM((8, 2, 8, PIECE, HD), jnp.bfloat16),
            pltpu.VMEM((8, 16, HD), jnp.float32),
            pltpu.VMEM((4, KVH, HD, 512), jnp.bfloat16),
            pltpu.VMEM((2, 8, PIECE, HD), jnp.bfloat16),
            pltpu.VMEM((2, 8, PIECE, HD), jnp.bfloat16),
            pltpu.VMEM((2, 2, NY, KVH, PIECE, HD), jnp.bfloat16),
            dma((8, 2)), dma((8, 2)), dma((8,)), dma((8,)), dma((2,)), dma((2,)), dma((2,)),
            dma((8, 2)), dma((8, 2)), dma((2, 2)), dma((2, 2)), dma((2,)), dma((2,)),
            dma((2, NY)), dma((2, NY)), dma((9,)),
        ],
        compiler_params=pltpu.CompilerParams(
            collective_id=1, has_side_effects=True, vmem_limit_bytes=56 * MIB
        ),
    )(part, lse, weight.reshape(KVH, 4, HD, 512))


def shards(queries, span_keys, span_values, cache_keys, cache_values, chosen, out_weight):
    weight = lax.all_gather(out_weight, "wide", axis=0, tiled=True)
    q, k_pair, v_pair, sk, sv = spread(queries, span_keys, span_values, cache_keys, cache_values)
    part, lse = attend(chosen, q, cache_keys, cache_values, k_pair, v_pair, sk, sv)
    return finish(part, lse, weight)


def solution(mesh):
    return jax.shard_map(
        shards,
        mesh=mesh,
        in_specs=(
            P("wide", None),
            P("wide", None),
            P("wide", None),
            P(("wide", "narrow"), None),
            P(("wide", "narrow"), None),
            P(),
            P("wide", "narrow"),
        ),
        out_specs=P("wide", "narrow"),
        check_vma=False,
    )
```

```python
import math

import jax
import jax.numpy as jnp
from jax import lax
from jax.experimental import pallas as pl
from jax.experimental.pallas import tpu as pltpu
from jax.sharding import PartitionSpec as P

HD = 128
QB = 512
KB = 4096
NQB = 8
NW = 16
KVH = 8
HALF = 256
ROWS = 2 * QB
NY = 4
PIECE = HALF // NY
CHUNK = 256
FLOOR_SCORE = -1e30
SCALE2 = math.log2(math.e) / math.sqrt(HD)
MESH = pl.DeviceIdType.MESH
MIB = 2**20


def place():
    wide = lax.axis_index("wide")
    narrow = lax.axis_index("narrow")
    return wide, narrow, narrow // 2, narrow % 2


def remote(src, dst, send_sem, recv_sem, device):
    return pltpu.make_async_remote_copy(
        src_ref=src, dst_ref=dst, send_sem=send_sem, recv_sem=recv_sem, device_id=device, device_id_type=MESH
    )


def spread_kernel(
    queries, span_k, span_v, cache_k, cache_v,
    q_out, pk_out, pv_out, s_out,
    s_in, q_send, q_recv, ring_send, ring_recv, pass_send, pass_recv,
    kv_send, kv_recv, s_send, s_recv, turn_send, turn_recv, share_send, share_recv, local_sem,
):
    wide, narrow, y, core = place()
    buddy = y * 2 + 1 - core
    z, x, side = wide // 4, wide % 4, wide % 2
    ring = [(y + 1) % NY, (y + NY - 1) % NY]
    behind = ring[::-1]
    barrier = pltpu.get_barrier_semaphore()

    def greet(step, carry):
        pl.semaphore_signal(
            barrier, inc=1, device_id=((wide + step) % NW, narrow), device_id_type=MESH
        )
        return carry

    lax.fori_loop(1, NW, greet, 0)
    for neighbour in (buddy, *((y + step) % NY * 2 + core for step in range(1, NY))):
        pl.semaphore_signal(barrier, inc=1, device_id=(wide, neighbour), device_id_type=MESH)
    pl.semaphore_wait(barrier, NW + 3)

    tokens = pl.ds(pl.multiple_of(y * PIECE, PIECE), PIECE)

    def q_src(kv):
        return queries.at[tokens, pl.ds(pl.multiple_of(kv * 512 + core * 256, 256), 256)]

    def q_copy(dz, dx):
        target = (z + dz) % 4 * 4 + (x + dx) % 4
        return remote(
            q_src(target // 2), q_out.at[wide, y], q_send.at[dz * 4 + dx], q_recv.at[wide], (target, narrow)
        )

    steps = [(dz, dx) for dz in (0, 1, 3, 2) for dx in (0, 1, 3, 2) if dz or dx]
    own_q = pltpu.make_async_copy(q_src(wide // 2), q_out.at[wide, y], local_sem.at[0])

    s_home = wide // 8
    own_s = s_home == side

    def s_src(which, kv):
        return (span_k, span_v)[which].at[tokens, pl.ds(pl.multiple_of(kv * HD, HD), HD)]

    def s_copy(which, kv):
        return remote(
            s_src(which, kv), s_in.at[wide % 8], s_send.at[kv], s_recv.at[wide % 8], (kv * 2 + s_home, narrow)
        )

    def s_local(which):
        return pltpu.make_async_copy(s_src(which, wide // 2), s_in.at[wide % 8], local_sem.at[1])

    def s_start(kv, carry):
        away = jnp.logical_not(own_s & (kv == wide // 2))
        for which in range(2):
            @pl.when((core == which) & away)
            def _():
                s_copy(which, kv).start()

            @pl.when((core == which) & jnp.logical_not(away))
            def _():
                s_local(which).start()

        return carry

    for dz, dx in steps[:3]:
        q_copy(dz, dx).start()
    own_q.start()
    lax.fori_loop(0, KVH, s_start, 0)
    for dz, dx in steps[3:]:
        q_copy(dz, dx).start()
    kv_copies = [
        remote(src, dst, kv_send.at[i], kv_recv.at[i], (wide, buddy))
        for i, (src, dst) in enumerate(((cache_k, pk_out), (cache_v, pv_out)))
    ]
    for copy in kv_copies:
        copy.start()

    def ring_copy(group, direction, piece):
        batch = q_out.at[pl.ds(group * 4, 4), piece]
        return remote(
            batch, batch, ring_send.at[group, direction], ring_recv.at[group, direction],
            (wide, ring[direction] * 2 + core),
        )

    def pass_copy(group, direction, piece):
        batch = q_out.at[pl.ds(group * 4 + direction * 2, 2), piece]
        return remote(
            batch, batch, pass_send.at[group, direction], pass_recv.at[group, direction],
            (wide, ring[direction] * 2 + core),
        )

    own_q.wait()
    groups = [(z + step) % 4 for step in (0, 3, 1, 2)]
    for group in groups:
        for i in range(4):
            source = group * 4 + i

            @pl.when(source != wide)
            def _():
                remote(
                    q_src(0), q_out.at[source, y], q_send.at[1], q_recv.at[source], (source, narrow)
                ).wait_recv()

        for direction in range(2):
            ring_copy(group, direction, y).start()

    def s_wait(i, carry):
        mine = own_s & (i == wide % 8)

        @pl.when(mine)
        def _():
            s_local(0).wait()

        @pl.when(jnp.logical_not(mine))
        def _():
            remote(s_src(0, 0), s_in.at[i], s_send.at[0], s_recv.at[i], (wide, buddy)).wait_recv()

        return carry

    lax.fori_loop(0, 8, s_wait, 0)

    def turn_copy(step):
        to = (y + step) % NY
        return remote(
            s_in.at[pl.ds(to * 2, 2)], s_out.at[core, :, y], turn_send.at[step], turn_recv.at[y],
            (wide, to * 2 + core),
        )

    keep = pltpu.make_async_copy(s_in.at[pl.ds(y * 2, 2)], s_out.at[core, :, y], local_sem.at[2])
    keep.start()
    for step in range(1, NY):
        turn_copy(step).start()

    for group in groups:
        for direction in range(2):
            ring_copy(group, direction, behind[direction]).wait_recv()
            pass_copy(group, direction, behind[direction]).start()

    keep.wait()
    for step in range(1, NY):
        origin = (y + step) % NY
        remote(
            s_in.at[pl.ds(0, 2)], s_out.at[core, :, origin], turn_send.at[step], turn_recv.at[origin], (wide, buddy)
        ).wait_recv()
    share = remote(s_out.at[core], s_out.at[core], share_send.at[0], share_recv.at[core], (wide, buddy))
    share.start()

    for group in groups:
        for direction in range(2):
            pass_copy(group, direction, (y + 2) % NY).wait_recv()
    remote(s_out.at[core], s_out.at[1 - core], share_send.at[0], share_recv.at[1 - core], (wide, buddy)).wait_recv()
    for copy in kv_copies:
        copy.wait()
    share.wait_send()
    for group in groups:
        for direction in range(2):
            ring_copy(group, direction, y).wait_send()
            pass_copy(group, direction, behind[direction]).wait_send()
    for step in range(1, NY):
        turn_copy(step).wait_send()
    for dz, dx in steps:
        q_copy(dz, dx).wait_send()

    def s_drain(kv, carry):
        @pl.when(jnp.logical_not(own_s & (kv == wide // 2)))
        def _():
            s_copy(0, kv).wait_send()

        return carry

    lax.fori_loop(0, KVH, s_drain, 0)


def spread(queries, span_k, span_v, cache_k, cache_v):
    anywhere = pl.BlockSpec(memory_space=pl.ANY)
    shape = lambda *dims: jax.ShapeDtypeStruct(dims, jnp.bfloat16)
    dma = pltpu.SemaphoreType.DMA
    return pl.pallas_call(
        spread_kernel,
        out_shape=[shape(NW, NY, PIECE, 2 * HD), shape(KB, HD), shape(KB, HD), shape(2, 2, NY, PIECE, HD)],
        in_specs=[anywhere] * 5,
        out_specs=[anywhere] * 4,
        scratch_shapes=[
            pltpu.VMEM((8, PIECE, HD), jnp.bfloat16),
            dma((NW,)), dma((NW,)), dma((4, 2)), dma((4, 2)), dma((4, 2)), dma((4, 2)),
            dma((2,)), dma((2,)), dma((KVH,)), dma((8,)), dma((NY,)), dma((NY,)), dma((1,)), dma((2,)), dma((3,)),
        ],
        compiler_params=pltpu.CompilerParams(
            collective_id=0, has_side_effects=True, vmem_limit_bytes=56 * MIB
        ),
    )(queries, span_k, span_v, cache_k, cache_v)


def attend_kernel(
    chosen, q, k_own, v_own, k_pair, v_pair, span, out, lse,
    q_in, k_both, v_wide, sk_in, s_wide, out_in, lse_in, acc, peak, sems, out_sem,
):
    wide, narrow, y, core = place()
    held = wide % 2 * 4 + y
    first = wide % 2 * 8 + y * 2
    moves = [
        (q, q_in),
        (span.at[0], sk_in),
        (span.at[1], s_wide.at[:, :, :, :HD]),
        (k_own, k_both.at[0]),
        (v_own, v_wide.at[0, :, :HD]),
        (k_pair, k_both.at[1]),
        (v_pair, v_wide.at[1, :, :HD]),
    ]
    loads = [pltpu.make_async_copy(src, dst, sems.at[i]) for i, (src, dst) in enumerate(moves)]
    for copy in loads:
        copy.start()
    s_wide[:, :, :, HD:] = jnp.ones((2, NY, PIECE, HD), jnp.bfloat16)
    lse_in[...] = jnp.full((NY, 2, 16, HD), FLOOR_SCORE, jnp.float32)
    for i in range(2):
        v_wide[i, :, HD:] = jnp.ones((KB, HD), jnp.bfloat16)

    def fold(state, queries, keys, values, mask):
        top, total = state
        scores = lax.dot_general(queries, keys, (((1,), (1,)), ((), ())), preferred_element_type=jnp.float32)
        if mask is not None:
            scores = jnp.where(mask, scores, FLOOR_SCORE)
        new_top = jnp.maximum(top, jnp.max(scores, axis=1, keepdims=True))
        decay = jnp.exp2((top - new_top) * SCALE2)
        weights = jnp.exp2((scores - new_top) * SCALE2).astype(jnp.bfloat16)
        total = total * decay + jnp.dot(weights, values, preferred_element_type=jnp.float32)
        return new_top, total

    def block_queries(b):
        rows = q_in[pl.ds(b * 2, 2)].reshape(QB, 2 * HD)
        return jnp.concatenate([rows[:, :HD], rows[:, HD:]], axis=0)

    def load():
        return jnp.max(peak[...], axis=1, keepdims=True), acc[...]

    def save(state):
        peak[...] = jnp.broadcast_to(state[0], (ROWS, HD))
        acc[...] = state[1]

    for copy in loads[:3]:
        copy.wait()
    row = lax.broadcasted_iota(jnp.int32, (ROWS, QB), 0) % QB
    mask = row >= lax.broadcasted_iota(jnp.int32, (ROWS, QB), 1)
    fresh = jnp.full((ROWS, 1), FLOOR_SCORE, jnp.float32), jnp.zeros((ROWS, 2 * HD), jnp.float32)
    save(fold(fresh, block_queries(held), sk_in[...].reshape(QB, HD), s_wide[...].reshape(QB, 2 * HD), mask))
    for copy in loads[3:]:
        copy.wait()

    def send_out(b):
        return pltpu.make_async_copy(
            out_in.at[:, pl.ds(b * 2, 2)], out.at[:, pl.ds(b * 2, 2)], out_sem.at[b]
        )

    def one_block(step, carry):
        b = (held + step) % NQB
        hits = []
        for i in range(2):
            c = first + jnp.where(core == 0, i, 1 - i)
            hits.append((chosen[b, 0] == c) | (chosen[b, 1] == c) | (chosen[b, 2] == c))
        used = hits[0] | hits[1] | (step == 0)

        @pl.when(used & (step != 0))
        def _():
            acc[...] = jnp.zeros((ROWS, 2 * HD), jnp.float32)
            peak[...] = jnp.full((ROWS, HD), FLOOR_SCORE, jnp.float32)

        def cached(i, carry):
            @pl.when(jnp.where(i == 0, hits[0], hits[1]))
            def _():
                queries = block_queries(b)
                state = load()
                for start in range(0, KB, CHUNK):
                    state = fold(
                        state, queries, k_both[i, start:start + CHUNK, :], v_wide[i, start:start + CHUNK, :], None
                    )
                save(state)

            return carry

        lax.fori_loop(0, 2, cached, 0)

        @pl.when(used)
        def _():
            total = acc[:, HD:]
            out_in[:, pl.ds(b * 2, 2)] = (
                (acc[:, :HD] / total).astype(jnp.bfloat16).reshape(2, 2, NY, PIECE, HD)
            )
            logs = peak[...] * SCALE2 + jnp.log2(total)
            eye = lax.broadcasted_iota(jnp.int32, (PIECE, HD), 0) == lax.broadcasted_iota(
                jnp.int32, (PIECE, HD), 1
            )
            for piece in range(NY):
                for part in range(4):
                    start = part * HALF + piece * PIECE
                    lse_in[piece, b // 4, pl.ds(b % 4 * 4 + part, 1), :] = jnp.sum(
                        jnp.where(eye, logs[start:start + PIECE], 0.0), axis=0, keepdims=True
                    )

        @pl.when(jnp.logical_not(used))
        def _():
            out_in[:, pl.ds(b * 2, 2)] = jnp.zeros((2, 2, NY, PIECE, HD), jnp.bfloat16)

        send_out(b).start()
        return carry

    lax.fori_loop(0, NQB, one_block, 0)
    lse_copy = pltpu.make_async_copy(lse_in, lse, sems.at[7])
    lse_copy.start()
    for b in range(NQB):
        send_out(b).wait()
    lse_copy.wait()


def attend(chosen, q, k_own, v_own, k_pair, v_pair, span):
    anywhere = pl.BlockSpec(memory_space=pl.ANY)
    dma = pltpu.SemaphoreType.DMA
    return pl.pallas_call(
        attend_kernel,
        out_shape=[
            jax.ShapeDtypeStruct((2, NW, NY, PIECE, HD), jnp.bfloat16),
            jax.ShapeDtypeStruct((NY, 2, 16, HD), jnp.float32),
        ],
        in_specs=[pl.BlockSpec(memory_space=pltpu.SMEM)] + [anywhere] * 6,
        out_specs=[anywhere] * 2,
        scratch_shapes=[
            pltpu.VMEM((NW, NY, PIECE, 2 * HD), jnp.bfloat16),
            pltpu.VMEM((2, KB, HD), jnp.bfloat16),
            pltpu.VMEM((2, KB, 2 * HD), jnp.bfloat16),
            pltpu.VMEM((2, NY, PIECE, HD), jnp.bfloat16),
            pltpu.VMEM((2, NY, PIECE, 2 * HD), jnp.bfloat16),
            pltpu.VMEM((2, NW, NY, PIECE, HD), jnp.bfloat16),
            pltpu.VMEM((NY, 2, 16, HD), jnp.float32),
            pltpu.VMEM((ROWS, 2 * HD), jnp.float32),
            pltpu.VMEM((ROWS, HD), jnp.float32),
            dma((8,)), dma((NQB,)),
        ],
        compiler_params=pltpu.CompilerParams(vmem_limit_bytes=56 * MIB),
        cost_estimate=pl.CostEstimate(flops=14 * 10**9, bytes_accessed=10 * MIB, transcendentals=25 * 10**6),
    )(chosen, q, k_own, v_own, k_pair, v_pair, span)


def finish_kernel(
    part, lse, weight, result,
    p_in, l_in, w_in, rows_out, rows_in,
    p_send, p_recv, l_send, l_recv,
    a_send, a_recv, ring_send, ring_recv, on_send, on_recv, f_send, f_recv, local_sem,
):
    wide, narrow, y, core = place()
    buddy = y * 2 + 1 - core
    kv, side = wide // 2, wide % 2
    held = side * 4 + y
    ring = [(y + 1) % NY, (y + NY - 1) % NY]
    behind = ring[::-1]
    own_target = wide // 8 == side
    barrier = pltpu.get_barrier_semaphore()

    def combiner(b):
        return kv * 2 + b // 4, b % 4 * 2 + core

    fetches = [pltpu.make_async_copy(weight.at[:, i], w_in.at[i], local_sem.at[i]) for i in range(4)]
    keep = [
        pltpu.make_async_copy(part.at[h, pl.ds(side * 8, 8), y], p_in.at[held, h], local_sem.at[4 + h])
        for h in range(2)
    ]
    keep.append(pltpu.make_async_copy(lse.at[y, side], l_in.at[held], local_sem.at[6]))
    for copy in (*keep, *fetches):
        copy.start()

    def greet(step, carry):
        pl.semaphore_signal(barrier, inc=1, device_id=combiner((held + step) % 8), device_id_type=MESH)
        return carry

    lax.fori_loop(1, 8, greet, 0)

    def greet_source(s, carry):
        @pl.when(jnp.logical_not(own_target & (s == kv)))
        def _():
            pl.semaphore_signal(barrier, inc=1, device_id=(s * 2 + wide // 8, narrow), device_id_type=MESH)

        return carry

    lax.fori_loop(0, 8, greet_source, 0)
    pl.semaphore_signal(barrier, inc=1, device_id=(wide, buddy), device_id_type=MESH)
    pl.semaphore_wait(barrier, 16 - own_target.astype(jnp.int32))

    def share(b, h):
        return part.at[h, pl.ds(b // 4 * 8, 8), b % 4]

    def part_copy(step, h):
        b = (held + step) % 8
        return remote(share(b, h), p_in.at[held, h], p_send.at[step, h], p_recv.at[held, h], combiner(b))

    def lse_copy(step):
        b = (held + step) % 8
        return remote(lse.at[b % 4, b // 4], l_in.at[held], l_send.at[step], l_recv.at[held], combiner(b))

    def start_lse(step, carry):
        lse_copy(step).start()
        return carry

    lax.fori_loop(1, 8, start_lse, 0)
    for h in range(2):
        def start_part(step, carry):
            part_copy(step, h).start()
            return carry

        lax.fori_loop(1, 8, start_part, 0)
    for copy in keep:
        copy.wait()

    def wait_lse(step, carry):
        s = (held + step) % 8
        remote(lse.at[0, 0], l_in.at[s], l_send.at[step], l_recv.at[s], combiner(s)).wait_recv()
        return carry

    lax.fori_loop(1, 8, wait_lse, 0)
    logs = l_in[...]
    shares = jnp.exp2(logs - jnp.max(logs, axis=0, keepdims=True))
    shares = shares / jnp.sum(shares, axis=0, keepdims=True)
    turned = jnp.transpose(shares.reshape(HD, HD))

    def row_copy(i, h):
        return remote(
            rows_out.at[h, i], rows_in.at[core, h, y, kv], a_send.at[i, h], a_recv.at[kv, h], (side * 8 + i, narrow)
        )

    def own_copy(h):
        return pltpu.make_async_copy(rows_out.at[h, wide % 8], rows_in.at[core, h, y, kv], local_sem.at[7 + h])

    def local(i):
        return own_target & (i == wide % 8)

    for h in range(2):
        def wait_part(step, carry):
            s = (held + step) % 8
            remote(share(s, h), p_in.at[s, h], p_send.at[step, h], p_recv.at[s, h], combiner(s)).wait_recv()
            return carry

        lax.fori_loop(1, 8, wait_part, 0)
        for i in range(8):
            total = jnp.zeros((PIECE, HD), jnp.float32)
            for s in range(8):
                column = s * 16 + i // 2 * 4 + h * 2 + i % 2
                total = total + p_in[s, h, i].astype(jnp.float32) * turned[:PIECE, column:column + 1]
            rows_out[h, i] = total.astype(jnp.bfloat16)

        def start_row(i, carry):
            @pl.when(local(i))
            def _():
                own_copy(h).start()

            @pl.when(jnp.logical_not(local(i)))
            def _():
                row_copy(i, h).start()

            return carry

        lax.fori_loop(0, 8, start_row, 0)

    def batch(side_core, h, piece):
        return rows_in.at[side_core, h, piece]

    def ring_copy(h, direction, piece):
        return remote(
            batch(core, h, piece), batch(core, h, piece),
            ring_send.at[h, direction], ring_recv.at[h, direction], (wide, ring[direction] * 2 + core),
        )

    def on_copy(h, piece):
        return remote(
            batch(core, h, piece), batch(core, h, piece), on_send.at[h], on_recv.at[h], (wide, ring[h] * 2 + core)
        )

    def forward(h, piece, side_core):
        return remote(
            batch(side_core, h, piece), batch(side_core, h, piece),
            f_send.at[h, piece], f_recv.at[h, piece], (wide, buddy),
        )

    for h in range(2):
        def wait_row(k, carry):
            mine = own_target & (k == kv)

            @pl.when(mine)
            def _():
                own_copy(h).wait()

            @pl.when(jnp.logical_not(mine))
            def _():
                remote(
                    rows_out.at[h, 0], rows_in.at[core, h, y, k], a_send.at[0, h], a_recv.at[k, h], (wide, buddy)
                ).wait_recv()

            return carry

        lax.fori_loop(0, 8, wait_row, 0)
        for direction in range(2):
            ring_copy(h, direction, y).start()
        forward(h, y, core).start()

    for h in range(2):
        ring_copy(h, h, behind[h]).wait_recv()
        on_copy(h, behind[h]).start()
        forward(h, behind[h], core).start()

    for copy in fetches:
        copy.wait()

    def product(side_core, h):
        rows = jnp.concatenate([rows_in[side_core, h, :, k].reshape(HALF, HD) for k in range(KVH)], axis=1)
        return jnp.dot(
            rows, w_in[side_core * 2 + h].reshape(KVH * HD, 512), preferred_element_type=jnp.float32
        )

    total = jnp.zeros((HALF, 512), jnp.float32)
    for h in range(2):
        ring_copy(h, 1 - h, behind[1 - h]).wait_recv()
        forward(h, behind[1 - h], core).start()
        on_copy(h, (y + 2) % NY).wait_recv()
        forward(h, (y + 2) % NY, core).start()
        total = total + product(core, h)
    for h in range(2):
        for piece in range(NY):
            forward(h, piece, 1 - core).wait_recv()
        total = total + product(1 - core, h)
    result[...] = total.astype(jnp.bfloat16)

    def drain(step, carry):
        lse_copy(step).wait_send()
        for h in range(2):
            part_copy(step, h).wait_send()
        return carry

    lax.fori_loop(1, 8, drain, 0)
    for h in range(2):
        def drain_row(i, carry):
            @pl.when(jnp.logical_not(local(i)))
            def _():
                row_copy(i, h).wait_send()

            return carry

        lax.fori_loop(0, 8, drain_row, 0)
        for direction in range(2):
            ring_copy(h, direction, y).wait_send()
        on_copy(h, behind[h]).wait_send()
        for piece in range(NY):
            forward(h, piece, core).wait_send()


def finish(part, lse, weight):
    anywhere = pl.BlockSpec(memory_space=pl.ANY)
    dma = pltpu.SemaphoreType.DMA
    return pl.pallas_call(
        finish_kernel,
        out_shape=jax.ShapeDtypeStruct((HALF, 512), jnp.bfloat16),
        in_specs=[anywhere] * 3,
        out_specs=pl.BlockSpec(memory_space=pltpu.VMEM),
        scratch_shapes=[
            pltpu.VMEM((8, 2, 8, PIECE, HD), jnp.bfloat16),
            pltpu.VMEM((8, 16, HD), jnp.float32),
            pltpu.VMEM((4, KVH, HD, 512), jnp.bfloat16),
            pltpu.VMEM((2, 8, PIECE, HD), jnp.bfloat16),
            pltpu.VMEM((2, 2, NY, KVH, PIECE, HD), jnp.bfloat16),
            dma((8, 2)), dma((8, 2)), dma((8,)), dma((8,)),
            dma((8, 2)), dma((8, 2)), dma((2, 2)), dma((2, 2)), dma((2,)), dma((2,)),
            dma((2, NY)), dma((2, NY)), dma((9,)),
        ],
        compiler_params=pltpu.CompilerParams(
            collective_id=1, has_side_effects=True, vmem_limit_bytes=56 * MIB
        ),
    )(part, lse, weight.reshape(KVH, 4, HD, 512))


def shards(queries, span_keys, span_values, cache_keys, cache_values, chosen, out_weight):
    weight = lax.all_gather(out_weight, "wide", axis=0, tiled=True)
    q, k_pair, v_pair, span = spread(queries, span_keys, span_values, cache_keys, cache_values)
    part, lse = attend(chosen, q, cache_keys, cache_values, k_pair, v_pair, span)
    return finish(part, lse, weight)


def solution(mesh):
    return jax.shard_map(
        shards,
        mesh=mesh,
        in_specs=(
            P("wide", None),
            P("wide", None),
            P("wide", None),
            P(("wide", "narrow"), None),
            P(("wide", "narrow"), None),
            P(),
            P("wide", "narrow"),
        ),
        out_specs=P("wide", "narrow"),
        check_vma=False,
    )
```

```python
import math

import jax
import jax.numpy as jnp
from jax import lax
from jax.experimental import pallas as pl
from jax.experimental.pallas import tpu as pltpu
from jax.sharding import PartitionSpec as P

HD = 128
QB = 512
KB = 4096
NQB = 8
NW = 16
KVH = 8
HALF = 256
ROWS = 2 * QB
NY = 4
PIECE = HALF // NY
CHUNK = 256
FLOOR_SCORE = -1e30
SCALE2 = math.log2(math.e) / math.sqrt(HD)
MESH = pl.DeviceIdType.MESH
MIB = 2**20


def place():
    wide = lax.axis_index("wide")
    narrow = lax.axis_index("narrow")
    return wide, narrow, narrow // 2, narrow % 2


def remote(src, dst, send_sem, recv_sem, device):
    return pltpu.make_async_remote_copy(
        src_ref=src, dst_ref=dst, send_sem=send_sem, recv_sem=recv_sem, device_id=device, device_id_type=MESH
    )


def spread_kernel(
    queries, span_k, span_v, cache_k, cache_v,
    q_out, pk_out, pv_out, s_out,
    s_in, q_send, q_recv, ring_send, ring_recv, pass_send, pass_recv,
    kv_send, kv_recv, s_send, s_recv, turn_send, turn_recv, share_send, share_recv, local_sem,
):
    wide, narrow, y, core = place()
    buddy = y * 2 + 1 - core
    z, x, side = wide // 4, wide % 4, wide % 2
    ring = [(y + 1) % NY, (y + NY - 1) % NY]
    behind = ring[::-1]
    barrier = pltpu.get_barrier_semaphore()

    def greet(step, carry):
        pl.semaphore_signal(
            barrier, inc=1, device_id=((wide + step) % NW, narrow), device_id_type=MESH
        )
        return carry

    lax.fori_loop(1, NW, greet, 0)
    for neighbour in (buddy, *((y + step) % NY * 2 + core for step in range(1, NY))):
        pl.semaphore_signal(barrier, inc=1, device_id=(wide, neighbour), device_id_type=MESH)
    pl.semaphore_wait(barrier, NW + 3)

    tokens = pl.ds(pl.multiple_of(y * PIECE, PIECE), PIECE)

    def columns(kv):
        return pl.ds(pl.multiple_of(kv * 512 + core * 256, 256), 256)

    def q_copy(dz, dx):
        target = (z + dz) % 4 * 4 + (x + dx) % 4
        rows = tokens if dz else slice(None)
        return remote(
            queries.at[rows, columns(target // 2)], q_out.at[wide, rows],
            q_send.at[dz * 4 + dx], q_recv.at[wide], (target, narrow),
        )

    def q_wait(source, rows):
        remote(
            queries.at[rows, columns(0)], q_out.at[source, rows], q_send.at[1], q_recv.at[source], (source, narrow)
        ).wait_recv()

    steps = [(dz, dx) for dz in (1, 3, 2, 0) for dx in (0, 1, 3, 2) if dz or dx]
    own_q = pltpu.make_async_copy(queries.at[:, columns(wide // 2)], q_out.at[wide], local_sem.at[0])

    s_home = wide // 8
    own_s = s_home == side

    def s_src(which, kv):
        return (span_k, span_v)[which].at[tokens, pl.ds(pl.multiple_of(kv * HD, HD), HD)]

    def s_copy(which, kv):
        return remote(
            s_src(which, kv), s_in.at[wide % 8], s_send.at[kv], s_recv.at[wide % 8], (kv * 2 + s_home, narrow)
        )

    def s_local(which):
        return pltpu.make_async_copy(s_src(which, wide // 2), s_in.at[wide % 8], local_sem.at[1])

    def s_start(kv, carry):
        away = jnp.logical_not(own_s & (kv == wide // 2))
        for which in range(2):
            @pl.when((core == which) & away)
            def _():
                s_copy(which, kv).start()

            @pl.when((core == which) & jnp.logical_not(away))
            def _():
                s_local(which).start()

        return carry

    for dz, dx in steps[:8]:
        q_copy(dz, dx).start()
    lax.fori_loop(0, KVH, s_start, 0)
    for dz, dx in steps[8:]:
        q_copy(dz, dx).start()
    own_q.start()
    kv_copies = [
        remote(src, dst, kv_send.at[i], kv_recv.at[i], (wide, buddy))
        for i, (src, dst) in enumerate(((cache_k, pk_out), (cache_v, pv_out)))
    ]
    for copy in kv_copies:
        copy.start()

    def piece_rows(piece):
        return pl.ds(pl.multiple_of(piece * PIECE, PIECE), PIECE)

    def ring_copy(group, direction, piece):
        batch = q_out.at[pl.ds(group * 4, 4), piece_rows(piece)]
        return remote(
            batch, batch, ring_send.at[group, direction], ring_recv.at[group, direction],
            (wide, ring[direction] * 2 + core),
        )

    def pass_copy(group, direction, piece):
        batch = q_out.at[pl.ds(group * 4 + direction * 2, 2), piece_rows(piece)]
        return remote(
            batch, batch, pass_send.at[group, direction], pass_recv.at[group, direction],
            (wide, ring[direction] * 2 + core),
        )

    groups = [(z + step) % 4 for step in (3, 1, 2)]
    for group in groups:
        for i in range(4):
            q_wait(group * 4 + i, tokens)
        for direction in range(2):
            ring_copy(group, direction, y).start()

    def s_wait(i, carry):
        mine = own_s & (i == wide % 8)

        @pl.when(mine)
        def _():
            s_local(0).wait()

        @pl.when(jnp.logical_not(mine))
        def _():
            remote(s_src(0, 0), s_in.at[i], s_send.at[0], s_recv.at[i], (wide, buddy)).wait_recv()

        return carry

    lax.fori_loop(0, 8, s_wait, 0)

    def turn_copy(step):
        to = (y + step) % NY
        return remote(
            s_in.at[pl.ds(to * 2, 2)], s_out.at[core, :, y], turn_send.at[step], turn_recv.at[y],
            (wide, to * 2 + core),
        )

    keep = pltpu.make_async_copy(s_in.at[pl.ds(y * 2, 2)], s_out.at[core, :, y], local_sem.at[2])
    keep.start()
    for step in range(1, NY):
        turn_copy(step).start()

    for group in groups:
        for direction in range(2):
            ring_copy(group, direction, behind[direction]).wait_recv()
            pass_copy(group, direction, behind[direction]).start()

    keep.wait()
    for step in range(1, NY):
        origin = (y + step) % NY
        remote(
            s_in.at[pl.ds(0, 2)], s_out.at[core, :, origin], turn_send.at[step], turn_recv.at[origin], (wide, buddy)
        ).wait_recv()
    share = remote(s_out.at[core], s_out.at[core], share_send.at[0], share_recv.at[core], (wide, buddy))
    share.start()

    for group in groups:
        for direction in range(2):
            pass_copy(group, direction, (y + 2) % NY).wait_recv()
    remote(s_out.at[core], s_out.at[1 - core], share_send.at[0], share_recv.at[1 - core], (wide, buddy)).wait_recv()
    own_q.wait()
    for dx in range(1, 4):
        q_wait(z * 4 + (x + dx) % 4, slice(None))
    for copy in kv_copies:
        copy.wait()
    share.wait_send()
    for group in groups:
        for direction in range(2):
            ring_copy(group, direction, y).wait_send()
            pass_copy(group, direction, behind[direction]).wait_send()
    for step in range(1, NY):
        turn_copy(step).wait_send()
    for dz, dx in steps:
        q_copy(dz, dx).wait_send()

    def s_drain(kv, carry):
        @pl.when(jnp.logical_not(own_s & (kv == wide // 2)))
        def _():
            s_copy(0, kv).wait_send()

        return carry

    lax.fori_loop(0, KVH, s_drain, 0)


def spread(queries, span_k, span_v, cache_k, cache_v):
    anywhere = pl.BlockSpec(memory_space=pl.ANY)
    shape = lambda *dims: jax.ShapeDtypeStruct(dims, jnp.bfloat16)
    dma = pltpu.SemaphoreType.DMA
    return pl.pallas_call(
        spread_kernel,
        out_shape=[shape(NW, HALF, 2 * HD), shape(KB, HD), shape(KB, HD), shape(2, 2, NY, PIECE, HD)],
        in_specs=[anywhere] * 5,
        out_specs=[anywhere] * 4,
        scratch_shapes=[
            pltpu.VMEM((8, PIECE, HD), jnp.bfloat16),
            dma((NW,)), dma((NW,)), dma((4, 2)), dma((4, 2)), dma((4, 2)), dma((4, 2)),
            dma((2,)), dma((2,)), dma((KVH,)), dma((8,)), dma((NY,)), dma((NY,)), dma((1,)), dma((2,)), dma((3,)),
        ],
        compiler_params=pltpu.CompilerParams(
            collective_id=0, has_side_effects=True, vmem_limit_bytes=56 * MIB
        ),
    )(queries, span_k, span_v, cache_k, cache_v)


def attend_kernel(
    chosen, q, k_own, v_own, k_pair, v_pair, span, out, lse,
    q_in, k_both, v_wide, sk_in, s_wide, out_in, lse_in, acc, peak, sems, out_sem,
):
    wide, narrow, y, core = place()
    held = wide % 2 * 4 + y
    first = wide % 2 * 8 + y * 2
    moves = [
        (q, q_in),
        (span.at[0], sk_in),
        (span.at[1], s_wide.at[:, :, :, :HD]),
        (k_own, k_both.at[0]),
        (v_own, v_wide.at[0, :, :HD]),
        (k_pair, k_both.at[1]),
        (v_pair, v_wide.at[1, :, :HD]),
    ]
    loads = [pltpu.make_async_copy(src, dst, sems.at[i]) for i, (src, dst) in enumerate(moves)]
    for copy in loads:
        copy.start()
    s_wide[:, :, :, HD:] = jnp.ones((2, NY, PIECE, HD), jnp.bfloat16)
    lse_in[...] = jnp.full((2, NY, 2, 8, HD), FLOOR_SCORE, jnp.float32)
    for i in range(2):
        v_wide[i, :, HD:] = jnp.ones((KB, HD), jnp.bfloat16)

    def fold(state, queries, keys, values, mask):
        top, total = state
        scores = lax.dot_general(queries, keys, (((1,), (1,)), ((), ())), preferred_element_type=jnp.float32)
        if mask is not None:
            scores = jnp.where(mask, scores, FLOOR_SCORE)
        new_top = jnp.maximum(top, jnp.max(scores, axis=1, keepdims=True))
        decay = jnp.exp2((top - new_top) * SCALE2)
        weights = jnp.exp2((scores - new_top) * SCALE2).astype(jnp.bfloat16)
        total = total * decay + jnp.dot(weights, values, preferred_element_type=jnp.float32)
        return new_top, total

    def block_queries(b):
        rows = q_in[pl.ds(b * 2, 2)].reshape(QB, 2 * HD)
        return jnp.concatenate([rows[:, :HD], rows[:, HD:]], axis=0)

    def load():
        return jnp.max(peak[...], axis=1, keepdims=True), acc[...]

    def save(state):
        peak[...] = jnp.broadcast_to(state[0], (ROWS, HD))
        acc[...] = state[1]

    for copy in loads[:3]:
        copy.wait()
    row = lax.broadcasted_iota(jnp.int32, (ROWS, QB), 0) % QB
    mask = row >= lax.broadcasted_iota(jnp.int32, (ROWS, QB), 1)
    fresh = jnp.full((ROWS, 1), FLOOR_SCORE, jnp.float32), jnp.zeros((ROWS, 2 * HD), jnp.float32)
    save(fold(fresh, block_queries(held), sk_in[...].reshape(QB, HD), s_wide[...].reshape(QB, 2 * HD), mask))
    for copy in loads[3:]:
        copy.wait()

    def send_out(b):
        return pltpu.make_async_copy(
            out_in.at[:, pl.ds(b * 2, 2)], out.at[:, pl.ds(b * 2, 2)], out_sem.at[b]
        )

    def one_block(step, carry):
        b = (held + step) % NQB
        hits = []
        for i in range(2):
            c = first + jnp.where(core == 0, i, 1 - i)
            hits.append((chosen[b, 0] == c) | (chosen[b, 1] == c) | (chosen[b, 2] == c))
        used = hits[0] | hits[1] | (step == 0)

        @pl.when(used & (step != 0))
        def _():
            acc[...] = jnp.zeros((ROWS, 2 * HD), jnp.float32)
            peak[...] = jnp.full((ROWS, HD), FLOOR_SCORE, jnp.float32)

        def cached(i, carry):
            @pl.when(jnp.where(i == 0, hits[0], hits[1]))
            def _():
                queries = block_queries(b)
                state = load()
                for start in range(0, KB, CHUNK):
                    state = fold(
                        state, queries, k_both[i, start:start + CHUNK, :], v_wide[i, start:start + CHUNK, :], None
                    )
                save(state)

            return carry

        lax.fori_loop(0, 2, cached, 0)

        @pl.when(used)
        def _():
            total = acc[:, HD:]
            out_in[:, pl.ds(b * 2, 2)] = (
                (acc[:, :HD] / total).astype(jnp.bfloat16).reshape(2, 2, NY, PIECE, HD)
            )
            logs = peak[...] * SCALE2 + jnp.log2(total)
            eye = lax.broadcasted_iota(jnp.int32, (PIECE, HD), 0) == lax.broadcasted_iota(
                jnp.int32, (PIECE, HD), 1
            )
            for piece in range(NY):
                for part in range(4):
                    start = part * HALF + piece * PIECE
                    lse_in[part // 2, piece, b // 4, pl.ds(b % 4 * 2 + part % 2, 1), :] = jnp.sum(
                        jnp.where(eye, logs[start:start + PIECE], 0.0), axis=0, keepdims=True
                    )

        @pl.when(jnp.logical_not(used))
        def _():
            out_in[:, pl.ds(b * 2, 2)] = jnp.zeros((2, 2, NY, PIECE, HD), jnp.bfloat16)

        send_out(b).start()
        return carry

    lax.fori_loop(0, NQB, one_block, 0)
    lse_copy = pltpu.make_async_copy(lse_in, lse, sems.at[7])
    lse_copy.start()
    for b in range(NQB):
        send_out(b).wait()
    lse_copy.wait()


def attend(chosen, q, k_own, v_own, k_pair, v_pair, span):
    anywhere = pl.BlockSpec(memory_space=pl.ANY)
    dma = pltpu.SemaphoreType.DMA
    return pl.pallas_call(
        attend_kernel,
        out_shape=[
            jax.ShapeDtypeStruct((2, NW, NY, PIECE, HD), jnp.bfloat16),
            jax.ShapeDtypeStruct((2, NY, 2, 8, HD), jnp.float32),
        ],
        in_specs=[pl.BlockSpec(memory_space=pltpu.SMEM)] + [anywhere] * 6,
        out_specs=[anywhere] * 2,
        scratch_shapes=[
            pltpu.VMEM((NW, HALF, 2 * HD), jnp.bfloat16),
            pltpu.VMEM((2, KB, HD), jnp.bfloat16),
            pltpu.VMEM((2, KB, 2 * HD), jnp.bfloat16),
            pltpu.VMEM((2, NY, PIECE, HD), jnp.bfloat16),
            pltpu.VMEM((2, NY, PIECE, 2 * HD), jnp.bfloat16),
            pltpu.VMEM((2, NW, NY, PIECE, HD), jnp.bfloat16),
            pltpu.VMEM((2, NY, 2, 8, HD), jnp.float32),
            pltpu.VMEM((ROWS, 2 * HD), jnp.float32),
            pltpu.VMEM((ROWS, HD), jnp.float32),
            dma((8,)), dma((NQB,)),
        ],
        compiler_params=pltpu.CompilerParams(vmem_limit_bytes=56 * MIB),
        cost_estimate=pl.CostEstimate(flops=14 * 10**9, bytes_accessed=10 * MIB, transcendentals=25 * 10**6),
    )(chosen, q, k_own, v_own, k_pair, v_pair, span)


def finish_kernel(
    part, lse, weight, result,
    x_in, y_in, x_mid, y_mid, x_last, y_last, lx_in, ly_in, lx_mid, ly_mid, lx_last, ly_last,
    w_in, rows_out, rows_in,
    x_send, x_recv, y_send, y_recv, xm_send, xm_recv, ym_send, ym_recv,
    a_send, a_recv, ring_send, ring_recv, on_send, on_recv, f_send, f_recv, local_sem,
):
    wide, narrow, y, core = place()
    buddy = y * 2 + 1 - core
    kv, side = wide // 2, wide % 2
    ring = [(y + 1) % NY, (y + NY - 1) % NY]
    behind = ring[::-1]
    own_target = wide // 8 == side
    barrier = pltpu.get_barrier_semaphore()

    across = wide + 1 - side * 2, narrow

    def along(step):
        return wide, (y + step) % NY * 2 + core

    fetches = [pltpu.make_async_copy(weight.at[:, i], w_in.at[i], local_sem.at[i]) for i in range(4)]
    keep = [
        pltpu.make_async_copy(part.at[0, pl.ds(side * 8, 8)], x_in.at[0], local_sem.at[4]),
        pltpu.make_async_copy(lse.at[0, :, side], lx_in.at[0], local_sem.at[5]),
        pltpu.make_async_copy(part.at[1, :, y], y_in.at[y], local_sem.at[6]),
        pltpu.make_async_copy(lse.at[1, y], ly_in.at[y], local_sem.at[9]),
    ]
    for copy in (*keep, *fetches):
        copy.start()
    for device in (across, *(along(step) for step in range(1, NY))):
        pl.semaphore_signal(barrier, inc=1, device_id=device, device_id_type=MESH)

    def greet_source(s, carry):
        @pl.when(jnp.logical_not(own_target & (s == kv)))
        def _():
            pl.semaphore_signal(barrier, inc=1, device_id=(s * 2 + wide // 8, narrow), device_id_type=MESH)

        return carry

    lax.fori_loop(0, 8, greet_source, 0)
    pl.semaphore_signal(barrier, inc=1, device_id=(wide, buddy), device_id_type=MESH)
    pl.semaphore_wait(barrier, 13 - own_target.astype(jnp.int32))

    x_copies = [
        remote(part.at[0, pl.ds((1 - side) * 8, 8)], x_in.at[1], x_send.at[0], x_recv.at[0], across),
        remote(lse.at[0, :, 1 - side], lx_in.at[1], x_send.at[1], x_recv.at[1], across),
    ]

    def y_copies(step):
        to = (y + step) % NY
        return [
            remote(part.at[1, :, to], y_in.at[y], y_send.at[step, 0], y_recv.at[y, 0], along(step)),
            remote(lse.at[1, to], ly_in.at[y], y_send.at[step, 1], y_recv.at[y, 1], along(step)),
        ]

    def y_arrivals(step):
        origin = (y + step) % NY
        return [
            remote(part.at[1, :, 0], y_in.at[origin], y_send.at[step, 0], y_recv.at[origin, 0], across),
            remote(lse.at[1, 0], ly_in.at[origin], y_send.at[step, 1], y_recv.at[origin, 1], across),
        ]

    def xm_copies(step):
        to = (y + step) % NY
        return [
            remote(x_mid.at[to], x_last.at[y], xm_send.at[step, 0], xm_recv.at[y, 0], along(step)),
            remote(lx_mid.at[to], lx_last.at[y], xm_send.at[step, 1], xm_recv.at[y, 1], along(step)),
        ]

    def xm_arrivals(step):
        origin = (y + step) % NY
        return [
            remote(x_mid.at[0], x_last.at[origin], xm_send.at[step, 0], xm_recv.at[origin, 0], across),
            remote(lx_mid.at[0], lx_last.at[origin], xm_send.at[step, 1], xm_recv.at[origin, 1], across),
        ]

    ym_copies = [
        remote(y_mid.at[1 - side], y_last, ym_send.at[0], ym_recv.at[0], across),
        remote(ly_mid.at[1 - side], ly_last, ym_send.at[1], ym_recv.at[1], across),
    ]

    for copy in x_copies:
        copy.start()
    for step in (1, 3, 2):
        for copy in y_copies(step):
            copy.start()

    def weigh(logs):
        top = jnp.max(logs, axis=0)
        shares = jnp.exp2(logs - top[None])
        total = jnp.sum(shares, axis=0)
        shares = (shares / total[None]).reshape(-1, HD)
        turned = jnp.transpose(jnp.concatenate([shares] * (HD // shares.shape[0]), axis=0))
        return turned[:PIECE], top + jnp.log2(total)

    def mix(turned, columns, pieces):
        total = jnp.zeros((PIECE, HD), jnp.float32)
        for column, piece in zip(columns, pieces):
            total = total + piece.astype(jnp.float32) * turned[:, column:column + 1]
        return total.astype(jnp.bfloat16)

    for copy in keep:
        copy.wait()
    for copy in x_copies:
        copy.wait_recv()
    turned, logs = weigh(lx_in[...].reshape(2, NY * 8, HD))
    lx_mid[...] = logs.reshape(NY, 8, HD)
    for piece in range(NY):
        for i in range(8):
            column = piece * 8 + i
            x_mid[piece, i] = mix(turned, (column, 32 + column), (x_in[0, i, piece], x_in[1, i, piece]))
    x_keep = [
        pltpu.make_async_copy(x_mid.at[y], x_last.at[y], local_sem.at[10]),
        pltpu.make_async_copy(lx_mid.at[y], lx_last.at[y], local_sem.at[11]),
    ]
    for copy in x_keep:
        copy.start()
    for step in (1, 3, 2):
        for copy in xm_copies(step):
            copy.start()

    for step in (1, 3, 2):
        for copy in y_arrivals(step):
            copy.wait_recv()
    turned, logs = weigh(ly_in[...].reshape(NY, 16, HD))
    ly_mid[...] = logs.reshape(2, 8, HD)
    for i in range(16):
        y_mid[i // 8, i % 8] = mix(turned, [s * 16 + i for s in range(NY)], [y_in[s, i] for s in range(NY)])
    for copy in ym_copies:
        copy.start()

    def row_copy(i, h):
        return remote(
            rows_out.at[h, i], rows_in.at[core, h, y, kv], a_send.at[i, h], a_recv.at[kv, h], (side * 8 + i, narrow)
        )

    def own_copy(h):
        return pltpu.make_async_copy(rows_out.at[h, wide % 8], rows_in.at[core, h, y, kv], local_sem.at[7 + h])

    def local(i):
        return own_target & (i == wide % 8)

    for h in range(2):
        if h == 0:
            for copy in x_keep:
                copy.wait()
            for step in (1, 3, 2):
                for copy in xm_arrivals(step):
                    copy.wait_recv()
            turned, logs = weigh(lx_last[...])
            for i in range(8):
                rows_out[h, i] = mix(turned, [s * 8 + i for s in range(NY)], [x_last[s, i] for s in range(NY)])
        else:
            for copy in ym_copies:
                copy.wait_recv()
            turned, logs = weigh(jnp.stack([ly_mid[side], ly_last[...]]))
            for i in range(8):
                rows_out[h, i] = mix(turned, (i, 8 + i), (y_mid[side, i], y_last[i]))

        def start_row(i, carry):
            @pl.when(local(i))
            def _():
                own_copy(h).start()

            @pl.when(jnp.logical_not(local(i)))
            def _():
                row_copy(i, h).start()

            return carry

        lax.fori_loop(0, 8, start_row, 0)

    def batch(side_core, h, piece):
        return rows_in.at[side_core, h, piece]

    def ring_copy(h, direction, piece):
        return remote(
            batch(core, h, piece), batch(core, h, piece),
            ring_send.at[h, direction], ring_recv.at[h, direction], (wide, ring[direction] * 2 + core),
        )

    def on_copy(h, piece):
        return remote(
            batch(core, h, piece), batch(core, h, piece), on_send.at[h], on_recv.at[h], (wide, ring[h] * 2 + core)
        )

    def forward(h, piece, side_core):
        return remote(
            batch(side_core, h, piece), batch(side_core, h, piece),
            f_send.at[h, piece], f_recv.at[h, piece], (wide, buddy),
        )

    for h in range(2):
        def wait_row(k, carry):
            mine = own_target & (k == kv)

            @pl.when(mine)
            def _():
                own_copy(h).wait()

            @pl.when(jnp.logical_not(mine))
            def _():
                remote(
                    rows_out.at[h, 0], rows_in.at[core, h, y, k], a_send.at[0, h], a_recv.at[k, h], (wide, buddy)
                ).wait_recv()

            return carry

        lax.fori_loop(0, 8, wait_row, 0)
        for direction in range(2):
            ring_copy(h, direction, y).start()
        forward(h, y, core).start()

    for h in range(2):
        ring_copy(h, h, behind[h]).wait_recv()
        on_copy(h, behind[h]).start()
        forward(h, behind[h], core).start()

    for copy in fetches:
        copy.wait()

    def product(side_core, h):
        rows = jnp.concatenate([rows_in[side_core, h, :, k].reshape(HALF, HD) for k in range(KVH)], axis=1)
        return jnp.dot(
            rows, w_in[side_core * 2 + h].reshape(KVH * HD, 512), preferred_element_type=jnp.float32
        )

    total = jnp.zeros((HALF, 512), jnp.float32)
    for h in range(2):
        ring_copy(h, 1 - h, behind[1 - h]).wait_recv()
        forward(h, behind[1 - h], core).start()
        on_copy(h, (y + 2) % NY).wait_recv()
        forward(h, (y + 2) % NY, core).start()
        total = total + product(core, h)
    for h in range(2):
        for piece in range(NY):
            forward(h, piece, 1 - core).wait_recv()
        total = total + product(1 - core, h)
    result[...] = total.astype(jnp.bfloat16)

    for copy in (*x_copies, *ym_copies):
        copy.wait_send()
    for step in range(1, NY):
        for copy in (*y_copies(step), *xm_copies(step)):
            copy.wait_send()
    for h in range(2):
        def drain_row(i, carry):
            @pl.when(jnp.logical_not(local(i)))
            def _():
                row_copy(i, h).wait_send()

            return carry

        lax.fori_loop(0, 8, drain_row, 0)
        for direction in range(2):
            ring_copy(h, direction, y).wait_send()
        on_copy(h, behind[h]).wait_send()
        for piece in range(NY):
            forward(h, piece, core).wait_send()


def finish(part, lse, weight):
    anywhere = pl.BlockSpec(memory_space=pl.ANY)
    dma = pltpu.SemaphoreType.DMA
    return pl.pallas_call(
        finish_kernel,
        out_shape=jax.ShapeDtypeStruct((HALF, 512), jnp.bfloat16),
        in_specs=[anywhere] * 3,
        out_specs=pl.BlockSpec(memory_space=pltpu.VMEM),
        scratch_shapes=[
            pltpu.VMEM((2, 8, NY, PIECE, HD), jnp.bfloat16),
            pltpu.VMEM((NY, 16, PIECE, HD), jnp.bfloat16),
            pltpu.VMEM((NY, 8, PIECE, HD), jnp.bfloat16),
            pltpu.VMEM((2, 8, PIECE, HD), jnp.bfloat16),
            pltpu.VMEM((NY, 8, PIECE, HD), jnp.bfloat16),
            pltpu.VMEM((8, PIECE, HD), jnp.bfloat16),
            pltpu.VMEM((2, NY, 8, HD), jnp.float32),
            pltpu.VMEM((NY, 2, 8, HD), jnp.float32),
            pltpu.VMEM((NY, 8, HD), jnp.float32),
            pltpu.VMEM((2, 8, HD), jnp.float32),
            pltpu.VMEM((NY, 8, HD), jnp.float32),
            pltpu.VMEM((8, HD), jnp.float32),
            pltpu.VMEM((4, KVH, HD, 512), jnp.bfloat16),
            pltpu.VMEM((2, 8, PIECE, HD), jnp.bfloat16),
            pltpu.VMEM((2, 2, NY, KVH, PIECE, HD), jnp.bfloat16),
            dma((2,)), dma((2,)), dma((NY, 2)), dma((NY, 2)), dma((NY, 2)), dma((NY, 2)), dma((2,)), dma((2,)),
            dma((8, 2)), dma((8, 2)), dma((2, 2)), dma((2, 2)), dma((2,)), dma((2,)),
            dma((2, NY)), dma((2, NY)), dma((12,)),
        ],
        compiler_params=pltpu.CompilerParams(
            collective_id=1, has_side_effects=True, vmem_limit_bytes=56 * MIB
        ),
    )(part, lse, weight.reshape(KVH, 4, HD, 512))


def shards(queries, span_keys, span_values, cache_keys, cache_values, chosen, out_weight):
    weight = lax.all_gather(out_weight, "wide", axis=0, tiled=True)
    q, k_pair, v_pair, span = spread(queries, span_keys, span_values, cache_keys, cache_values)
    part, lse = attend(chosen, q, cache_keys, cache_values, k_pair, v_pair, span)
    return finish(part, lse, weight)


def solution(mesh):
    return jax.shard_map(
        shards,
        mesh=mesh,
        in_specs=(
            P("wide", None),
            P("wide", None),
            P("wide", None),
            P(("wide", "narrow"), None),
            P(("wide", "narrow"), None),
            P(),
            P("wide", "narrow"),
        ),
        out_specs=P("wide", "narrow"),
        check_vma=False,
    )
```

```python
import math

import jax
import jax.numpy as jnp
from jax import lax
from jax.experimental import pallas as pl
from jax.experimental.pallas import tpu as pltpu
from jax.sharding import PartitionSpec as P

HD = 128
QB = 512
KB = 4096
NQB = 8
NW = 16
KVH = 8
HALF = 256
ROWS = 2 * QB
NY = 4
PIECE = HALF // NY
CHUNK = 256
FLOOR_SCORE = -1e30
SCALE2 = math.log2(math.e) / math.sqrt(HD)
MESH = pl.DeviceIdType.MESH
MIB = 2**20


def place():
    wide = lax.axis_index("wide")
    narrow = lax.axis_index("narrow")
    return wide, narrow, narrow // 2, narrow % 2


def remote(src, dst, send_sem, recv_sem, device):
    return pltpu.make_async_remote_copy(
        src_ref=src, dst_ref=dst, send_sem=send_sem, recv_sem=recv_sem, device_id=device, device_id_type=MESH
    )


def spread_kernel(
    queries, span_k, span_v, cache_k, cache_v,
    q_out, pk_out, pv_out, s_out,
    s_in, q_send, q_recv, ring_send, ring_recv, pass_send, pass_recv,
    kv_send, kv_recv, s_send, s_recv, turn_send, turn_recv, share_send, share_recv, local_sem,
):
    wide, narrow, y, core = place()
    buddy = y * 2 + 1 - core
    z, x, side = wide // 4, wide % 4, wide % 2
    ring = [(y + 1) % NY, (y + NY - 1) % NY]
    behind = ring[::-1]
    barrier = pltpu.get_barrier_semaphore()

    def greet(step, carry):
        pl.semaphore_signal(
            barrier, inc=1, device_id=((wide + step) % NW, narrow), device_id_type=MESH
        )
        return carry

    lax.fori_loop(1, NW, greet, 0)
    for neighbour in (buddy, *((y + step) % NY * 2 + core for step in range(1, NY))):
        pl.semaphore_signal(barrier, inc=1, device_id=(wide, neighbour), device_id_type=MESH)
    pl.semaphore_wait(barrier, NW + 3)

    tokens = pl.ds(pl.multiple_of(y * PIECE, PIECE), PIECE)

    def columns(kv):
        return pl.ds(pl.multiple_of(kv * 512 + core * 256, 256), 256)

    def q_copy(dz, dx):
        target = (z + dz) % 4 * 4 + (x + dx) % 4
        rows = tokens if dz else slice(None)
        return remote(
            queries.at[rows, columns(target // 2)], q_out.at[wide, rows],
            q_send.at[dz * 4 + dx], q_recv.at[wide], (target, narrow),
        )

    def q_wait(source, rows):
        remote(
            queries.at[rows, columns(0)], q_out.at[source, rows], q_send.at[1], q_recv.at[source], (source, narrow)
        ).wait_recv()

    steps = [(dz, dx) for dz in (1, 3, 2, 0) for dx in (0, 1, 3, 2) if dz or dx]
    own_q = pltpu.make_async_copy(queries.at[:, columns(wide // 2)], q_out.at[wide], local_sem.at[0])

    s_home = wide // 8
    own_s = s_home == side

    def s_src(which, kv):
        return (span_k, span_v)[which].at[tokens, pl.ds(pl.multiple_of(kv * HD, HD), HD)]

    def s_copy(which, kv):
        return remote(
            s_src(which, kv), s_in.at[wide % 8], s_send.at[kv], s_recv.at[wide % 8], (kv * 2 + s_home, narrow)
        )

    def s_local(which):
        return pltpu.make_async_copy(s_src(which, wide // 2), s_in.at[wide % 8], local_sem.at[1])

    def s_start(kv, carry):
        away = jnp.logical_not(own_s & (kv == wide // 2))
        for which in range(2):
            @pl.when((core == which) & away)
            def _():
                s_copy(which, kv).start()

            @pl.when((core == which) & jnp.logical_not(away))
            def _():
                s_local(which).start()

        return carry

    for dz, dx in steps[:8]:
        q_copy(dz, dx).start()
    lax.fori_loop(0, KVH, s_start, 0)
    for dz, dx in steps[8:]:
        q_copy(dz, dx).start()
    own_q.start()
    kv_copies = [
        remote(src, dst, kv_send.at[i], kv_recv.at[i], (wide, buddy))
        for i, (src, dst) in enumerate(((cache_k, pk_out), (cache_v, pv_out)))
    ]
    for copy in kv_copies:
        copy.start()

    def piece_rows(piece):
        return pl.ds(pl.multiple_of(piece * PIECE, PIECE), PIECE)

    def ring_copy(group, direction, piece):
        batch = q_out.at[pl.ds(group * 4, 4), piece_rows(piece)]
        return remote(
            batch, batch, ring_send.at[group, direction], ring_recv.at[group, direction],
            (wide, ring[direction] * 2 + core),
        )

    def pass_copy(group, direction, piece):
        batch = q_out.at[pl.ds(group * 4 + direction * 2, 2), piece_rows(piece)]
        return remote(
            batch, batch, pass_send.at[group, direction], pass_recv.at[group, direction],
            (wide, ring[direction] * 2 + core),
        )

    groups = [(z + step) % 4 for step in (3, 1, 2)]
    for group in groups:
        for i in range(4):
            q_wait(group * 4 + i, tokens)
        for direction in range(2):
            ring_copy(group, direction, y).start()

    def s_wait(i, carry):
        mine = own_s & (i == wide % 8)

        @pl.when(mine)
        def _():
            s_local(0).wait()

        @pl.when(jnp.logical_not(mine))
        def _():
            remote(s_src(0, 0), s_in.at[i], s_send.at[0], s_recv.at[i], (wide, buddy)).wait_recv()

        return carry

    lax.fori_loop(0, 8, s_wait, 0)

    def turn_copy(step):
        to = (y + step) % NY
        return remote(
            s_in.at[pl.ds(to * 2, 2)], s_out.at[core, :, y], turn_send.at[step], turn_recv.at[y],
            (wide, to * 2 + core),
        )

    keep = pltpu.make_async_copy(s_in.at[pl.ds(y * 2, 2)], s_out.at[core, :, y], local_sem.at[2])
    keep.start()
    for step in range(1, NY):
        turn_copy(step).start()

    for group in groups:
        for direction in range(2):
            ring_copy(group, direction, behind[direction]).wait_recv()
            pass_copy(group, direction, behind[direction]).start()

    keep.wait()
    for step in range(1, NY):
        origin = (y + step) % NY
        remote(
            s_in.at[pl.ds(0, 2)], s_out.at[core, :, origin], turn_send.at[step], turn_recv.at[origin], (wide, buddy)
        ).wait_recv()
    share = remote(s_out.at[core], s_out.at[core], share_send.at[0], share_recv.at[core], (wide, buddy))
    share.start()

    for group in groups:
        for direction in range(2):
            pass_copy(group, direction, (y + 2) % NY).wait_recv()
    remote(s_out.at[core], s_out.at[1 - core], share_send.at[0], share_recv.at[1 - core], (wide, buddy)).wait_recv()
    own_q.wait()
    for dx in range(1, 4):
        q_wait(z * 4 + (x + dx) % 4, slice(None))
    for copy in kv_copies:
        copy.wait()
    share.wait_send()
    for group in groups:
        for direction in range(2):
            ring_copy(group, direction, y).wait_send()
            pass_copy(group, direction, behind[direction]).wait_send()
    for step in range(1, NY):
        turn_copy(step).wait_send()
    for dz, dx in steps:
        q_copy(dz, dx).wait_send()

    def s_drain(kv, carry):
        @pl.when(jnp.logical_not(own_s & (kv == wide // 2)))
        def _():
            s_copy(0, kv).wait_send()

        return carry

    lax.fori_loop(0, KVH, s_drain, 0)


def spread(queries, span_k, span_v, cache_k, cache_v):
    anywhere = pl.BlockSpec(memory_space=pl.ANY)
    shape = lambda *dims: jax.ShapeDtypeStruct(dims, jnp.bfloat16)
    dma = pltpu.SemaphoreType.DMA
    return pl.pallas_call(
        spread_kernel,
        out_shape=[shape(NW, HALF, 2 * HD), shape(KB, HD), shape(KB, HD), shape(2, 2, NY, PIECE, HD)],
        in_specs=[anywhere] * 5,
        out_specs=[anywhere] * 4,
        scratch_shapes=[
            pltpu.VMEM((8, PIECE, HD), jnp.bfloat16),
            dma((NW,)), dma((NW,)), dma((4, 2)), dma((4, 2)), dma((4, 2)), dma((4, 2)),
            dma((2,)), dma((2,)), dma((KVH,)), dma((8,)), dma((NY,)), dma((NY,)), dma((1,)), dma((2,)), dma((3,)),
        ],
        compiler_params=pltpu.CompilerParams(
            collective_id=0, has_side_effects=True, vmem_limit_bytes=56 * MIB
        ),
    )(queries, span_k, span_v, cache_k, cache_v)


def attend_kernel(
    chosen, q, k_own, v_own, k_pair, v_pair, span, out, lse,
    q_in, k_both, v_wide, sk_in, s_wide, out_in, lse_in, acc, peak, sems, out_sem,
):
    wide, narrow, y, core = place()
    held = wide % 2 * 4 + y
    first = wide % 2 * 8 + y * 2
    moves = [
        (q, q_in),
        (span.at[0], sk_in),
        (span.at[1], s_wide.at[:, :, :, :HD]),
        (k_own, k_both.at[0]),
        (v_own, v_wide.at[0, :, :HD]),
        (k_pair, k_both.at[1]),
        (v_pair, v_wide.at[1, :, :HD]),
    ]
    loads = [pltpu.make_async_copy(src, dst, sems.at[i]) for i, (src, dst) in enumerate(moves)]
    for copy in loads:
        copy.start()
    s_wide[:, :, :, HD:] = jnp.ones((2, NY, PIECE, HD), jnp.bfloat16)
    lse_in[...] = jnp.full((2, NY, 2, 8, HD), FLOOR_SCORE, jnp.float32)
    for i in range(2):
        v_wide[i, :, HD:] = jnp.ones((KB, HD), jnp.bfloat16)

    def fold(state, queries, keys, values, mask):
        top, total = state
        scores = lax.dot_general(queries, keys, (((1,), (1,)), ((), ())), preferred_element_type=jnp.float32)
        if mask is not None:
            scores = jnp.where(mask, scores, FLOOR_SCORE)
        new_top = jnp.maximum(top, jnp.max(scores, axis=1, keepdims=True))
        decay = jnp.exp2((top - new_top) * SCALE2)
        weights = jnp.exp2((scores - new_top) * SCALE2).astype(jnp.bfloat16)
        total = total * decay + jnp.dot(weights, values, preferred_element_type=jnp.float32)
        return new_top, total

    def block_queries(b):
        rows = q_in[pl.ds(b * 2, 2)].reshape(QB, 2 * HD)
        return jnp.concatenate([rows[:, :HD], rows[:, HD:]], axis=0)

    def load():
        return jnp.max(peak[...], axis=1, keepdims=True), acc[...]

    def save(state):
        peak[...] = jnp.broadcast_to(state[0], (ROWS, HD))
        acc[...] = state[1]

    for copy in loads[:3]:
        copy.wait()
    row = lax.broadcasted_iota(jnp.int32, (ROWS, QB), 0) % QB
    mask = row >= lax.broadcasted_iota(jnp.int32, (ROWS, QB), 1)
    fresh = jnp.full((ROWS, 1), FLOOR_SCORE, jnp.float32), jnp.zeros((ROWS, 2 * HD), jnp.float32)
    save(fold(fresh, block_queries(held), sk_in[...].reshape(QB, HD), s_wide[...].reshape(QB, 2 * HD), mask))
    for copy in loads[3:]:
        copy.wait()

    def send_out(b):
        return pltpu.make_async_copy(
            out_in.at[:, pl.ds(b * 2, 2)], out.at[:, pl.ds(b * 2, 2)], out_sem.at[b]
        )

    def one_block(step, carry):
        b = (held + step) % NQB
        hits = []
        for i in range(2):
            c = first + jnp.where(core == 0, i, 1 - i)
            hits.append((chosen[0, b] == c) | (chosen[1, b] == c) | (chosen[2, b] == c))
        used = hits[0] | hits[1] | (step == 0)

        @pl.when(used & (step != 0))
        def _():
            acc[...] = jnp.zeros((ROWS, 2 * HD), jnp.float32)
            peak[...] = jnp.full((ROWS, HD), FLOOR_SCORE, jnp.float32)

        def cached(i, carry):
            @pl.when(jnp.where(i == 0, hits[0], hits[1]))
            def _():
                queries = block_queries(b)
                state = load()
                for start in range(0, KB, CHUNK):
                    state = fold(
                        state, queries, k_both[i, start:start + CHUNK, :], v_wide[i, start:start + CHUNK, :], None
                    )
                save(state)

            return carry

        lax.fori_loop(0, 2, cached, 0)

        @pl.when(used)
        def _():
            total = acc[:, HD:]
            out_in[:, pl.ds(b * 2, 2)] = (
                (acc[:, :HD] / total).astype(jnp.bfloat16).reshape(2, 2, NY, PIECE, HD)
            )
            logs = peak[...] * SCALE2 + jnp.log2(total)
            eye = lax.broadcasted_iota(jnp.int32, (PIECE, HD), 0) == lax.broadcasted_iota(
                jnp.int32, (PIECE, HD), 1
            )
            for piece in range(NY):
                for part in range(4):
                    start = part * HALF + piece * PIECE
                    lse_in[part // 2, piece, b // 4, pl.ds(b % 4 * 2 + part % 2, 1), :] = jnp.sum(
                        jnp.where(eye, logs[start:start + PIECE], 0.0), axis=0, keepdims=True
                    )

        @pl.when(jnp.logical_not(used))
        def _():
            out_in[:, pl.ds(b * 2, 2)] = jnp.zeros((2, 2, NY, PIECE, HD), jnp.bfloat16)

        send_out(b).start()
        return carry

    lax.fori_loop(0, NQB, one_block, 0)
    lse_copy = pltpu.make_async_copy(lse_in, lse, sems.at[7])
    lse_copy.start()
    for b in range(NQB):
        send_out(b).wait()
    lse_copy.wait()


def attend(chosen, q, k_own, v_own, k_pair, v_pair, span):
    anywhere = pl.BlockSpec(memory_space=pl.ANY)
    dma = pltpu.SemaphoreType.DMA
    return pl.pallas_call(
        attend_kernel,
        out_shape=[
            jax.ShapeDtypeStruct((2, NW, NY, PIECE, HD), jnp.bfloat16),
            jax.ShapeDtypeStruct((2, NY, 2, 8, HD), jnp.float32),
        ],
        in_specs=[pl.BlockSpec(memory_space=pltpu.SMEM)] + [anywhere] * 6,
        out_specs=[anywhere] * 2,
        scratch_shapes=[
            pltpu.VMEM((NW, HALF, 2 * HD), jnp.bfloat16),
            pltpu.VMEM((2, KB, HD), jnp.bfloat16),
            pltpu.VMEM((2, KB, 2 * HD), jnp.bfloat16),
            pltpu.VMEM((2, NY, PIECE, HD), jnp.bfloat16),
            pltpu.VMEM((2, NY, PIECE, 2 * HD), jnp.bfloat16),
            pltpu.VMEM((2, NW, NY, PIECE, HD), jnp.bfloat16),
            pltpu.VMEM((2, NY, 2, 8, HD), jnp.float32),
            pltpu.VMEM((ROWS, 2 * HD), jnp.float32),
            pltpu.VMEM((ROWS, HD), jnp.float32),
            dma((8,)), dma((NQB,)),
        ],
        compiler_params=pltpu.CompilerParams(vmem_limit_bytes=56 * MIB),
        cost_estimate=pl.CostEstimate(flops=14 * 10**9, bytes_accessed=10 * MIB, transcendentals=25 * 10**6),
    )(chosen, q, k_own, v_own, k_pair, v_pair, span)


def finish_kernel(
    part, lse, weight, result,
    x_in, y_in, x_mid, y_mid, x_last, y_last, lx_in, ly_in, lx_mid, ly_mid, lx_last, ly_last,
    w_in, rows_out, rows_in,
    x_send, x_recv, y_send, y_recv, xm_send, xm_recv, ym_send, ym_recv,
    a_send, a_recv, ring_send, ring_recv, on_send, on_recv, f_send, f_recv, local_sem,
):
    wide, narrow, y, core = place()
    buddy = y * 2 + 1 - core
    kv, side = wide // 2, wide % 2
    ring = [(y + 1) % NY, (y + NY - 1) % NY]
    behind = ring[::-1]
    own_target = wide // 8 == side
    barrier = pltpu.get_barrier_semaphore()

    across = wide + 1 - side * 2, narrow

    def along(step):
        return wide, (y + step) % NY * 2 + core

    fetches = [pltpu.make_async_copy(weight.at[:, i], w_in.at[i], local_sem.at[i]) for i in range(4)]
    keep = [
        pltpu.make_async_copy(part.at[0, pl.ds(side * 8, 8)], x_in.at[0], local_sem.at[4]),
        pltpu.make_async_copy(lse.at[0, :, side], lx_in.at[0], local_sem.at[5]),
        pltpu.make_async_copy(part.at[1, :, y], y_in.at[y], local_sem.at[6]),
        pltpu.make_async_copy(lse.at[1, y], ly_in.at[y], local_sem.at[9]),
    ]
    for copy in (*keep, *fetches):
        copy.start()
    for device in (across, *(along(step) for step in range(1, NY))):
        pl.semaphore_signal(barrier, inc=1, device_id=device, device_id_type=MESH)

    def greet_source(s, carry):
        @pl.when(jnp.logical_not(own_target & (s == kv)))
        def _():
            pl.semaphore_signal(barrier, inc=1, device_id=(s * 2 + wide // 8, narrow), device_id_type=MESH)

        return carry

    lax.fori_loop(0, 8, greet_source, 0)
    pl.semaphore_signal(barrier, inc=1, device_id=(wide, buddy), device_id_type=MESH)
    pl.semaphore_wait(barrier, 13 - own_target.astype(jnp.int32))

    x_copies = [
        remote(part.at[0, pl.ds((1 - side) * 8, 8)], x_in.at[1], x_send.at[0], x_recv.at[0], across),
        remote(lse.at[0, :, 1 - side], lx_in.at[1], x_send.at[1], x_recv.at[1], across),
    ]

    def y_copies(step):
        to = (y + step) % NY
        return [
            remote(part.at[1, :, to], y_in.at[y], y_send.at[step, 0], y_recv.at[y, 0], along(step)),
            remote(lse.at[1, to], ly_in.at[y], y_send.at[step, 1], y_recv.at[y, 1], along(step)),
        ]

    def y_arrivals(step):
        origin = (y + step) % NY
        return [
            remote(part.at[1, :, 0], y_in.at[origin], y_send.at[step, 0], y_recv.at[origin, 0], across),
            remote(lse.at[1, 0], ly_in.at[origin], y_send.at[step, 1], y_recv.at[origin, 1], across),
        ]

    def xm_copies(step):
        to = (y + step) % NY
        return [
            remote(x_mid.at[to], x_last.at[y], xm_send.at[step, 0], xm_recv.at[y, 0], along(step)),
            remote(lx_mid.at[to], lx_last.at[y], xm_send.at[step, 1], xm_recv.at[y, 1], along(step)),
        ]

    def xm_arrivals(step):
        origin = (y + step) % NY
        return [
            remote(x_mid.at[0], x_last.at[origin], xm_send.at[step, 0], xm_recv.at[origin, 0], across),
            remote(lx_mid.at[0], lx_last.at[origin], xm_send.at[step, 1], xm_recv.at[origin, 1], across),
        ]

    ym_copies = [
        remote(y_mid.at[1 - side], y_last, ym_send.at[0], ym_recv.at[0], across),
        remote(ly_mid.at[1 - side], ly_last, ym_send.at[1], ym_recv.at[1], across),
    ]

    for copy in x_copies:
        copy.start()
    for step in (1, 3, 2):
        for copy in y_copies(step):
            copy.start()

    def weigh(logs):
        top = jnp.max(logs, axis=0)
        shares = jnp.exp2(logs - top[None])
        total = jnp.sum(shares, axis=0)
        shares = (shares / total[None]).reshape(-1, HD)
        turned = jnp.transpose(jnp.concatenate([shares] * (HD // shares.shape[0]), axis=0))
        return turned[:PIECE], top + jnp.log2(total)

    def mix(turned, columns, pieces):
        total = jnp.zeros((PIECE, HD), jnp.float32)
        for column, piece in zip(columns, pieces):
            total = total + piece.astype(jnp.float32) * turned[:, column:column + 1]
        return total.astype(jnp.bfloat16)

    for copy in keep:
        copy.wait()
    for copy in x_copies:
        copy.wait_recv()
    turned, logs = weigh(lx_in[...].reshape(2, NY * 8, HD))
    lx_mid[...] = logs.reshape(NY, 8, HD)
    for piece in range(NY):
        for i in range(8):
            column = piece * 8 + i
            x_mid[piece, i] = mix(turned, (column, 32 + column), (x_in[0, i, piece], x_in[1, i, piece]))
    x_keep = [
        pltpu.make_async_copy(x_mid.at[y], x_last.at[y], local_sem.at[10]),
        pltpu.make_async_copy(lx_mid.at[y], lx_last.at[y], local_sem.at[11]),
    ]
    for copy in x_keep:
        copy.start()
    for step in (1, 3, 2):
        for copy in xm_copies(step):
            copy.start()

    for step in (1, 3, 2):
        for copy in y_arrivals(step):
            copy.wait_recv()
    turned, logs = weigh(ly_in[...].reshape(NY, 16, HD))
    ly_mid[...] = logs.reshape(2, 8, HD)
    for i in range(16):
        y_mid[i // 8, i % 8] = mix(turned, [s * 16 + i for s in range(NY)], [y_in[s, i] for s in range(NY)])
    for copy in ym_copies:
        copy.start()

    def row_copy(i, h):
        return remote(
            rows_out.at[h, i], rows_in.at[core, h, y, kv], a_send.at[i, h], a_recv.at[kv, h], (side * 8 + i, narrow)
        )

    def own_copy(h):
        return pltpu.make_async_copy(rows_out.at[h, wide % 8], rows_in.at[core, h, y, kv], local_sem.at[7 + h])

    def local(i):
        return own_target & (i == wide % 8)

    for h in (1, 0):
        if h == 0:
            for copy in x_keep:
                copy.wait()
            for step in (1, 3, 2):
                for copy in xm_arrivals(step):
                    copy.wait_recv()
            turned, logs = weigh(lx_last[...])
            for i in range(8):
                rows_out[h, i] = mix(turned, [s * 8 + i for s in range(NY)], [x_last[s, i] for s in range(NY)])
        else:
            for copy in ym_copies:
                copy.wait_recv()
            turned, logs = weigh(jnp.stack([ly_mid[side], ly_last[...]]))
            for i in range(8):
                rows_out[h, i] = mix(turned, (i, 8 + i), (y_mid[side, i], y_last[i]))

        def start_row(i, carry):
            @pl.when(local(i))
            def _():
                own_copy(h).start()

            @pl.when(jnp.logical_not(local(i)))
            def _():
                row_copy(i, h).start()

            return carry

        lax.fori_loop(0, 8, start_row, 0)

    def batch(side_core, h, piece):
        return rows_in.at[side_core, h, piece]

    def ring_copy(h, direction, piece):
        return remote(
            batch(core, h, piece), batch(core, h, piece),
            ring_send.at[h, direction], ring_recv.at[h, direction], (wide, ring[direction] * 2 + core),
        )

    def on_copy(h, piece):
        return remote(
            batch(core, h, piece), batch(core, h, piece), on_send.at[h], on_recv.at[h], (wide, ring[h] * 2 + core)
        )

    def forward(h, piece, side_core):
        return remote(
            batch(side_core, h, piece), batch(side_core, h, piece),
            f_send.at[h, piece], f_recv.at[h, piece], (wide, buddy),
        )

    for h in (1, 0):
        def wait_row(k, carry):
            mine = own_target & (k == kv)

            @pl.when(mine)
            def _():
                own_copy(h).wait()

            @pl.when(jnp.logical_not(mine))
            def _():
                remote(
                    rows_out.at[h, 0], rows_in.at[core, h, y, k], a_send.at[0, h], a_recv.at[k, h], (wide, buddy)
                ).wait_recv()

            return carry

        lax.fori_loop(0, 8, wait_row, 0)
        for direction in range(2):
            ring_copy(h, direction, y).start()
        forward(h, y, core).start()

    for h in (1, 0):
        ring_copy(h, h, behind[h]).wait_recv()
        on_copy(h, behind[h]).start()
        forward(h, behind[h], core).start()

    for copy in fetches:
        copy.wait()

    def product(side_core, h):
        rows = jnp.concatenate([rows_in[side_core, h, :, k].reshape(HALF, HD) for k in range(KVH)], axis=1)
        return jnp.dot(
            rows, w_in[side_core * 2 + h].reshape(KVH * HD, 512), preferred_element_type=jnp.float32
        )

    total = jnp.zeros((HALF, 512), jnp.float32)
    for h in (1, 0):
        ring_copy(h, 1 - h, behind[1 - h]).wait_recv()
        forward(h, behind[1 - h], core).start()
        on_copy(h, (y + 2) % NY).wait_recv()
        forward(h, (y + 2) % NY, core).start()
        total = total + product(core, h)
    for h in (1, 0):
        for piece in range(NY):
            forward(h, piece, 1 - core).wait_recv()
        total = total + product(1 - core, h)
    result[...] = total.astype(jnp.bfloat16)

    for copy in (*x_copies, *ym_copies):
        copy.wait_send()
    for step in range(1, NY):
        for copy in (*y_copies(step), *xm_copies(step)):
            copy.wait_send()
    for h in range(2):
        def drain_row(i, carry):
            @pl.when(jnp.logical_not(local(i)))
            def _():
                row_copy(i, h).wait_send()

            return carry

        lax.fori_loop(0, 8, drain_row, 0)
        for direction in range(2):
            ring_copy(h, direction, y).wait_send()
        on_copy(h, behind[h]).wait_send()
        for piece in range(NY):
            forward(h, piece, core).wait_send()


def finish(part, lse, weight):
    anywhere = pl.BlockSpec(memory_space=pl.ANY)
    dma = pltpu.SemaphoreType.DMA
    return pl.pallas_call(
        finish_kernel,
        out_shape=jax.ShapeDtypeStruct((HALF, 512), jnp.bfloat16),
        in_specs=[anywhere] * 3,
        out_specs=pl.BlockSpec(memory_space=pltpu.VMEM),
        scratch_shapes=[
            pltpu.VMEM((2, 8, NY, PIECE, HD), jnp.bfloat16),
            pltpu.VMEM((NY, 16, PIECE, HD), jnp.bfloat16),
            pltpu.VMEM((NY, 8, PIECE, HD), jnp.bfloat16),
            pltpu.VMEM((2, 8, PIECE, HD), jnp.bfloat16),
            pltpu.VMEM((NY, 8, PIECE, HD), jnp.bfloat16),
            pltpu.VMEM((8, PIECE, HD), jnp.bfloat16),
            pltpu.VMEM((2, NY, 8, HD), jnp.float32),
            pltpu.VMEM((NY, 2, 8, HD), jnp.float32),
            pltpu.VMEM((NY, 8, HD), jnp.float32),
            pltpu.VMEM((2, 8, HD), jnp.float32),
            pltpu.VMEM((NY, 8, HD), jnp.float32),
            pltpu.VMEM((8, HD), jnp.float32),
            pltpu.VMEM((4, KVH, HD, 512), jnp.bfloat16),
            pltpu.VMEM((2, 8, PIECE, HD), jnp.bfloat16),
            pltpu.VMEM((2, 2, NY, KVH, PIECE, HD), jnp.bfloat16),
            dma((2,)), dma((2,)), dma((NY, 2)), dma((NY, 2)), dma((NY, 2)), dma((NY, 2)), dma((2,)), dma((2,)),
            dma((8, 2)), dma((8, 2)), dma((2, 2)), dma((2, 2)), dma((2,)), dma((2,)),
            dma((2, NY)), dma((2, NY)), dma((12,)),
        ],
        compiler_params=pltpu.CompilerParams(
            collective_id=1, has_side_effects=True, vmem_limit_bytes=56 * MIB
        ),
    )(part, lse, weight.reshape(KVH, 4, HD, 512))


def shards(queries, span_keys, span_values, cache_keys, cache_values, chosen, out_weight):
    weight = lax.all_gather(out_weight, "wide", axis=0, tiled=True)
    q, k_pair, v_pair, span = spread(queries, span_keys, span_values, cache_keys, cache_values)
    part, lse = attend(chosen.T, q, cache_keys, cache_values, k_pair, v_pair, span)
    return finish(part, lse, weight)


def solution(mesh):
    return jax.shard_map(
        shards,
        mesh=mesh,
        in_specs=(
            P("wide", None),
            P("wide", None),
            P("wide", None),
            P(("wide", "narrow"), None),
            P(("wide", "narrow"), None),
            P(),
            P("wide", "narrow"),
        ),
        out_specs=P("wide", "narrow"),
        check_vma=False,
    )
```

```python
import math

import jax
import jax.numpy as jnp
from jax import lax
from jax.experimental import pallas as pl
from jax.experimental.pallas import tpu as pltpu
from jax.sharding import PartitionSpec as P

HD = 128
QB = 512
KB = 4096
NQB = 8
NW = 16
KVH = 8
HALF = 256
ROWS = 2 * QB
NY = 4
PIECE = HALF // NY
CHUNK = 256
FLOOR_SCORE = -1e30
SCALE2 = math.log2(math.e) / math.sqrt(HD)
MESH = pl.DeviceIdType.MESH
MIB = 2**20


def place():
    wide = lax.axis_index("wide")
    narrow = lax.axis_index("narrow")
    return wide, narrow, narrow // 2, narrow % 2


def remote(src, dst, send_sem, recv_sem, device):
    return pltpu.make_async_remote_copy(
        src_ref=src, dst_ref=dst, send_sem=send_sem, recv_sem=recv_sem, device_id=device, device_id_type=MESH
    )


def spread_kernel(
    queries, span_k, span_v, cache_k, cache_v,
    q_out, pk_out, pv_out, s_out,
    s_in, q_send, q_recv, ring_send, ring_recv, pass_send, pass_recv,
    kv_send, kv_recv, s_send, s_recv, turn_send, turn_recv, share_send, share_recv, local_sem,
):
    wide, narrow, y, core = place()
    buddy = y * 2 + 1 - core
    z, x, side = wide // 4, wide % 4, wide % 2
    ring = [(y + 1) % NY, (y + NY - 1) % NY]
    behind = ring[::-1]
    barrier = pltpu.get_barrier_semaphore()

    def greet(step, carry):
        pl.semaphore_signal(
            barrier, inc=1, device_id=((wide + step) % NW, narrow), device_id_type=MESH
        )
        return carry

    lax.fori_loop(1, NW, greet, 0)
    for neighbour in (buddy, *((y + step) % NY * 2 + core for step in range(1, NY))):
        pl.semaphore_signal(barrier, inc=1, device_id=(wide, neighbour), device_id_type=MESH)
    pl.semaphore_wait(barrier, NW + 3)

    tokens = pl.ds(pl.multiple_of(y * PIECE, PIECE), PIECE)

    def columns(kv):
        return pl.ds(pl.multiple_of(kv * 512 + core * 256, 256), 256)

    def q_copy(dz, dx):
        target = (z + dz) % 4 * 4 + (x + dx) % 4
        rows = tokens if dz else slice(None)
        return remote(
            queries.at[rows, columns(target // 2)], q_out.at[wide, rows],
            q_send.at[dz * 4 + dx], q_recv.at[wide], (target, narrow),
        )

    def q_wait(source, rows):
        remote(
            queries.at[rows, columns(0)], q_out.at[source, rows], q_send.at[1], q_recv.at[source], (source, narrow)
        ).wait_recv()

    steps = [(dz, dx) for dz in (1, 3, 2, 0) for dx in (0, 1, 3, 2) if dz or dx]
    own_q = pltpu.make_async_copy(queries.at[:, columns(wide // 2)], q_out.at[wide], local_sem.at[0])

    s_home = wide // 8
    own_s = s_home == side

    def s_src(which, kv):
        return (span_k, span_v)[which].at[tokens, pl.ds(pl.multiple_of(kv * HD, HD), HD)]

    def s_copy(which, kv):
        return remote(
            s_src(which, kv), s_in.at[wide % 8], s_send.at[kv], s_recv.at[wide % 8], (kv * 2 + s_home, narrow)
        )

    def s_local(which):
        return pltpu.make_async_copy(s_src(which, wide // 2), s_in.at[wide % 8], local_sem.at[1])

    def s_start(kv, carry):
        away = jnp.logical_not(own_s & (kv == wide // 2))
        for which in range(2):
            @pl.when((core == which) & away)
            def _():
                s_copy(which, kv).start()

            @pl.when((core == which) & jnp.logical_not(away))
            def _():
                s_local(which).start()

        return carry

    for dz, dx in steps[:8]:
        q_copy(dz, dx).start()
    lax.fori_loop(0, KVH, s_start, 0)
    for dz, dx in steps[8:]:
        q_copy(dz, dx).start()
    own_q.start()
    kv_copies = [
        remote(src, dst, kv_send.at[i], kv_recv.at[i], (wide, buddy))
        for i, (src, dst) in enumerate(((cache_k, pk_out), (cache_v, pv_out)))
    ]
    for copy in kv_copies:
        copy.start()

    def piece_rows(piece):
        return pl.ds(pl.multiple_of(piece * PIECE, PIECE), PIECE)

    def ring_copy(group, direction, piece):
        batch = q_out.at[pl.ds(group * 4, 4), piece_rows(piece)]
        return remote(
            batch, batch, ring_send.at[group, direction], ring_recv.at[group, direction],
            (wide, ring[direction] * 2 + core),
        )

    def pass_copy(group, direction, piece):
        batch = q_out.at[pl.ds(group * 4 + direction * 2, 2), piece_rows(piece)]
        return remote(
            batch, batch, pass_send.at[group, direction], pass_recv.at[group, direction],
            (wide, ring[direction] * 2 + core),
        )

    groups = [(z + step) % 4 for step in (3, 1, 2)]
    for group in groups:
        for i in range(4):
            q_wait(group * 4 + i, tokens)
        for direction in range(2):
            ring_copy(group, direction, y).start()

    def s_wait(i, carry):
        mine = own_s & (i == wide % 8)

        @pl.when(mine)
        def _():
            s_local(0).wait()

        @pl.when(jnp.logical_not(mine))
        def _():
            remote(s_src(0, 0), s_in.at[i], s_send.at[0], s_recv.at[i], (wide, buddy)).wait_recv()

        return carry

    lax.fori_loop(0, 8, s_wait, 0)

    def turn_copy(step):
        to = (y + step) % NY
        return remote(
            s_in.at[pl.ds(to * 2, 2)], s_out.at[core, :, y], turn_send.at[step], turn_recv.at[y],
            (wide, to * 2 + core),
        )

    keep = pltpu.make_async_copy(s_in.at[pl.ds(y * 2, 2)], s_out.at[core, :, y], local_sem.at[2])
    keep.start()
    for step in range(1, NY):
        turn_copy(step).start()

    for group in groups:
        for direction in range(2):
            ring_copy(group, direction, behind[direction]).wait_recv()
            pass_copy(group, direction, behind[direction]).start()

    keep.wait()
    for step in range(1, NY):
        origin = (y + step) % NY
        remote(
            s_in.at[pl.ds(0, 2)], s_out.at[core, :, origin], turn_send.at[step], turn_recv.at[origin], (wide, buddy)
        ).wait_recv()
    share = remote(s_out.at[core], s_out.at[core], share_send.at[0], share_recv.at[core], (wide, buddy))
    share.start()

    for group in groups:
        for direction in range(2):
            pass_copy(group, direction, (y + 2) % NY).wait_recv()
    remote(s_out.at[core], s_out.at[1 - core], share_send.at[0], share_recv.at[1 - core], (wide, buddy)).wait_recv()
    own_q.wait()
    for dx in range(1, 4):
        q_wait(z * 4 + (x + dx) % 4, slice(None))
    for copy in kv_copies:
        copy.wait()
    share.wait_send()
    for group in groups:
        for direction in range(2):
            ring_copy(group, direction, y).wait_send()
            pass_copy(group, direction, behind[direction]).wait_send()
    for step in range(1, NY):
        turn_copy(step).wait_send()
    for dz, dx in steps:
        q_copy(dz, dx).wait_send()

    def s_drain(kv, carry):
        @pl.when(jnp.logical_not(own_s & (kv == wide // 2)))
        def _():
            s_copy(0, kv).wait_send()

        return carry

    lax.fori_loop(0, KVH, s_drain, 0)


def spread(queries, span_k, span_v, cache_k, cache_v):
    anywhere = pl.BlockSpec(memory_space=pl.ANY)
    shape = lambda *dims: jax.ShapeDtypeStruct(dims, jnp.bfloat16)
    dma = pltpu.SemaphoreType.DMA
    return pl.pallas_call(
        spread_kernel,
        out_shape=[shape(NW, HALF, 2 * HD), shape(KB, HD), shape(KB, HD), shape(2, 2, NY, PIECE, HD)],
        in_specs=[anywhere] * 5,
        out_specs=[anywhere] * 4,
        scratch_shapes=[
            pltpu.VMEM((8, PIECE, HD), jnp.bfloat16),
            dma((NW,)), dma((NW,)), dma((4, 2)), dma((4, 2)), dma((4, 2)), dma((4, 2)),
            dma((2,)), dma((2,)), dma((KVH,)), dma((8,)), dma((NY,)), dma((NY,)), dma((1,)), dma((2,)), dma((3,)),
        ],
        compiler_params=pltpu.CompilerParams(
            collective_id=0, has_side_effects=True, vmem_limit_bytes=56 * MIB
        ),
    )(queries, span_k, span_v, cache_k, cache_v)


def attend_kernel(
    chosen, q, k_own, v_own, k_pair, v_pair, span, out, lse,
    q_in, k_both, v_wide, sk_in, s_wide, out_in, lse_in, acc, peak, sems, out_sem,
):
    wide, narrow, y, core = place()
    held = wide % 2 * 4 + y
    first = wide % 2 * 8 + y * 2
    moves = [
        (q, q_in),
        (span.at[0], sk_in),
        (span.at[1], s_wide.at[:, :, :, :HD]),
        (k_own, k_both.at[0]),
        (v_own, v_wide.at[0, :, :HD]),
        (k_pair, k_both.at[1]),
        (v_pair, v_wide.at[1, :, :HD]),
    ]
    loads = [pltpu.make_async_copy(src, dst, sems.at[i]) for i, (src, dst) in enumerate(moves)]
    for copy in loads:
        copy.start()
    s_wide[:, :, :, HD:] = jnp.ones((2, NY, PIECE, HD), jnp.bfloat16)
    lse_in[...] = jnp.full((2, NY, 2, 8, HD), FLOOR_SCORE, jnp.float32)
    for i in range(2):
        v_wide[i, :, HD:] = jnp.ones((KB, HD), jnp.bfloat16)

    def fold(state, queries, keys, values, mask):
        top, total = state
        scores = lax.dot_general(queries, keys, (((1,), (1,)), ((), ())), preferred_element_type=jnp.float32)
        if mask is not None:
            scores = jnp.where(mask, scores, FLOOR_SCORE)
        new_top = jnp.maximum(top, jnp.max(scores, axis=1, keepdims=True))
        decay = jnp.exp2((top - new_top) * SCALE2)
        weights = jnp.exp2((scores - new_top) * SCALE2).astype(jnp.bfloat16)
        total = total * decay + jnp.dot(weights, values, preferred_element_type=jnp.float32)
        return new_top, total

    def block_queries(b):
        rows = q_in[pl.ds(b * 2, 2)].reshape(QB, 2 * HD)
        return jnp.concatenate([rows[:, :HD], rows[:, HD:]], axis=0)

    def load():
        return jnp.max(peak[...], axis=1, keepdims=True), acc[...]

    def save(state):
        peak[...] = jnp.broadcast_to(state[0], (ROWS, HD))
        acc[...] = state[1]

    for copy in loads[:3]:
        copy.wait()
    row = lax.broadcasted_iota(jnp.int32, (ROWS, QB), 0) % QB
    mask = row >= lax.broadcasted_iota(jnp.int32, (ROWS, QB), 1)
    fresh = jnp.full((ROWS, 1), FLOOR_SCORE, jnp.float32), jnp.zeros((ROWS, 2 * HD), jnp.float32)
    save(fold(fresh, block_queries(held), sk_in[...].reshape(QB, HD), s_wide[...].reshape(QB, 2 * HD), mask))
    for copy in loads[3:]:
        copy.wait()

    def send_out(b):
        return pltpu.make_async_copy(
            out_in.at[:, pl.ds(b * 2, 2)], out.at[:, pl.ds(b * 2, 2)], out_sem.at[b]
        )

    def one_block(step, carry):
        b = (held + step) % NQB
        hits = []
        for i in range(2):
            c = first + jnp.where(core == 0, i, 1 - i)
            hits.append((chosen[0, b] == c) | (chosen[1, b] == c) | (chosen[2, b] == c))
        used = hits[0] | hits[1] | (step == 0)

        @pl.when(used & (step != 0))
        def _():
            acc[...] = jnp.zeros((ROWS, 2 * HD), jnp.float32)
            peak[...] = jnp.full((ROWS, HD), FLOOR_SCORE, jnp.float32)

        def cached(i, carry):
            @pl.when(jnp.where(i == 0, hits[0], hits[1]))
            def _():
                queries = block_queries(b)
                state = load()
                for start in range(0, KB, CHUNK):
                    state = fold(
                        state, queries, k_both[i, start:start + CHUNK, :], v_wide[i, start:start + CHUNK, :], None
                    )
                save(state)

            return carry

        lax.fori_loop(0, 2, cached, 0)

        @pl.when(used)
        def _():
            total = acc[:, HD:]
            out_in[:, pl.ds(b * 2, 2)] = (
                (acc[:, :HD] / total).astype(jnp.bfloat16).reshape(2, 2, NY, PIECE, HD)
            )
            logs = peak[...] * SCALE2 + jnp.log2(total)
            eye = lax.broadcasted_iota(jnp.int32, (PIECE, HD), 0) == lax.broadcasted_iota(
                jnp.int32, (PIECE, HD), 1
            )
            for piece in range(NY):
                for part in range(4):
                    start = part * HALF + piece * PIECE
                    lse_in[part // 2, piece, b // 4, pl.ds(b % 4 * 2 + part % 2, 1), :] = jnp.sum(
                        jnp.where(eye, logs[start:start + PIECE], 0.0), axis=0, keepdims=True
                    )

        @pl.when(jnp.logical_not(used))
        def _():
            out_in[:, pl.ds(b * 2, 2)] = jnp.zeros((2, 2, NY, PIECE, HD), jnp.bfloat16)

        send_out(b).start()
        return carry

    lax.fori_loop(0, NQB, one_block, 0)
    lse_copy = pltpu.make_async_copy(lse_in, lse, sems.at[7])
    lse_copy.start()
    for b in range(NQB):
        send_out(b).wait()
    lse_copy.wait()


def attend(chosen, q, k_own, v_own, k_pair, v_pair, span):
    anywhere = pl.BlockSpec(memory_space=pl.ANY)
    dma = pltpu.SemaphoreType.DMA
    return pl.pallas_call(
        attend_kernel,
        out_shape=[
            jax.ShapeDtypeStruct((2, NW, NY, PIECE, HD), jnp.bfloat16),
            jax.ShapeDtypeStruct((2, NY, 2, 8, HD), jnp.float32),
        ],
        in_specs=[pl.BlockSpec(memory_space=pltpu.SMEM)] + [anywhere] * 6,
        out_specs=[anywhere] * 2,
        scratch_shapes=[
            pltpu.VMEM((NW, HALF, 2 * HD), jnp.bfloat16),
            pltpu.VMEM((2, KB, HD), jnp.bfloat16),
            pltpu.VMEM((2, KB, 2 * HD), jnp.bfloat16),
            pltpu.VMEM((2, NY, PIECE, HD), jnp.bfloat16),
            pltpu.VMEM((2, NY, PIECE, 2 * HD), jnp.bfloat16),
            pltpu.VMEM((2, NW, NY, PIECE, HD), jnp.bfloat16),
            pltpu.VMEM((2, NY, 2, 8, HD), jnp.float32),
            pltpu.VMEM((ROWS, 2 * HD), jnp.float32),
            pltpu.VMEM((ROWS, HD), jnp.float32),
            dma((8,)), dma((NQB,)),
        ],
        compiler_params=pltpu.CompilerParams(vmem_limit_bytes=56 * MIB),
        cost_estimate=pl.CostEstimate(flops=14 * 10**9, bytes_accessed=10 * MIB, transcendentals=25 * 10**6),
    )(chosen, q, k_own, v_own, k_pair, v_pair, span)


def finish_kernel(
    part, lse, weight, result,
    x_in, y_in, x_mid, y_mid, x_last, y_last, lx_in, ly_in, lx_mid, ly_mid, lx_last, ly_last,
    w_in, rows_out, rows_in,
    x_send, x_recv, y_send, y_recv, xm_send, xm_recv, ym_send, ym_recv,
    a_send, a_recv, f_send, f_recv, local_sem,
):
    wide, narrow, y, core = place()
    buddy = y * 2 + 1 - core
    kv, side = wide // 2, wide % 2
    own_target = wide // 8 == side
    barrier = pltpu.get_barrier_semaphore()

    across = wide + 1 - side * 2, narrow

    def along(step):
        return wide, (y + step) % NY * 2 + core

    fetches = [pltpu.make_async_copy(weight.at[:, i], w_in.at[i], local_sem.at[i]) for i in range(4)]
    keep = [
        pltpu.make_async_copy(part.at[0, pl.ds(side * 8, 8)], x_in.at[0], local_sem.at[4]),
        pltpu.make_async_copy(lse.at[0, :, side], lx_in.at[0], local_sem.at[5]),
        pltpu.make_async_copy(part.at[1, :, y], y_in.at[y], local_sem.at[6]),
        pltpu.make_async_copy(lse.at[1, y], ly_in.at[y], local_sem.at[9]),
    ]
    for copy in (*keep, *fetches):
        copy.start()
    for device in (across, *(along(step) for step in range(1, NY))):
        pl.semaphore_signal(barrier, inc=1, device_id=device, device_id_type=MESH)

    def greet_source(n, carry):
        s, step = n // NY, n % NY

        @pl.when(jnp.logical_not(own_target & (s == kv) & (step == 0)))
        def _():
            pl.semaphore_signal(
                barrier, inc=1, device_id=(s * 2 + wide // 8, (y + step) % NY * 2 + core), device_id_type=MESH
            )

        return carry

    lax.fori_loop(0, 8 * NY, greet_source, 0)
    pl.semaphore_signal(barrier, inc=1, device_id=(wide, buddy), device_id_type=MESH)
    pl.semaphore_wait(barrier, 37 - own_target.astype(jnp.int32))

    x_copies = [
        remote(part.at[0, pl.ds((1 - side) * 8, 8)], x_in.at[1], x_send.at[0], x_recv.at[0], across),
        remote(lse.at[0, :, 1 - side], lx_in.at[1], x_send.at[1], x_recv.at[1], across),
    ]

    def y_copies(step):
        to = (y + step) % NY
        return [
            remote(part.at[1, :, to], y_in.at[y], y_send.at[step, 0], y_recv.at[y, 0], along(step)),
            remote(lse.at[1, to], ly_in.at[y], y_send.at[step, 1], y_recv.at[y, 1], along(step)),
        ]

    def y_arrivals(step):
        origin = (y + step) % NY
        return [
            remote(part.at[1, :, 0], y_in.at[origin], y_send.at[step, 0], y_recv.at[origin, 0], across),
            remote(lse.at[1, 0], ly_in.at[origin], y_send.at[step, 1], y_recv.at[origin, 1], across),
        ]

    def xm_copies(step):
        to = (y + step) % NY
        return [
            remote(x_mid.at[to], x_last.at[y], xm_send.at[step, 0], xm_recv.at[y, 0], along(step)),
            remote(lx_mid.at[to], lx_last.at[y], xm_send.at[step, 1], xm_recv.at[y, 1], along(step)),
        ]

    def xm_arrivals(step):
        origin = (y + step) % NY
        return [
            remote(x_mid.at[0], x_last.at[origin], xm_send.at[step, 0], xm_recv.at[origin, 0], across),
            remote(lx_mid.at[0], lx_last.at[origin], xm_send.at[step, 1], xm_recv.at[origin, 1], across),
        ]

    ym_copies = [
        remote(y_mid.at[1 - side], y_last, ym_send.at[0], ym_recv.at[0], across),
        remote(ly_mid.at[1 - side], ly_last, ym_send.at[1], ym_recv.at[1], across),
    ]

    for copy in x_copies:
        copy.start()
    for step in (1, 3, 2):
        for copy in y_copies(step):
            copy.start()

    def weigh(logs):
        top = jnp.max(logs, axis=0)
        shares = jnp.exp2(logs - top[None])
        total = jnp.sum(shares, axis=0)
        shares = (shares / total[None]).reshape(-1, HD)
        turned = jnp.transpose(jnp.concatenate([shares] * (HD // shares.shape[0]), axis=0))
        return turned[:PIECE], top + jnp.log2(total)

    def mix(turned, columns, pieces):
        total = jnp.zeros((PIECE, HD), jnp.float32)
        for column, piece in zip(columns, pieces):
            total = total + piece.astype(jnp.float32) * turned[:, column:column + 1]
        return total.astype(jnp.bfloat16)

    for copy in keep:
        copy.wait()
    for copy in x_copies:
        copy.wait_recv()
    turned, logs = weigh(lx_in[...].reshape(2, NY * 8, HD))
    lx_mid[...] = logs.reshape(NY, 8, HD)
    for piece in range(NY):
        for i in range(8):
            column = piece * 8 + i
            x_mid[piece, i] = mix(turned, (column, 32 + column), (x_in[0, i, piece], x_in[1, i, piece]))
    x_keep = [
        pltpu.make_async_copy(x_mid.at[y], x_last.at[y], local_sem.at[10]),
        pltpu.make_async_copy(lx_mid.at[y], lx_last.at[y], local_sem.at[11]),
    ]
    for copy in x_keep:
        copy.start()
    for step in (1, 3, 2):
        for copy in xm_copies(step):
            copy.start()

    for step in (1, 3, 2):
        for copy in y_arrivals(step):
            copy.wait_recv()
    turned, logs = weigh(ly_in[...].reshape(NY, 16, HD))
    ly_mid[...] = logs.reshape(2, 8, HD)
    for i in range(16):
        y_mid[i // 8, i % 8] = mix(turned, [s * 16 + i for s in range(NY)], [y_in[s, i] for s in range(NY)])
    for copy in ym_copies:
        copy.start()

    def row_copy(n, h):
        i, step = n // NY, n % NY
        return remote(
            rows_out.at[h, i], rows_in.at[core, h, y, kv], a_send.at[n, h], a_recv.at[y, kv, h],
            (side * 8 + i, (y + step) % NY * 2 + core),
        )

    def own_copy(h):
        return pltpu.make_async_copy(rows_out.at[h, wide % 8], rows_in.at[core, h, y, kv], local_sem.at[7 + h])

    def local(n):
        return own_target & (n == wide % 8 * NY)

    for h in (1, 0):
        if h == 0:
            for copy in x_keep:
                copy.wait()
            for step in (1, 3, 2):
                for copy in xm_arrivals(step):
                    copy.wait_recv()
            turned, logs = weigh(lx_last[...])
            for i in range(8):
                rows_out[h, i] = mix(turned, [s * 8 + i for s in range(NY)], [x_last[s, i] for s in range(NY)])
        else:
            for copy in ym_copies:
                copy.wait_recv()
            turned, logs = weigh(jnp.stack([ly_mid[side], ly_last[...]]))
            for i in range(8):
                rows_out[h, i] = mix(turned, (i, 8 + i), (y_mid[side, i], y_last[i]))

        def start_row(i, carry):
            @pl.when(local(i))
            def _():
                own_copy(h).start()

            @pl.when(jnp.logical_not(local(i)))
            def _():
                row_copy(i, h).start()

            return carry

        lax.fori_loop(0, 8 * NY, start_row, 0)

    def batch(side_core, h, piece):
        return rows_in.at[side_core, h, piece]

    def forward(h, piece, side_core):
        return remote(
            batch(side_core, h, piece), batch(side_core, h, piece),
            f_send.at[h, piece], f_recv.at[h, piece], (wide, buddy),
        )

    for copy in fetches:
        copy.wait()

    def product(side_core, h):
        rows = jnp.concatenate([rows_in[side_core, h, :, k].reshape(HALF, HD) for k in range(KVH)], axis=1)
        return jnp.dot(
            rows, w_in[side_core * 2 + h].reshape(KVH * HD, 512), preferred_element_type=jnp.float32
        )

    total = jnp.zeros((HALF, 512), jnp.float32)
    for h in (1, 0):
        for step in (0, 1, 3, 2):
            piece = (y + step) % NY

            def wait_row(k, carry):
                mine = own_target & (k == kv) & (step == 0)

                @pl.when(mine)
                def _():
                    own_copy(h).wait()

                @pl.when(jnp.logical_not(mine))
                def _():
                    remote(
                        rows_out.at[h, 0], rows_in.at[core, h, piece, k],
                        a_send.at[0, h], a_recv.at[piece, k, h], (wide, buddy),
                    ).wait_recv()

                return carry

            lax.fori_loop(0, 8, wait_row, 0)
            forward(h, piece, core).start()
        total = total + product(core, h)
    for h in (1, 0):
        for piece in range(NY):
            forward(h, piece, 1 - core).wait_recv()
        total = total + product(1 - core, h)
    result[...] = total.astype(jnp.bfloat16)

    for copy in (*x_copies, *ym_copies):
        copy.wait_send()
    for step in range(1, NY):
        for copy in (*y_copies(step), *xm_copies(step)):
            copy.wait_send()
    for h in range(2):
        def drain_row(i, carry):
            @pl.when(jnp.logical_not(local(i)))
            def _():
                row_copy(i, h).wait_send()

            return carry

        lax.fori_loop(0, 8 * NY, drain_row, 0)
        for piece in range(NY):
            forward(h, piece, core).wait_send()


def finish(part, lse, weight):
    anywhere = pl.BlockSpec(memory_space=pl.ANY)
    dma = pltpu.SemaphoreType.DMA
    return pl.pallas_call(
        finish_kernel,
        out_shape=jax.ShapeDtypeStruct((HALF, 512), jnp.bfloat16),
        in_specs=[anywhere] * 3,
        out_specs=pl.BlockSpec(memory_space=pltpu.VMEM),
        scratch_shapes=[
            pltpu.VMEM((2, 8, NY, PIECE, HD), jnp.bfloat16),
            pltpu.VMEM((NY, 16, PIECE, HD), jnp.bfloat16),
            pltpu.VMEM((NY, 8, PIECE, HD), jnp.bfloat16),
            pltpu.VMEM((2, 8, PIECE, HD), jnp.bfloat16),
            pltpu.VMEM((NY, 8, PIECE, HD), jnp.bfloat16),
            pltpu.VMEM((8, PIECE, HD), jnp.bfloat16),
            pltpu.VMEM((2, NY, 8, HD), jnp.float32),
            pltpu.VMEM((NY, 2, 8, HD), jnp.float32),
            pltpu.VMEM((NY, 8, HD), jnp.float32),
            pltpu.VMEM((2, 8, HD), jnp.float32),
            pltpu.VMEM((NY, 8, HD), jnp.float32),
            pltpu.VMEM((8, HD), jnp.float32),
            pltpu.VMEM((4, KVH, HD, 512), jnp.bfloat16),
            pltpu.VMEM((2, 8, PIECE, HD), jnp.bfloat16),
            pltpu.VMEM((2, 2, NY, KVH, PIECE, HD), jnp.bfloat16),
            dma((2,)), dma((2,)), dma((NY, 2)), dma((NY, 2)), dma((NY, 2)), dma((NY, 2)), dma((2,)), dma((2,)),
            dma((8 * NY, 2)), dma((NY, KVH, 2)),
            dma((2, NY)), dma((2, NY)), dma((12,)),
        ],
        compiler_params=pltpu.CompilerParams(
            collective_id=1, has_side_effects=True, vmem_limit_bytes=56 * MIB
        ),
    )(part, lse, weight.reshape(KVH, 4, HD, 512))


def shards(queries, span_keys, span_values, cache_keys, cache_values, chosen, out_weight):
    weight = lax.all_gather(out_weight, "wide", axis=0, tiled=True)
    q, k_pair, v_pair, span = spread(queries, span_keys, span_values, cache_keys, cache_values)
    part, lse = attend(chosen.T, q, cache_keys, cache_values, k_pair, v_pair, span)
    return finish(part, lse, weight)


def solution(mesh):
    return jax.shard_map(
        shards,
        mesh=mesh,
        in_specs=(
            P("wide", None),
            P("wide", None),
            P("wide", None),
            P(("wide", "narrow"), None),
            P(("wide", "narrow"), None),
            P(),
            P("wide", "narrow"),
        ),
        out_specs=P("wide", "narrow"),
        check_vma=False,
    )
```

```python
import math

import jax
import jax.numpy as jnp
from jax import lax
from jax.experimental import pallas as pl
from jax.experimental.pallas import tpu as pltpu
from jax.sharding import PartitionSpec as P

HD = 128
QB = 512
KB = 4096
NQB = 8
NW = 16
KVH = 8
HALF = 256
ROWS = 2 * QB
NY = 4
PIECE = HALF // NY
CHUNK = 256
FLOOR_SCORE = -1e30
SCALE2 = math.log2(math.e) / math.sqrt(HD)
MESH = pl.DeviceIdType.MESH
MIB = 2**20


def place():
    wide = lax.axis_index("wide")
    narrow = lax.axis_index("narrow")
    return wide, narrow, narrow // 2, narrow % 2


def remote(src, dst, send_sem, recv_sem, device):
    return pltpu.make_async_remote_copy(
        src_ref=src, dst_ref=dst, send_sem=send_sem, recv_sem=recv_sem, device_id=device, device_id_type=MESH
    )


def spread_kernel(
    queries, span_k, span_v, cache_k, cache_v,
    q_out, pk_out, pv_out, s_out,
    s_in, q_send, q_recv, ring_send, ring_recv, pass_send, pass_recv,
    kv_send, kv_recv, s_send, s_recv, turn_send, turn_recv, share_send, share_recv, local_sem,
):
    wide, narrow, y, core = place()
    buddy = y * 2 + 1 - core
    z, x, side = wide // 4, wide % 4, wide % 2
    ring = [(y + 1) % NY, (y + NY - 1) % NY]
    behind = ring[::-1]
    barrier = pltpu.get_barrier_semaphore()

    def greet(step, carry):
        pl.semaphore_signal(
            barrier, inc=1, device_id=((wide + step) % NW, narrow), device_id_type=MESH
        )
        return carry

    lax.fori_loop(1, NW, greet, 0)
    for neighbour in (buddy, *((y + step) % NY * 2 + core for step in range(1, NY))):
        pl.semaphore_signal(barrier, inc=1, device_id=(wide, neighbour), device_id_type=MESH)
    pl.semaphore_wait(barrier, NW + 3)

    tokens = pl.ds(pl.multiple_of(y * PIECE, PIECE), PIECE)

    def columns(kv):
        return pl.ds(pl.multiple_of(kv * 512 + core * 256, 256), 256)

    def q_copy(dz, dx):
        target = (z + dz) % 4 * 4 + (x + dx) % 4
        rows = tokens if dz else slice(None)
        return remote(
            queries.at[rows, columns(target // 2)], q_out.at[wide, rows],
            q_send.at[dz * 4 + dx], q_recv.at[wide], (target, narrow),
        )

    def q_wait(source, rows):
        remote(
            queries.at[rows, columns(0)], q_out.at[source, rows], q_send.at[1], q_recv.at[source], (source, narrow)
        ).wait_recv()

    steps = [(dz, dx) for dz in (1, 3, 2, 0) for dx in (0, 1, 3, 2) if dz or dx]
    own_q = pltpu.make_async_copy(queries.at[:, columns(wide // 2)], q_out.at[wide], local_sem.at[0])

    s_home = wide // 8
    own_s = s_home == side

    def s_src(which, kv):
        return (span_k, span_v)[which].at[tokens, pl.ds(pl.multiple_of(kv * HD, HD), HD)]

    def s_copy(which, kv):
        return remote(
            s_src(which, kv), s_in.at[wide % 8], s_send.at[kv], s_recv.at[wide % 8], (kv * 2 + s_home, narrow)
        )

    def s_local(which):
        return pltpu.make_async_copy(s_src(which, wide // 2), s_in.at[wide % 8], local_sem.at[1])

    def s_start(kv, carry):
        away = jnp.logical_not(own_s & (kv == wide // 2))
        for which in range(2):
            @pl.when((core == which) & away)
            def _():
                s_copy(which, kv).start()

            @pl.when((core == which) & jnp.logical_not(away))
            def _():
                s_local(which).start()

        return carry

    for dz, dx in steps[:8]:
        q_copy(dz, dx).start()
    lax.fori_loop(0, KVH, s_start, 0)
    for dz, dx in steps[8:]:
        q_copy(dz, dx).start()
    own_q.start()
    kv_copies = [
        remote(src, dst, kv_send.at[i], kv_recv.at[i], (wide, buddy))
        for i, (src, dst) in enumerate(((cache_k, pk_out), (cache_v, pv_out)))
    ]
    for copy in kv_copies:
        copy.start()

    def piece_rows(piece):
        return pl.ds(pl.multiple_of(piece * PIECE, PIECE), PIECE)

    def ring_copy(group, direction, piece):
        batch = q_out.at[pl.ds(group * 4, 4), piece_rows(piece)]
        return remote(
            batch, batch, ring_send.at[group, direction], ring_recv.at[group, direction],
            (wide, ring[direction] * 2 + core),
        )

    def pass_copy(group, direction, piece):
        batch = q_out.at[pl.ds(group * 4 + direction * 2, 2), piece_rows(piece)]
        return remote(
            batch, batch, pass_send.at[group, direction], pass_recv.at[group, direction],
            (wide, ring[direction] * 2 + core),
        )

    groups = [(z + step) % 4 for step in (3, 1, 2)]
    for group in groups:
        for i in range(4):
            q_wait(group * 4 + i, tokens)
        for direction in range(2):
            ring_copy(group, direction, y).start()

    def s_wait(i, carry):
        mine = own_s & (i == wide % 8)

        @pl.when(mine)
        def _():
            s_local(0).wait()

        @pl.when(jnp.logical_not(mine))
        def _():
            remote(s_src(0, 0), s_in.at[i], s_send.at[0], s_recv.at[i], (wide, buddy)).wait_recv()

        return carry

    lax.fori_loop(0, 8, s_wait, 0)

    def turn_copy(step):
        to = (y + step) % NY
        return remote(
            s_in.at[pl.ds(to * 2, 2)], s_out.at[core, :, y], turn_send.at[step], turn_recv.at[y],
            (wide, to * 2 + core),
        )

    keep = pltpu.make_async_copy(s_in.at[pl.ds(y * 2, 2)], s_out.at[core, :, y], local_sem.at[2])
    keep.start()
    for step in range(1, NY):
        turn_copy(step).start()

    for group in groups:
        for direction in range(2):
            ring_copy(group, direction, behind[direction]).wait_recv()
            pass_copy(group, direction, behind[direction]).start()

    keep.wait()
    for step in range(1, NY):
        origin = (y + step) % NY
        remote(
            s_in.at[pl.ds(0, 2)], s_out.at[core, :, origin], turn_send.at[step], turn_recv.at[origin], (wide, buddy)
        ).wait_recv()
    share = remote(s_out.at[core], s_out.at[core], share_send.at[0], share_recv.at[core], (wide, buddy))
    share.start()

    for group in groups:
        for direction in range(2):
            pass_copy(group, direction, (y + 2) % NY).wait_recv()
    remote(s_out.at[core], s_out.at[1 - core], share_send.at[0], share_recv.at[1 - core], (wide, buddy)).wait_recv()
    own_q.wait()
    for dx in range(1, 4):
        q_wait(z * 4 + (x + dx) % 4, slice(None))
    for copy in kv_copies:
        copy.wait()
    share.wait_send()
    for group in groups:
        for direction in range(2):
            ring_copy(group, direction, y).wait_send()
            pass_copy(group, direction, behind[direction]).wait_send()
    for step in range(1, NY):
        turn_copy(step).wait_send()
    for dz, dx in steps:
        q_copy(dz, dx).wait_send()

    def s_drain(kv, carry):
        @pl.when(jnp.logical_not(own_s & (kv == wide // 2)))
        def _():
            s_copy(0, kv).wait_send()

        return carry

    lax.fori_loop(0, KVH, s_drain, 0)


def spread(queries, span_k, span_v, cache_k, cache_v):
    anywhere = pl.BlockSpec(memory_space=pl.ANY)
    shape = lambda *dims: jax.ShapeDtypeStruct(dims, jnp.bfloat16)
    dma = pltpu.SemaphoreType.DMA
    return pl.pallas_call(
        spread_kernel,
        out_shape=[shape(NW, HALF, 2 * HD), shape(KB, HD), shape(KB, HD), shape(2, 2, NY, PIECE, HD)],
        in_specs=[anywhere] * 5,
        out_specs=[anywhere] * 4,
        scratch_shapes=[
            pltpu.VMEM((8, PIECE, HD), jnp.bfloat16),
            dma((NW,)), dma((NW,)), dma((4, 2)), dma((4, 2)), dma((4, 2)), dma((4, 2)),
            dma((2,)), dma((2,)), dma((KVH,)), dma((8,)), dma((NY,)), dma((NY,)), dma((1,)), dma((2,)), dma((3,)),
        ],
        compiler_params=pltpu.CompilerParams(
            collective_id=0, has_side_effects=True, vmem_limit_bytes=56 * MIB
        ),
    )(queries, span_k, span_v, cache_k, cache_v)


def attend_kernel(
    chosen, q, k_own, v_own, k_pair, v_pair, span, out, lse,
    q_in, k_both, v_wide, sk_in, s_wide, out_in, lse_in, acc, peak, sems, out_sem,
):
    wide, narrow, y, core = place()
    held = wide % 2 * 4 + y
    first = wide % 2 * 8 + y * 2
    moves = [
        (q, q_in),
        (span.at[0], sk_in),
        (span.at[1], s_wide.at[:, :, :, :HD]),
        (k_own, k_both.at[0]),
        (v_own, v_wide.at[0, :, :HD]),
        (k_pair, k_both.at[1]),
        (v_pair, v_wide.at[1, :, :HD]),
    ]
    loads = [pltpu.make_async_copy(src, dst, sems.at[i]) for i, (src, dst) in enumerate(moves)]
    for copy in loads:
        copy.start()
    s_wide[:, :, :, HD:] = jnp.ones((2, NY, PIECE, HD), jnp.bfloat16)
    lse_in[...] = jnp.full((2, NY, 2, 8, HD), FLOOR_SCORE, jnp.float32)
    for i in range(2):
        v_wide[i, :, HD:] = jnp.ones((KB, HD), jnp.bfloat16)

    def fold(state, queries, keys, values, mask):
        top, total = state
        scores = lax.dot_general(queries, keys, (((1,), (1,)), ((), ())), preferred_element_type=jnp.float32)
        if mask is not None:
            scores = jnp.where(mask, scores, FLOOR_SCORE)
        new_top = jnp.maximum(top, jnp.max(scores, axis=1, keepdims=True))
        decay = jnp.exp2((top - new_top) * SCALE2)
        weights = jnp.exp2((scores - new_top) * SCALE2).astype(jnp.bfloat16)
        total = total * decay + jnp.dot(weights, values, preferred_element_type=jnp.float32)
        return new_top, total

    def block_queries(b):
        rows = q_in[pl.ds(b * 2, 2)].reshape(QB, 2 * HD)
        return jnp.concatenate([rows[:, :HD], rows[:, HD:]], axis=0)

    def load():
        return jnp.max(peak[...], axis=1, keepdims=True), acc[...]

    def save(state):
        peak[...] = jnp.broadcast_to(state[0], (ROWS, HD))
        acc[...] = state[1]

    for copy in loads[:3]:
        copy.wait()
    row = lax.broadcasted_iota(jnp.int32, (ROWS, QB), 0) % QB
    mask = row >= lax.broadcasted_iota(jnp.int32, (ROWS, QB), 1)
    fresh = jnp.full((ROWS, 1), FLOOR_SCORE, jnp.float32), jnp.zeros((ROWS, 2 * HD), jnp.float32)
    save(fold(fresh, block_queries(held), sk_in[...].reshape(QB, HD), s_wide[...].reshape(QB, 2 * HD), mask))
    for copy in loads[3:]:
        copy.wait()

    def send_out(b):
        return pltpu.make_async_copy(
            out_in.at[:, pl.ds(b * 2, 2)], out.at[:, pl.ds(b * 2, 2)], out_sem.at[b]
        )

    def one_block(step, carry):
        b = (held + step) % NQB
        hits = []
        for i in range(2):
            c = first + jnp.where(core == 0, i, 1 - i)
            hits.append((chosen[0, b] == c) | (chosen[1, b] == c) | (chosen[2, b] == c))
        used = hits[0] | hits[1] | (step == 0)

        @pl.when(used & (step != 0))
        def _():
            acc[...] = jnp.zeros((ROWS, 2 * HD), jnp.float32)
            peak[...] = jnp.full((ROWS, HD), FLOOR_SCORE, jnp.float32)

        def cached(i, carry):
            @pl.when(jnp.where(i == 0, hits[0], hits[1]))
            def _():
                queries = block_queries(b)
                state = load()
                for start in range(0, KB, CHUNK):
                    state = fold(
                        state, queries, k_both[i, start:start + CHUNK, :], v_wide[i, start:start + CHUNK, :], None
                    )
                save(state)

            return carry

        lax.fori_loop(0, 2, cached, 0)

        @pl.when(used)
        def _():
            total = acc[:, HD:]
            out_in[:, pl.ds(b * 2, 2)] = (
                (acc[:, :HD] / total).astype(jnp.bfloat16).reshape(2, 2, NY, PIECE, HD)
            )
            logs = peak[...] * SCALE2 + jnp.log2(total)
            eye = lax.broadcasted_iota(jnp.int32, (PIECE, HD), 0) == lax.broadcasted_iota(
                jnp.int32, (PIECE, HD), 1
            )
            for piece in range(NY):
                for part in range(4):
                    start = part * HALF + piece * PIECE
                    lse_in[part // 2, piece, b // 4, pl.ds(b % 4 * 2 + part % 2, 1), :] = jnp.sum(
                        jnp.where(eye, logs[start:start + PIECE], 0.0), axis=0, keepdims=True
                    )

        @pl.when(jnp.logical_not(used))
        def _():
            out_in[:, pl.ds(b * 2, 2)] = jnp.zeros((2, 2, NY, PIECE, HD), jnp.bfloat16)

        send_out(b).start()
        return carry

    lax.fori_loop(0, NQB, one_block, 0)
    lse_copy = pltpu.make_async_copy(lse_in, lse, sems.at[7])
    lse_copy.start()
    for b in range(NQB):
        send_out(b).wait()
    lse_copy.wait()


def attend(chosen, q, k_own, v_own, k_pair, v_pair, span):
    anywhere = pl.BlockSpec(memory_space=pl.ANY)
    dma = pltpu.SemaphoreType.DMA
    return pl.pallas_call(
        attend_kernel,
        out_shape=[
            jax.ShapeDtypeStruct((2, NW, NY, PIECE, HD), jnp.bfloat16),
            jax.ShapeDtypeStruct((2, NY, 2, 8, HD), jnp.float32),
        ],
        in_specs=[pl.BlockSpec(memory_space=pltpu.SMEM)] + [anywhere] * 6,
        out_specs=[anywhere] * 2,
        scratch_shapes=[
            pltpu.VMEM((NW, HALF, 2 * HD), jnp.bfloat16),
            pltpu.VMEM((2, KB, HD), jnp.bfloat16),
            pltpu.VMEM((2, KB, 2 * HD), jnp.bfloat16),
            pltpu.VMEM((2, NY, PIECE, HD), jnp.bfloat16),
            pltpu.VMEM((2, NY, PIECE, 2 * HD), jnp.bfloat16),
            pltpu.VMEM((2, NW, NY, PIECE, HD), jnp.bfloat16),
            pltpu.VMEM((2, NY, 2, 8, HD), jnp.float32),
            pltpu.VMEM((ROWS, 2 * HD), jnp.float32),
            pltpu.VMEM((ROWS, HD), jnp.float32),
            dma((8,)), dma((NQB,)),
        ],
        compiler_params=pltpu.CompilerParams(vmem_limit_bytes=56 * MIB),
        cost_estimate=pl.CostEstimate(flops=14 * 10**9, bytes_accessed=10 * MIB, transcendentals=25 * 10**6),
    )(chosen, q, k_own, v_own, k_pair, v_pair, span)


def finish_kernel(
    part, lse, weight, result,
    x_in, y_in, x_mid, y_mid, x_last, y_last, lx_in, ly_in, lx_mid, ly_mid, lx_last, ly_last,
    w_in, rows_out, rows_in,
    x_send, x_recv, y_send, y_recv, xm_send, xm_recv, ym_send, ym_recv,
    a_send, a_recv, ring_send, ring_recv, on_send, on_recv, f_send, f_recv, local_sem,
):
    wide, narrow, y, core = place()
    buddy = y * 2 + 1 - core
    kv, side = wide // 2, wide % 2
    ring = [(y + 1) % NY, (y + NY - 1) % NY]
    behind = ring[::-1]
    own_target = wide // 8 == side
    barrier = pltpu.get_barrier_semaphore()

    across = wide + 1 - side * 2, narrow

    def along(step):
        return wide, (y + step) % NY * 2 + core

    fetches = [pltpu.make_async_copy(weight.at[:, i], w_in.at[i], local_sem.at[i]) for i in range(4)]
    keep = [
        pltpu.make_async_copy(part.at[0, pl.ds(side * 8, 8)], x_in.at[0], local_sem.at[4]),
        pltpu.make_async_copy(lse.at[0, :, side], lx_in.at[0], local_sem.at[5]),
        pltpu.make_async_copy(part.at[1, :, y], y_in.at[y], local_sem.at[6]),
        pltpu.make_async_copy(lse.at[1, y], ly_in.at[y], local_sem.at[9]),
    ]
    for copy in (*keep, *fetches):
        copy.start()
    for device in (across, *(along(step) for step in range(1, NY))):
        pl.semaphore_signal(barrier, inc=1, device_id=device, device_id_type=MESH)

    def greet_source(s, carry):
        @pl.when(jnp.logical_not(own_target & (s == kv)))
        def _():
            pl.semaphore_signal(barrier, inc=1, device_id=(s * 2 + wide // 8, narrow), device_id_type=MESH)

        return carry

    lax.fori_loop(0, 8, greet_source, 0)
    pl.semaphore_signal(barrier, inc=1, device_id=(wide, buddy), device_id_type=MESH)
    pl.semaphore_wait(barrier, 13 - own_target.astype(jnp.int32))

    x_copies = [
        remote(part.at[0, pl.ds((1 - side) * 8, 8)], x_in.at[1], x_send.at[0], x_recv.at[0], across),
        remote(lse.at[0, :, 1 - side], lx_in.at[1], x_send.at[1], x_recv.at[1], across),
    ]

    def y_copies(step):
        to = (y + step) % NY
        return [
            remote(part.at[1, :, to], y_in.at[y], y_send.at[step, 0], y_recv.at[y, 0], along(step)),
            remote(lse.at[1, to], ly_in.at[y], y_send.at[step, 1], y_recv.at[y, 1], along(step)),
        ]

    def y_arrivals(step):
        origin = (y + step) % NY
        return [
            remote(part.at[1, :, 0], y_in.at[origin], y_send.at[step, 0], y_recv.at[origin, 0], across),
            remote(lse.at[1, 0], ly_in.at[origin], y_send.at[step, 1], y_recv.at[origin, 1], across),
        ]

    def xm_copies(step):
        to = (y + step) % NY
        return [
            remote(x_mid.at[to], x_last.at[y], xm_send.at[step, 0], xm_recv.at[y, 0], along(step)),
            remote(lx_mid.at[to], lx_last.at[y], xm_send.at[step, 1], xm_recv.at[y, 1], along(step)),
        ]

    def xm_arrivals(step):
        origin = (y + step) % NY
        return [
            remote(x_mid.at[0], x_last.at[origin], xm_send.at[step, 0], xm_recv.at[origin, 0], across),
            remote(lx_mid.at[0], lx_last.at[origin], xm_send.at[step, 1], xm_recv.at[origin, 1], across),
        ]

    ym_copies = [
        remote(y_mid.at[1 - side], y_last, ym_send.at[0], ym_recv.at[0], across),
        remote(ly_mid.at[1 - side], ly_last, ym_send.at[1], ym_recv.at[1], across),
    ]

    for copy in x_copies:
        copy.start()
    for step in (1, 3, 2):
        for copy in y_copies(step):
            copy.start()

    def weigh(logs):
        top = jnp.max(logs, axis=0)
        shares = jnp.exp2(logs - top[None])
        total = jnp.sum(shares, axis=0)
        shares = (shares / total[None]).reshape(-1, HD)
        turned = jnp.transpose(jnp.concatenate([shares] * (HD // shares.shape[0]), axis=0))
        return turned[:PIECE], top + jnp.log2(total)

    def mix(turned, columns, pieces):
        total = jnp.zeros((PIECE, HD), jnp.float32)
        for column, piece in zip(columns, pieces):
            total = total + piece.astype(jnp.float32) * turned[:, column:column + 1]
        return total.astype(jnp.bfloat16)

    for copy in keep:
        copy.wait()
    for copy in x_copies:
        copy.wait_recv()
    turned, logs = weigh(lx_in[...].reshape(2, NY * 8, HD))
    lx_mid[...] = logs.reshape(NY, 8, HD)
    for piece in range(NY):
        for i in range(8):
            column = piece * 8 + i
            x_mid[piece, i] = mix(turned, (column, 32 + column), (x_in[0, i, piece], x_in[1, i, piece]))
    x_keep = [
        pltpu.make_async_copy(x_mid.at[y], x_last.at[y], local_sem.at[10]),
        pltpu.make_async_copy(lx_mid.at[y], lx_last.at[y], local_sem.at[11]),
    ]
    for copy in x_keep:
        copy.start()
    for step in (1, 3, 2):
        for copy in xm_copies(step):
            copy.start()

    for step in (1, 3, 2):
        for copy in y_arrivals(step):
            copy.wait_recv()
    turned, logs = weigh(ly_in[...].reshape(NY, 16, HD))
    ly_mid[...] = logs.reshape(2, 8, HD)
    for i in range(16):
        y_mid[i // 8, i % 8] = mix(turned, [s * 16 + i for s in range(NY)], [y_in[s, i] for s in range(NY)])
    for copy in ym_copies:
        copy.start()

    def row_copy(i, h):
        return remote(
            rows_out.at[h, i], rows_in.at[core, h, y, kv], a_send.at[i, h], a_recv.at[kv, h], (side * 8 + i, narrow)
        )

    def own_copy(h):
        return pltpu.make_async_copy(rows_out.at[h, wide % 8], rows_in.at[core, h, y, kv], local_sem.at[7 + h])

    def local(i):
        return own_target & (i == wide % 8)

    for h in (1, 0):
        if h == 0:
            for copy in x_keep:
                copy.wait()
            for step in (1, 3, 2):
                for copy in xm_arrivals(step):
                    copy.wait_recv()
            turned, logs = weigh(lx_last[...])
            for i in range(8):
                rows_out[h, i] = mix(turned, [s * 8 + i for s in range(NY)], [x_last[s, i] for s in range(NY)])
        else:
            for copy in ym_copies:
                copy.wait_recv()
            turned, logs = weigh(jnp.stack([ly_mid[side], ly_last[...]]))
            for i in range(8):
                rows_out[h, i] = mix(turned, (i, 8 + i), (y_mid[side, i], y_last[i]))

        def start_row(i, carry):
            @pl.when(local(i))
            def _():
                own_copy(h).start()

            @pl.when(jnp.logical_not(local(i)))
            def _():
                row_copy(i, h).start()

            return carry

        lax.fori_loop(0, 8, start_row, 0)

    def batch(side_core, h, piece):
        return rows_in.at[side_core, h, piece]

    def ring_copy(h, direction, piece):
        return remote(
            batch(core, h, piece), batch(core, h, piece),
            ring_send.at[h, direction], ring_recv.at[h, direction], (wide, ring[direction] * 2 + core),
        )

    def on_copy(h, piece):
        return remote(
            batch(core, h, piece), batch(core, h, piece), on_send.at[h], on_recv.at[h], (wide, ring[h] * 2 + core)
        )

    def forward(h, piece, side_core):
        return remote(
            batch(side_core, h, piece), batch(side_core, h, piece),
            f_send.at[h, piece], f_recv.at[h, piece], (wide, buddy),
        )

    for h in (1, 0):
        def wait_row(k, carry):
            mine = own_target & (k == kv)

            @pl.when(mine)
            def _():
                own_copy(h).wait()

            @pl.when(jnp.logical_not(mine))
            def _():
                remote(
                    rows_out.at[h, 0], rows_in.at[core, h, y, k], a_send.at[0, h], a_recv.at[k, h], (wide, buddy)
                ).wait_recv()

            return carry

        lax.fori_loop(0, 8, wait_row, 0)
        for direction in range(2):
            ring_copy(h, direction, y).start()
        forward(h, y, core).start()

    for h in (1, 0):
        ring_copy(h, h, behind[h]).wait_recv()
        on_copy(h, behind[h]).start()
        forward(h, behind[h], core).start()

    for copy in fetches:
        copy.wait()

    def product(side_core, h):
        rows = jnp.concatenate([rows_in[side_core, h, :, k].reshape(HALF, HD) for k in range(KVH)], axis=1)
        return jnp.dot(
            rows, w_in[side_core * 2 + h].reshape(KVH * HD, 512), preferred_element_type=jnp.float32
        )

    total = jnp.zeros((HALF, 512), jnp.float32)
    for h in (1, 0):
        ring_copy(h, 1 - h, behind[1 - h]).wait_recv()
        forward(h, behind[1 - h], core).start()
        on_copy(h, (y + 2) % NY).wait_recv()
        forward(h, (y + 2) % NY, core).start()
    for h in (1, 0):
        total = total + product(core, h)
    for h in (1, 0):
        for piece in range(NY):
            forward(h, piece, 1 - core).wait_recv()
        total = total + product(1 - core, h)
    result[...] = total

    for copy in (*x_copies, *ym_copies):
        copy.wait_send()
    for step in range(1, NY):
        for copy in (*y_copies(step), *xm_copies(step)):
            copy.wait_send()
    for h in range(2):
        def drain_row(i, carry):
            @pl.when(jnp.logical_not(local(i)))
            def _():
                row_copy(i, h).wait_send()

            return carry

        lax.fori_loop(0, 8, drain_row, 0)
        for direction in range(2):
            ring_copy(h, direction, y).wait_send()
        on_copy(h, behind[h]).wait_send()
        for piece in range(NY):
            forward(h, piece, core).wait_send()


def finish(part, lse, weight):
    anywhere = pl.BlockSpec(memory_space=pl.ANY)
    dma = pltpu.SemaphoreType.DMA
    return pl.pallas_call(
        finish_kernel,
        out_shape=jax.ShapeDtypeStruct((HALF, 512), jnp.float32),
        in_specs=[anywhere] * 3,
        out_specs=pl.BlockSpec(memory_space=pltpu.VMEM),
        scratch_shapes=[
            pltpu.VMEM((2, 8, NY, PIECE, HD), jnp.bfloat16),
            pltpu.VMEM((NY, 16, PIECE, HD), jnp.bfloat16),
            pltpu.VMEM((NY, 8, PIECE, HD), jnp.bfloat16),
            pltpu.VMEM((2, 8, PIECE, HD), jnp.bfloat16),
            pltpu.VMEM((NY, 8, PIECE, HD), jnp.bfloat16),
            pltpu.VMEM((8, PIECE, HD), jnp.bfloat16),
            pltpu.VMEM((2, NY, 8, HD), jnp.float32),
            pltpu.VMEM((NY, 2, 8, HD), jnp.float32),
            pltpu.VMEM((NY, 8, HD), jnp.float32),
            pltpu.VMEM((2, 8, HD), jnp.float32),
            pltpu.VMEM((NY, 8, HD), jnp.float32),
            pltpu.VMEM((8, HD), jnp.float32),
            pltpu.VMEM((4, KVH, HD, 512), jnp.bfloat16),
            pltpu.VMEM((2, 8, PIECE, HD), jnp.bfloat16),
            pltpu.VMEM((2, 2, NY, KVH, PIECE, HD), jnp.bfloat16),
            dma((2,)), dma((2,)), dma((NY, 2)), dma((NY, 2)), dma((NY, 2)), dma((NY, 2)), dma((2,)), dma((2,)),
            dma((8, 2)), dma((8, 2)), dma((2, 2)), dma((2, 2)), dma((2,)), dma((2,)),
            dma((2, NY)), dma((2, NY)), dma((12,)),
        ],
        compiler_params=pltpu.CompilerParams(
            collective_id=1, has_side_effects=True, vmem_limit_bytes=56 * MIB
        ),
    )(part, lse, weight.reshape(KVH, 4, HD, 512))


def shards(queries, span_keys, span_values, cache_keys, cache_values, chosen, out_weight):
    weight = lax.all_gather(out_weight, "wide", axis=0, tiled=True)
    q, k_pair, v_pair, span = spread(queries, span_keys, span_values, cache_keys, cache_values)
    part, lse = attend(chosen.T, q, cache_keys, cache_values, k_pair, v_pair, span)
    return finish(part, lse, weight).astype(jnp.bfloat16)


def solution(mesh):
    return jax.shard_map(
        shards,
        mesh=mesh,
        in_specs=(
            P("wide", None),
            P("wide", None),
            P("wide", None),
            P(("wide", "narrow"), None),
            P(("wide", "narrow"), None),
            P(),
            P("wide", "narrow"),
        ),
        out_specs=P("wide", "narrow"),
        check_vma=False,
    )
```

```python
import math

import jax
import jax.numpy as jnp
from jax import lax
from jax.experimental import pallas as pl
from jax.experimental.pallas import tpu as pltpu
from jax.sharding import PartitionSpec as P

HD = 128
QB = 512
KB = 4096
NQB = 8
NW = 16
KVH = 8
HALF = 256
ROWS = 2 * QB
NY = 4
PIECE = HALF // NY
CHUNK = 256
FLOOR_SCORE = -1e30
SCALE2 = math.log2(math.e) / math.sqrt(HD)
MESH = pl.DeviceIdType.MESH
MIB = 2**20


def place():
    wide = lax.axis_index("wide")
    narrow = lax.axis_index("narrow")
    return wide, narrow, narrow // 2, narrow % 2


def remote(src, dst, send_sem, recv_sem, device):
    return pltpu.make_async_remote_copy(
        src_ref=src, dst_ref=dst, send_sem=send_sem, recv_sem=recv_sem, device_id=device, device_id_type=MESH
    )


def spread_kernel(
    queries, span_k, span_v, cache_k, cache_v,
    q_out, pk_out, pv_out, s_out,
    s_in, q_send, q_recv, ring_send, ring_recv, pass_send, pass_recv,
    kv_send, kv_recv, s_send, s_recv, turn_send, turn_recv, share_send, share_recv, local_sem,
):
    wide, narrow, y, core = place()
    buddy = y * 2 + 1 - core
    z, x, side = wide // 4, wide % 4, wide % 2
    ring = [(y + 1) % NY, (y + NY - 1) % NY]
    behind = ring[::-1]
    barrier = pltpu.get_barrier_semaphore()

    def greet(step, carry):
        pl.semaphore_signal(
            barrier, inc=1, device_id=((wide + step) % NW, narrow), device_id_type=MESH
        )
        return carry

    lax.fori_loop(1, NW, greet, 0)
    for neighbour in (buddy, *((y + step) % NY * 2 + core for step in range(1, NY))):
        pl.semaphore_signal(barrier, inc=1, device_id=(wide, neighbour), device_id_type=MESH)
    pl.semaphore_wait(barrier, NW + 3)

    tokens = pl.ds(pl.multiple_of(y * PIECE, PIECE), PIECE)

    def columns(kv):
        return pl.ds(pl.multiple_of(kv * 512 + core * 256, 256), 256)

    def q_copy(dz, dx):
        target = (z + dz) % 4 * 4 + (x + dx) % 4
        rows = tokens if dz else slice(None)
        return remote(
            queries.at[rows, columns(target // 2)], q_out.at[wide, rows],
            q_send.at[dz * 4 + dx], q_recv.at[wide], (target, narrow),
        )

    def q_wait(source, rows):
        remote(
            queries.at[rows, columns(0)], q_out.at[source, rows], q_send.at[1], q_recv.at[source], (source, narrow)
        ).wait_recv()

    steps = [(dz, dx) for dz in (1, 3, 2, 0) for dx in (0, 1, 3, 2) if dz or dx]
    own_q = pltpu.make_async_copy(queries.at[:, columns(wide // 2)], q_out.at[wide], local_sem.at[0])

    s_home = wide // 8
    own_s = s_home == side

    def s_src(which, kv):
        return (span_k, span_v)[which].at[tokens, pl.ds(pl.multiple_of(kv * HD, HD), HD)]

    def s_copy(which, kv):
        return remote(
            s_src(which, kv), s_in.at[wide % 8], s_send.at[kv], s_recv.at[wide % 8], (kv * 2 + s_home, narrow)
        )

    def s_local(which):
        return pltpu.make_async_copy(s_src(which, wide // 2), s_in.at[wide % 8], local_sem.at[1])

    def s_start(kv, carry):
        away = jnp.logical_not(own_s & (kv == wide // 2))
        for which in range(2):
            @pl.when((core == which) & away)
            def _():
                s_copy(which, kv).start()

            @pl.when((core == which) & jnp.logical_not(away))
            def _():
                s_local(which).start()

        return carry

    for dz, dx in steps[:8]:
        q_copy(dz, dx).start()
    lax.fori_loop(0, KVH, s_start, 0)
    for dz, dx in steps[8:]:
        q_copy(dz, dx).start()
    own_q.start()
    kv_copies = [
        remote(src, dst, kv_send.at[i], kv_recv.at[i], (wide, buddy))
        for i, (src, dst) in enumerate(((cache_k, pk_out), (cache_v, pv_out)))
    ]
    for copy in kv_copies:
        copy.start()

    def piece_rows(piece):
        return pl.ds(pl.multiple_of(piece * PIECE, PIECE), PIECE)

    def ring_copy(group, direction, piece):
        batch = q_out.at[pl.ds(group * 4, 4), piece_rows(piece)]
        return remote(
            batch, batch, ring_send.at[group, direction], ring_recv.at[group, direction],
            (wide, ring[direction] * 2 + core),
        )

    def pass_copy(group, direction, piece):
        batch = q_out.at[pl.ds(group * 4 + direction * 2, 2), piece_rows(piece)]
        return remote(
            batch, batch, pass_send.at[group, direction], pass_recv.at[group, direction],
            (wide, ring[direction] * 2 + core),
        )

    groups = [(z + step) % 4 for step in (3, 1, 2)]
    for group in groups:
        for i in range(4):
            q_wait(group * 4 + i, tokens)
        for direction in range(2):
            ring_copy(group, direction, y).start()

    def s_wait(i, carry):
        mine = own_s & (i == wide % 8)

        @pl.when(mine)
        def _():
            s_local(0).wait()

        @pl.when(jnp.logical_not(mine))
        def _():
            remote(s_src(0, 0), s_in.at[i], s_send.at[0], s_recv.at[i], (wide, buddy)).wait_recv()

        return carry

    lax.fori_loop(0, 8, s_wait, 0)

    def turn_copy(step):
        to = (y + step) % NY
        return remote(
            s_in.at[pl.ds(to * 2, 2)], s_out.at[core, :, y], turn_send.at[step], turn_recv.at[y],
            (wide, to * 2 + core),
        )

    keep = pltpu.make_async_copy(s_in.at[pl.ds(y * 2, 2)], s_out.at[core, :, y], local_sem.at[2])
    keep.start()
    for step in range(1, NY):
        turn_copy(step).start()

    for group in groups:
        for direction in range(2):
            ring_copy(group, direction, behind[direction]).wait_recv()
            pass_copy(group, direction, behind[direction]).start()

    keep.wait()
    for step in range(1, NY):
        origin = (y + step) % NY
        remote(
            s_in.at[pl.ds(0, 2)], s_out.at[core, :, origin], turn_send.at[step], turn_recv.at[origin], (wide, buddy)
        ).wait_recv()
    share = remote(s_out.at[core], s_out.at[core], share_send.at[0], share_recv.at[core], (wide, buddy))
    share.start()

    for group in groups:
        for direction in range(2):
            pass_copy(group, direction, (y + 2) % NY).wait_recv()
    remote(s_out.at[core], s_out.at[1 - core], share_send.at[0], share_recv.at[1 - core], (wide, buddy)).wait_recv()
    own_q.wait()
    for dx in range(1, 4):
        q_wait(z * 4 + (x + dx) % 4, slice(None))
    for copy in kv_copies:
        copy.wait()
    share.wait_send()
    for group in groups:
        for direction in range(2):
            ring_copy(group, direction, y).wait_send()
            pass_copy(group, direction, behind[direction]).wait_send()
    for step in range(1, NY):
        turn_copy(step).wait_send()
    for dz, dx in steps:
        q_copy(dz, dx).wait_send()

    def s_drain(kv, carry):
        @pl.when(jnp.logical_not(own_s & (kv == wide // 2)))
        def _():
            s_copy(0, kv).wait_send()

        return carry

    lax.fori_loop(0, KVH, s_drain, 0)


def spread(queries, span_k, span_v, cache_k, cache_v):
    anywhere = pl.BlockSpec(memory_space=pl.ANY)
    shape = lambda *dims: jax.ShapeDtypeStruct(dims, jnp.bfloat16)
    dma = pltpu.SemaphoreType.DMA
    return pl.pallas_call(
        spread_kernel,
        out_shape=[shape(NW, HALF, 2 * HD), shape(KB, HD), shape(KB, HD), shape(2, 2, NY, PIECE, HD)],
        in_specs=[anywhere] * 5,
        out_specs=[anywhere] * 4,
        scratch_shapes=[
            pltpu.VMEM((8, PIECE, HD), jnp.bfloat16),
            dma((NW,)), dma((NW,)), dma((4, 2)), dma((4, 2)), dma((4, 2)), dma((4, 2)),
            dma((2,)), dma((2,)), dma((KVH,)), dma((8,)), dma((NY,)), dma((NY,)), dma((1,)), dma((2,)), dma((3,)),
        ],
        compiler_params=pltpu.CompilerParams(
            collective_id=0, has_side_effects=True, vmem_limit_bytes=56 * MIB
        ),
    )(queries, span_k, span_v, cache_k, cache_v)


def attend_kernel(
    chosen, q, k_own, v_own, k_pair, v_pair, span, out, lse,
    q_in, k_both, v_wide, sk_in, s_wide, out_in, lse_in, acc, peak, sems, out_sem,
):
    wide, narrow, y, core = place()
    held = wide % 2 * 4 + y
    first = wide % 2 * 8 + y * 2
    moves = [
        (q, q_in),
        (span.at[0], sk_in),
        (span.at[1], s_wide.at[:, :, :, :HD]),
        (k_own, k_both.at[0]),
        (v_own, v_wide.at[0, :, :HD]),
        (k_pair, k_both.at[1]),
        (v_pair, v_wide.at[1, :, :HD]),
    ]
    loads = [pltpu.make_async_copy(src, dst, sems.at[i]) for i, (src, dst) in enumerate(moves)]
    for copy in loads:
        copy.start()
    s_wide[:, :, :, HD:] = jnp.ones((2, NY, PIECE, HD), jnp.bfloat16)
    lse_in[...] = jnp.full((2, NY, 2, 8, HD), FLOOR_SCORE, jnp.float32)
    for i in range(2):
        v_wide[i, :, HD:] = jnp.ones((KB, HD), jnp.bfloat16)

    def fold(state, queries, keys, values, mask):
        top, total = state
        scores = lax.dot_general(queries, keys, (((1,), (1,)), ((), ())), preferred_element_type=jnp.float32)
        if mask is not None:
            scores = jnp.where(mask, scores, FLOOR_SCORE)
        new_top = jnp.maximum(top, jnp.max(scores, axis=1, keepdims=True))
        decay = jnp.exp2((top - new_top) * SCALE2)
        weights = jnp.exp2((scores - new_top) * SCALE2).astype(jnp.bfloat16)
        total = total * decay + jnp.dot(weights, values, preferred_element_type=jnp.float32)
        return new_top, total

    def block_queries(b):
        rows = q_in[pl.ds(b * 2, 2)].reshape(QB, 2 * HD)
        return jnp.concatenate([rows[:, :HD], rows[:, HD:]], axis=0)

    def load():
        return jnp.max(peak[...], axis=1, keepdims=True), acc[...]

    def save(state):
        peak[...] = jnp.broadcast_to(state[0], (ROWS, HD))
        acc[...] = state[1]

    for copy in loads[:3]:
        copy.wait()
    row = lax.broadcasted_iota(jnp.int32, (ROWS, QB), 0) % QB
    mask = row >= lax.broadcasted_iota(jnp.int32, (ROWS, QB), 1)
    fresh = jnp.full((ROWS, 1), FLOOR_SCORE, jnp.float32), jnp.zeros((ROWS, 2 * HD), jnp.float32)
    save(fold(fresh, block_queries(held), sk_in[...].reshape(QB, HD), s_wide[...].reshape(QB, 2 * HD), mask))
    for copy in loads[3:]:
        copy.wait()

    def send_out(b):
        return pltpu.make_async_copy(
            out_in.at[:, pl.ds(b * 2, 2)], out.at[:, pl.ds(b * 2, 2)], out_sem.at[b]
        )

    def one_block(step, carry):
        b = (held + step) % NQB
        hits = []
        for i in range(2):
            c = first + jnp.where(core == 0, i, 1 - i)
            hits.append((chosen[0, b] == c) | (chosen[1, b] == c) | (chosen[2, b] == c))
        used = hits[0] | hits[1] | (step == 0)

        @pl.when(used & (step != 0))
        def _():
            acc[...] = jnp.zeros((ROWS, 2 * HD), jnp.float32)
            peak[...] = jnp.full((ROWS, HD), FLOOR_SCORE, jnp.float32)

        def cached(i, carry):
            @pl.when(jnp.where(i == 0, hits[0], hits[1]))
            def _():
                queries = block_queries(b)
                state = load()
                for start in range(0, KB, CHUNK):
                    state = fold(
                        state, queries, k_both[i, start:start + CHUNK, :], v_wide[i, start:start + CHUNK, :], None
                    )
                save(state)

            return carry

        lax.fori_loop(0, 2, cached, 0)

        @pl.when(used)
        def _():
            total = acc[:, HD:]
            out_in[:, pl.ds(b * 2, 2)] = (
                (acc[:, :HD] / total).astype(jnp.bfloat16).reshape(2, 2, NY, PIECE, HD)
            )
            logs = peak[...] * SCALE2 + jnp.log2(total)
            eye = lax.broadcasted_iota(jnp.int32, (PIECE, HD), 0) == lax.broadcasted_iota(
                jnp.int32, (PIECE, HD), 1
            )
            for piece in range(NY):
                for part in range(4):
                    start = part * HALF + piece * PIECE
                    lse_in[part // 2, piece, b // 4, pl.ds(b % 4 * 2 + part % 2, 1), :] = jnp.sum(
                        jnp.where(eye, logs[start:start + PIECE], 0.0), axis=0, keepdims=True
                    )

        @pl.when(jnp.logical_not(used))
        def _():
            out_in[:, pl.ds(b * 2, 2)] = jnp.zeros((2, 2, NY, PIECE, HD), jnp.bfloat16)

        send_out(b).start()
        return carry

    lax.fori_loop(0, NQB, one_block, 0)
    lse_copy = pltpu.make_async_copy(lse_in, lse, sems.at[7])
    lse_copy.start()
    for b in range(NQB):
        send_out(b).wait()
    lse_copy.wait()


def attend(chosen, q, k_own, v_own, k_pair, v_pair, span):
    anywhere = pl.BlockSpec(memory_space=pl.ANY)
    dma = pltpu.SemaphoreType.DMA
    return pl.pallas_call(
        attend_kernel,
        out_shape=[
            jax.ShapeDtypeStruct((2, NW, NY, PIECE, HD), jnp.bfloat16),
            jax.ShapeDtypeStruct((2, NY, 2, 8, HD), jnp.float32),
        ],
        in_specs=[pl.BlockSpec(memory_space=pltpu.SMEM)] + [anywhere] * 6,
        out_specs=[anywhere] * 2,
        scratch_shapes=[
            pltpu.VMEM((NW, HALF, 2 * HD), jnp.bfloat16),
            pltpu.VMEM((2, KB, HD), jnp.bfloat16),
            pltpu.VMEM((2, KB, 2 * HD), jnp.bfloat16),
            pltpu.VMEM((2, NY, PIECE, HD), jnp.bfloat16),
            pltpu.VMEM((2, NY, PIECE, 2 * HD), jnp.bfloat16),
            pltpu.VMEM((2, NW, NY, PIECE, HD), jnp.bfloat16),
            pltpu.VMEM((2, NY, 2, 8, HD), jnp.float32),
            pltpu.VMEM((ROWS, 2 * HD), jnp.float32),
            pltpu.VMEM((ROWS, HD), jnp.float32),
            dma((8,)), dma((NQB,)),
        ],
        compiler_params=pltpu.CompilerParams(vmem_limit_bytes=56 * MIB),
        cost_estimate=pl.CostEstimate(flops=14 * 10**9, bytes_accessed=10 * MIB, transcendentals=25 * 10**6),
    )(chosen, q, k_own, v_own, k_pair, v_pair, span)


def finish_kernel(
    part, lse, weight, result,
    x_in, y_in, x_mid, y_mid, x_last, y_last, lx_in, ly_in, lx_mid, ly_mid, lx_last, ly_last,
    w_in, rows_out, rows_in,
    x_send, x_recv, y_send, y_recv, xm_send, xm_recv, ym_send, ym_recv,
    a_send, a_recv, ring_send, ring_recv, on_send, on_recv, f_send, f_recv, local_sem,
):
    wide, narrow, y, core = place()
    buddy = y * 2 + 1 - core
    kv, side = wide // 2, wide % 2
    ring = [(y + 1) % NY, (y + NY - 1) % NY]
    behind = ring[::-1]
    own_target = wide // 8 == side
    barrier = pltpu.get_barrier_semaphore()

    across = wide + 1 - side * 2, narrow

    def along(step):
        return wide, (y + step) % NY * 2 + core

    fetches = [pltpu.make_async_copy(weight.at[:, i], w_in.at[i], local_sem.at[i]) for i in range(4)]
    keep = [
        pltpu.make_async_copy(part.at[0, pl.ds(side * 8, 8)], x_in.at[0], local_sem.at[4]),
        pltpu.make_async_copy(lse.at[0, :, side], lx_in.at[0], local_sem.at[5]),
        pltpu.make_async_copy(part.at[1, :, y], y_in.at[y], local_sem.at[6]),
        pltpu.make_async_copy(lse.at[1, y], ly_in.at[y], local_sem.at[9]),
    ]
    for copy in (*keep, *fetches):
        copy.start()
    for device in (across, *(along(step) for step in range(1, NY))):
        pl.semaphore_signal(barrier, inc=1, device_id=device, device_id_type=MESH)

    def greet_source(s, carry):
        @pl.when(jnp.logical_not(own_target & (s == kv)))
        def _():
            pl.semaphore_signal(barrier, inc=1, device_id=(s * 2 + wide // 8, narrow), device_id_type=MESH)

        return carry

    lax.fori_loop(0, 8, greet_source, 0)
    pl.semaphore_signal(barrier, inc=1, device_id=(wide, buddy), device_id_type=MESH)
    pl.semaphore_wait(barrier, 13 - own_target.astype(jnp.int32))

    x_copies = [
        remote(part.at[0, pl.ds((1 - side) * 8, 8)], x_in.at[1], x_send.at[0], x_recv.at[0], across),
        remote(lse.at[0, :, 1 - side], lx_in.at[1], x_send.at[1], x_recv.at[1], across),
    ]

    def y_copies(step):
        to = (y + step) % NY
        return [
            remote(part.at[1, :, to], y_in.at[y], y_send.at[step, 0], y_recv.at[y, 0], along(step)),
            remote(lse.at[1, to], ly_in.at[y], y_send.at[step, 1], y_recv.at[y, 1], along(step)),
        ]

    def y_arrivals(step):
        origin = (y + step) % NY
        return [
            remote(part.at[1, :, 0], y_in.at[origin], y_send.at[step, 0], y_recv.at[origin, 0], across),
            remote(lse.at[1, 0], ly_in.at[origin], y_send.at[step, 1], y_recv.at[origin, 1], across),
        ]

    def xm_copies(step):
        to = (y + step) % NY
        return [
            remote(x_mid.at[to], x_last.at[y], xm_send.at[step, 0], xm_recv.at[y, 0], along(step)),
            remote(lx_mid.at[to], lx_last.at[y], xm_send.at[step, 1], xm_recv.at[y, 1], along(step)),
        ]

    def xm_arrivals(step):
        origin = (y + step) % NY
        return [
            remote(x_mid.at[0], x_last.at[origin], xm_send.at[step, 0], xm_recv.at[origin, 0], across),
            remote(lx_mid.at[0], lx_last.at[origin], xm_send.at[step, 1], xm_recv.at[origin, 1], across),
        ]

    ym_copies = [
        remote(y_mid.at[1 - side], y_last, ym_send.at[0], ym_recv.at[0], across),
        remote(ly_mid.at[1 - side], ly_last, ym_send.at[1], ym_recv.at[1], across),
    ]

    for copy in x_copies:
        copy.start()
    for step in (1, 3, 2):
        for copy in y_copies(step):
            copy.start()

    def weigh(logs):
        top = jnp.max(logs, axis=0)
        shares = jnp.exp2(logs - top[None])
        total = jnp.sum(shares, axis=0)
        shares = (shares / total[None]).reshape(-1, HD)
        turned = jnp.transpose(jnp.concatenate([shares] * (HD // shares.shape[0]), axis=0))
        return turned[:PIECE], top + jnp.log2(total)

    def mix(turned, columns, pieces):
        total = jnp.zeros((PIECE, HD), jnp.float32)
        for column, piece in zip(columns, pieces):
            total = total + piece.astype(jnp.float32) * turned[:, column:column + 1]
        return total.astype(jnp.bfloat16)

    for copy in keep:
        copy.wait()
    for copy in x_copies:
        copy.wait_recv()
    turned, logs = weigh(lx_in[...].reshape(2, NY * 8, HD))
    lx_mid[...] = logs.reshape(NY, 8, HD)
    for piece in range(NY):
        for i in range(8):
            column = piece * 8 + i
            x_mid[piece, i] = mix(turned, (column, 32 + column), (x_in[0, i, piece], x_in[1, i, piece]))
    x_keep = [
        pltpu.make_async_copy(x_mid.at[y], x_last.at[y], local_sem.at[10]),
        pltpu.make_async_copy(lx_mid.at[y], lx_last.at[y], local_sem.at[11]),
    ]
    for copy in x_keep:
        copy.start()
    for step in (1, 3, 2):
        for copy in xm_copies(step):
            copy.start()

    for step in (1, 3, 2):
        for copy in y_arrivals(step):
            copy.wait_recv()
    turned, logs = weigh(ly_in[...].reshape(NY, 16, HD))
    ly_mid[...] = logs.reshape(2, 8, HD)
    for i in range(16):
        y_mid[i // 8, i % 8] = mix(turned, [s * 16 + i for s in range(NY)], [y_in[s, i] for s in range(NY)])
    for copy in ym_copies:
        copy.start()

    def row_copy(i, h):
        return remote(
            rows_out.at[h, i], rows_in.at[core, h, y, kv], a_send.at[i, h], a_recv.at[kv, h], (side * 8 + i, narrow)
        )

    def own_copy(h):
        return pltpu.make_async_copy(rows_out.at[h, wide % 8], rows_in.at[core, h, y, kv], local_sem.at[7 + h])

    def local(i):
        return own_target & (i == wide % 8)

    for h in (1, 0):
        if h == 0:
            for copy in x_keep:
                copy.wait()
            for step in (1, 3, 2):
                for copy in xm_arrivals(step):
                    copy.wait_recv()
            turned, logs = weigh(lx_last[...])
            for i in range(8):
                rows_out[h, i] = mix(turned, [s * 8 + i for s in range(NY)], [x_last[s, i] for s in range(NY)])
        else:
            for copy in ym_copies:
                copy.wait_recv()
            turned, logs = weigh(jnp.stack([ly_mid[side], ly_last[...]]))
            for i in range(8):
                rows_out[h, i] = mix(turned, (i, 8 + i), (y_mid[side, i], y_last[i]))

        def start_row(i, carry):
            @pl.when(local(i))
            def _():
                own_copy(h).start()

            @pl.when(jnp.logical_not(local(i)))
            def _():
                row_copy(i, h).start()

            return carry

        lax.fori_loop(0, 8, start_row, 0)

    def batch(side_core, h, piece):
        return rows_in.at[side_core, h, piece]

    def ring_copy(h, direction, piece):
        return remote(
            batch(core, h, piece), batch(core, h, piece),
            ring_send.at[h, direction], ring_recv.at[h, direction], (wide, ring[direction] * 2 + core),
        )

    def on_copy(h, piece):
        return remote(
            batch(core, h, piece), batch(core, h, piece), on_send.at[h], on_recv.at[h], (wide, ring[h] * 2 + core)
        )

    def forward(h, piece, side_core):
        return remote(
            batch(side_core, h, piece), batch(side_core, h, piece),
            f_send.at[h, piece], f_recv.at[h, piece], (wide, buddy),
        )

    for h in (1, 0):
        def wait_row(k, carry):
            mine = own_target & (k == kv)

            @pl.when(mine)
            def _():
                own_copy(h).wait()

            @pl.when(jnp.logical_not(mine))
            def _():
                remote(
                    rows_out.at[h, 0], rows_in.at[core, h, y, k], a_send.at[0, h], a_recv.at[k, h], (wide, buddy)
                ).wait_recv()

            return carry

        lax.fori_loop(0, 8, wait_row, 0)
        for direction in range(2):
            ring_copy(h, direction, y).start()
        forward(h, y, core).start()

    for h in (1, 0):
        ring_copy(h, h, behind[h]).wait_recv()
        on_copy(h, behind[h]).start()
        forward(h, behind[h], core).start()

    for copy in fetches:
        copy.wait()

    def product(side_core, h):
        rows = jnp.concatenate([rows_in[side_core, h, :, k].reshape(HALF, HD) for k in range(KVH)], axis=1)
        return jnp.dot(
            rows, w_in[side_core * 2 + h].reshape(KVH * HD, 512), preferred_element_type=jnp.float32
        )

    total = jnp.zeros((HALF, 512), jnp.float32)
    for h in (1, 0):
        ring_copy(h, 1 - h, behind[1 - h]).wait_recv()
        forward(h, behind[1 - h], core).start()
        on_copy(h, (y + 2) % NY).wait_recv()
        forward(h, (y + 2) % NY, core).start()
    for h in (1, 0):
        total = total + product(core, h)
    for h in (1, 0):
        for piece in range(NY):
            forward(h, piece, 1 - core).wait_recv()
        total = total + product(1 - core, h)
    result[...] = total.astype(jnp.bfloat16)

    for copy in (*x_copies, *ym_copies):
        copy.wait_send()
    for step in range(1, NY):
        for copy in (*y_copies(step), *xm_copies(step)):
            copy.wait_send()
    for h in range(2):
        def drain_row(i, carry):
            @pl.when(jnp.logical_not(local(i)))
            def _():
                row_copy(i, h).wait_send()

            return carry

        lax.fori_loop(0, 8, drain_row, 0)
        for direction in range(2):
            ring_copy(h, direction, y).wait_send()
        on_copy(h, behind[h]).wait_send()
        for piece in range(NY):
            forward(h, piece, core).wait_send()


def finish(part, lse, weight):
    anywhere = pl.BlockSpec(memory_space=pl.ANY)
    dma = pltpu.SemaphoreType.DMA
    return pl.pallas_call(
        finish_kernel,
        out_shape=jax.ShapeDtypeStruct((HALF, 512), jnp.bfloat16),
        in_specs=[anywhere] * 3,
        out_specs=pl.BlockSpec(memory_space=pltpu.VMEM),
        scratch_shapes=[
            pltpu.VMEM((2, 8, NY, PIECE, HD), jnp.bfloat16),
            pltpu.VMEM((NY, 16, PIECE, HD), jnp.bfloat16),
            pltpu.VMEM((NY, 8, PIECE, HD), jnp.bfloat16),
            pltpu.VMEM((2, 8, PIECE, HD), jnp.bfloat16),
            pltpu.VMEM((NY, 8, PIECE, HD), jnp.bfloat16),
            pltpu.VMEM((8, PIECE, HD), jnp.bfloat16),
            pltpu.VMEM((2, NY, 8, HD), jnp.float32),
            pltpu.VMEM((NY, 2, 8, HD), jnp.float32),
            pltpu.VMEM((NY, 8, HD), jnp.float32),
            pltpu.VMEM((2, 8, HD), jnp.float32),
            pltpu.VMEM((NY, 8, HD), jnp.float32),
            pltpu.VMEM((8, HD), jnp.float32),
            pltpu.VMEM((4, KVH, HD, 512), jnp.bfloat16),
            pltpu.VMEM((2, 8, PIECE, HD), jnp.bfloat16),
            pltpu.VMEM((2, 2, NY, KVH, PIECE, HD), jnp.bfloat16),
            dma((2,)), dma((2,)), dma((NY, 2)), dma((NY, 2)), dma((NY, 2)), dma((NY, 2)), dma((2,)), dma((2,)),
            dma((8, 2)), dma((8, 2)), dma((2, 2)), dma((2, 2)), dma((2,)), dma((2,)),
            dma((2, NY)), dma((2, NY)), dma((12,)),
        ],
        compiler_params=pltpu.CompilerParams(
            collective_id=1, has_side_effects=True, vmem_limit_bytes=56 * MIB
        ),
    )(part, lse, weight.reshape(KVH, 4, HD, 512))


def shards(queries, span_keys, span_values, cache_keys, cache_values, chosen, out_weight):
    weight = lax.all_gather(out_weight, "wide", axis=0, tiled=True)
    q, k_pair, v_pair, span = spread(queries, span_keys, span_values, cache_keys, cache_values)
    part, lse = attend(chosen.T, q, cache_keys, cache_values, k_pair, v_pair, span)
    return finish(part, lse, weight)


def solution(mesh):
    return jax.shard_map(
        shards,
        mesh=mesh,
        in_specs=(
            P("wide", None),
            P("wide", None),
            P("wide", None),
            P(("wide", "narrow"), None),
            P(("wide", "narrow"), None),
            P(),
            P("wide", "narrow"),
        ),
        out_specs=P("wide", "narrow"),
        check_vma=False,
    )
```
